128 devices in a mesh: row: 16 (over y, z_hi, core), col: 8 (over x, z_lo).
Axes of the slice: x: 4, y: 4, z: 4 (z_hi: 2, z_lo: 2; z = z_hi * 2 + z_lo), core: 2. Of those that a mesh axis runs over, the one named last changes fastest.
Arguments:
- hidden: bfloat16 [16384, 3584], P('row'), may hold values from -6 to 6
- projection: bfloat16 [3584, 2048], P(None, 'col'), may hold values from -0.09375 to 0.09375
- grades: int32 [16384], P(('row', 'col')), may hold values from 0 to 9
- pattern: int32 [128, 128], replicated, may hold values from 0 to 1
Outputs:
- embed_grad: float32 [16384, 2048], P('row', 'col')
- weight_grad: float32 [3584, 2048], P('row', 'col')
The draws below stay inside these ranges and needn't reach their ends.
All inputs are finite; a program needn't handle non-finite values.
Results may differ from the reference program's by a relative error of at most 0.005.
Values may be sent and summed in bfloat16 or wider, within the bound.
No kernel may reach another device: no remote copies, remote signals or barrier semaphores. Data moves between devices by JAX's collectives and lax.ppermute only.
A program may use at most 128 MiB of HBM per device.

```python
import jax
import jax.numpy as jnp
from jax import lax

D = 3584
E = 2048
ANSWERS_PER_SET = 128
CLUSTERS = 4
BLOCKS = 128
RESP = 16384


def draw_pattern(key, part):
    key = jax.random.fold_in(key, 7)
    key_cluster, key_other, retained_mask_entry = jax.random.split(key, 3)
    cluster = jnp.minimum(jax.random.randint(key_cluster, (BLOCKS,), 0, CLUSTERS), jax.random.randint(key_other, (BLOCKS,), 0, CLUSTERS))
    kept_mask = jax.random.randint(retained_mask_entry, (BLOCKS, BLOCKS), 0, 4) > 0
    return ((cluster[:, None] == cluster[None, :]) & kept_mask).astype(jnp.int32)


def place_ends(drawn, own_key, low, high):
    spot = [jax.random.randint(jax.random.fold_in(own_key, axis), (), 0, length) for axis, length in enumerate(drawn.shape)]
    longest = drawn.shape.index(max(drawn.shape))
    next_to = spot[:longest] + [(spot[longest] + 1) % drawn.shape[longest]] + spot[longest + 1:]
    return drawn.at[tuple(spot)].set(low).at[tuple(next_to)].set(high)


def steps_of(own_key, shape, pieces, low, largest):
    def one(dim, shards_of):
        heights = jax.random.uniform(jax.random.fold_in(jax.random.fold_in(own_key, 6), dim), (shards_of,), jnp.float32, low / len(pieces), largest / len(pieces))
        return jnp.repeat(jnp.exp(heights), shape[dim] // shards_of).reshape((-1,) + (1,) * (len(shape) - dim - 1))

    loudness = one(*pieces[0])
    for cut in pieces[1:]:
        loudness = loudness * one(*cut)
    return loudness


def bell_draw(rng, dims, deviation, limit, pieces=(), held_as=jnp.bfloat16):
    level = steps_of(rng, dims, pieces, -0.22, 0.18) if pieces else 1.0
    entries = jax.random.normal(rng, dims, jnp.float32) * deviation * level
    return jnp.minimum(jnp.maximum(entries, -limit), limit).astype(held_as)


def setup_inputs(seed: int = 0) -> dict:
    keys = jax.random.split(jax.random.key(seed), 5)
    return {
        "hidden": bell_draw(keys[0], (RESP, D), 1.0, 6.0, ((0, 16),)),
        "projection": bell_draw(keys[1], (D, E), D ** -0.5, 0.09375, ((1, 8),)),
        "grades": place_ends(jax.random.randint(keys[2], (RESP,), 0, 10), jax.random.fold_in(keys[2], 1), 0, 9).astype(jnp.int32),
        "pattern": draw_pattern(jax.random.fold_in(keys[4], 71), 0),
    }


smoothing_divisor = 64.0
epsilon = 1e-06

def rotate(values):
    half_width = values.shape[1] // 2
    return jnp.concatenate([values[:, half_width:], -values[:, :half_width]], axis=1)

def reference(hidden, projection, grades, pattern):
    projected = jnp.dot(hidden, projection, preferred_element_type=jnp.float32).astype(jnp.bfloat16)
    as_float = projected.astype(jnp.float32)
    row_norms = jnp.sqrt(lax.optimization_barrier(jnp.sum(as_float * as_float, axis=1)) + epsilon)
    unit_rows = as_float / row_norms[:, None]
    unit_bf = unit_rows.astype(jnp.bfloat16)
    turned = rotate(unit_bf)
    blocks_total = pattern.shape[0]
    emb_width = projection.shape[1]
    normalized_partitions = unit_bf.reshape(blocks_total, ANSWERS_PER_SET, emb_width)
    turned_blocks = turned.reshape(blocks_total, ANSWERS_PER_SET, emb_width)
    grade_blocks = grades.astype(jnp.float32).reshape(blocks_total, ANSWERS_PER_SET)
    logit_multiplier = smoothing_divisor / ANSWERS_PER_SET

    def left_step(left_id, grads_all):
        row_mask = pattern[left_id]
        active_order = jnp.argsort(1 - row_mask, stable=True).astype(jnp.int32)
        active = jnp.sum(row_mask).astype(jnp.int32)
        first_answer_patch = normalized_partitions[left_id]
        left_turn = turned_blocks[left_id]
        grade_here = grade_blocks[left_id]

        def right_step(position, state_pair):
            running, grads_now = state_pair
            right_id = active_order[position]
            second_cyclic_shift = turned_blocks[right_id]
            grade_there = grade_blocks[right_id]
            duel_logits = smoothing_divisor * lax.dot_general(first_answer_patch, second_cyclic_shift, (((1,), (1,)), ((), ())), preferred_element_type=jnp.float32)
            label_sign = jnp.sign(grade_here[:, None] - grade_there[None, :])
            slopes = (logit_multiplier * (-label_sign * jax.nn.sigmoid(-label_sign * duel_logits))).astype(jnp.bfloat16)
            running = running + jnp.dot(slopes, second_cyclic_shift, preferred_element_type=jnp.float32)
            right_piece = lax.dot_general(slopes, left_turn, (((0,), (0,)), ((), ())), preferred_element_type=jnp.float32)
            grads_now = grads_now.at[right_id].add(-right_piece)
            return (running, grads_now)
        running, grads_all = lax.fori_loop(0, active, right_step, (jnp.zeros((ANSWERS_PER_SET, emb_width), jnp.float32), grads_all))
        return grads_all.at[left_id].add(running)
    grads_all = lax.fori_loop(0, blocks_total, left_step, jnp.zeros((blocks_total, ANSWERS_PER_SET, emb_width), jnp.float32))
    embed_grad = grads_all.reshape(blocks_total * ANSWERS_PER_SET, emb_width)
    inner_prod = lax.optimization_barrier(jnp.sum(unit_rows * embed_grad, axis=1))
    pre_grad = ((embed_grad - unit_rows * inner_prod[:, None]) / row_norms[:, None]).astype(jnp.bfloat16)
    weight_grad = lax.dot_general(hidden, pre_grad, (((0,), (0,)), ((), ())), preferred_element_type=jnp.float32)
    return (embed_grad, weight_grad)
```

```python
import functools

import jax
import jax.numpy as jnp
import numpy as np
from jax import lax
from jax.experimental import pallas as pl
from jax.experimental.pallas import tpu as pltpu
from jax.sharding import Mesh, PartitionSpec as P

smoothing_divisor = 64.0
epsilon = 1e-06
AXES = ("y", "zh", "core", "x", "zl")
SIZES = (4, 2, 2, 4, 2)
ROW = ("y", "zh", "core")
COL = ("x", "zl")
B = 128


def shift(value, axis, by):
    size = SIZES[AXES.index(axis)]
    return lax.ppermute(value, axis, [(i, (i + by) % size) for i in range(size)])


def ring(value, axis):
    half = value.shape[0] // 2
    below = shift(value, axis, 1)
    above = shift(value, axis, -1)
    far_low = shift(below[:half], axis, 1)
    far_high = shift(above[half:], axis, -1)
    return value, above, jnp.concatenate([far_low, far_high], axis=0), below


def pair_kernel(active_ref, weight_ref, left_grade_ref, right_grade_ref, extra_ref, left_ref, right_ref, out_ref, acc, inner):
    step = pl.program_id(0)
    rows = 256

    @pl.when(step == 0)
    def _():
        acc[...] = jnp.zeros_like(acc)
        inner[...] = jnp.zeros_like(inner)

    for part in range(4):
        @pl.when(active_ref[part, step] > 0)
        def _(part=part):
            at = pl.ds(part * rows, rows)
            right = right_ref[...]
            scores = lax.dot_general(
                left_ref[at, :], right, (((1,), (1,)), ((), ())), preferred_element_type=jnp.float32
            )
            diff = left_grade_ref[at, :] - right_grade_ref[0]
            weight = weight_ref[0, part * 2 : part * 2 + 2, :]
            weight = jnp.concatenate(
                [jnp.broadcast_to(weight[0:1], (B, 256)), jnp.broadcast_to(weight[1:2], (B, 256))], axis=0
            )
            ahead = diff > 0
            factor = jnp.where(ahead, -weight, jnp.where(diff < 0, weight, 0.0))
            grown = jnp.exp(jnp.where(ahead, scores, -scores))
            slopes = (factor / (1.0 + grown)).astype(jnp.bfloat16)
            terms = slopes.astype(jnp.float32) * scores
            inner[at, :] += terms[:, :128] + terms[:, 128:]
            acc[at, :] += jnp.dot(slopes, right, preferred_element_type=jnp.float32)

    @pl.when(step == pl.num_programs(0) - 1)
    def _():
        for chunk in range(8):
            source = (chunk + 4) % 8
            values = acc[:, source * 256 : (source + 1) * 256]
            out_ref[chunk, :1024, :] = (values if chunk < 4 else -values).astype(jnp.bfloat16)
        lines = [jnp.sum(inner[k * 256 : (k + 1) * 256, :].T, axis=0, keepdims=True) for k in range(4)]
        whole = jnp.concatenate(lines, axis=0) * (1.0 / smoothing_divisor)
        high = whole.astype(jnp.bfloat16).astype(jnp.float32)
        tail = jnp.concatenate([high, whole - high, extra_ref[...]], axis=0).astype(jnp.bfloat16)
        for chunk in range(8):
            out_ref[chunk, 1024:, :] = tail


def pair_pass(active, weight, left_grade, right_grade, extra, left, right):
    return pl.pallas_call(
        pair_kernel,
        grid=(8,),
        in_specs=[
            pl.BlockSpec(memory_space=pltpu.SMEM),
            pl.BlockSpec((1, 8, 256), lambda s: (s, 0, 0)),
            pl.BlockSpec((1024, 1), lambda s: (0, 0)),
            pl.BlockSpec((1, 1, 256), lambda s: (s, 0, 0)),
            pl.BlockSpec((8, 256), lambda s: (0, 0)),
            pl.BlockSpec((1024, 2048), lambda s: (0, 0)),
            pl.BlockSpec((256, 2048), lambda s: (s, 0)),
        ],
        out_specs=pl.BlockSpec((8, 1040, 256), lambda s: (0, 0, 0)),
        out_shape=jax.ShapeDtypeStruct((8, 1040, 256), jnp.bfloat16),
        scratch_shapes=[pltpu.VMEM((1024, 2048), jnp.float32), pltpu.VMEM((1024, 128), jnp.float32)],
        compiler_params=pltpu.CompilerParams(vmem_limit_bytes=48 * 2**20),
        cost_estimate=pl.CostEstimate(flops=12 * 10**9, bytes_accessed=18 * 2**20, transcendentals=2**21),
    )(active, weight, left_grade, right_grade, extra, left, right)


def split_two(values):
    high = values.astype(jnp.bfloat16)
    return high, (values - high.astype(jnp.float32)).astype(jnp.bfloat16)


def shards(hidden, projection, grades, pattern):
    y, zh, core, x, zl = (lax.axis_index(a) for a in AXES)
    row_here = (y * 2 + zh) * 2 + core
    col_here = x * 2 + zl

    grade_mine = grades.astype(jnp.float32).reshape(1, B)
    two = jnp.concatenate([grade_mine, shift(grade_mine, "core", 1)], axis=0)
    four = jnp.concatenate([two, shift(two, "zh", 1)], axis=0)
    right_grade = jnp.concatenate([four] + [shift(four, "y", -d) for d in (1, 2, 3)], axis=0)

    projected = jnp.dot(hidden, projection, preferred_element_type=jnp.float32).astype(jnp.bfloat16)
    grade_rows = jnp.broadcast_to(
        jnp.tile(grade_mine, (1, 2)).astype(jnp.bfloat16)[None], (8, 16, 256)
    )
    sent = jnp.concatenate([projected.reshape(8, B, 256), grade_rows], axis=1)
    came = lax.all_to_all(sent, COL, 0, 0, tiled=True)
    left_grade = came[:, B, :B].astype(jnp.float32).reshape(1024, 1)
    own = jnp.concatenate([came[k, :B] for k in range(8)], axis=1).astype(jnp.float32)
    own_norm = jnp.sqrt(jnp.sum(own * own, axis=1) + epsilon)
    unit = (own / own_norm[:, None]).astype(jnp.bfloat16)
    scaled = unit * jnp.bfloat16(smoothing_divisor)
    turned = jnp.concatenate([-scaled[:, 1024:], scaled[:, :1024]], axis=1)

    turned_z = shift(turned, "zl", 1)
    unit_z = shift(unit, "zh", 1)
    left_a = ring(turned, "x")
    right_a = ring(unit, "y")
    left_b = ring(turned_z, "x")
    right_b = ring(unit_z, "y")
    left = jnp.zeros((1024, 2048), jnp.bfloat16)
    for distance in range(4):
        at = (x + distance) % 4 * 2
        left = lax.dynamic_update_slice_in_dim(left, left_a[distance], (at + zl) * B, 0)
        left = lax.dynamic_update_slice_in_dim(left, left_b[distance], (at + 1 - zl) * B, 0)
    near = jnp.concatenate([right_a[0], right_b[0], right_a[1], right_b[1], right_a[3], right_b[3]], axis=0)
    far = jnp.concatenate([right_a[2], right_b[2]], axis=0)
    right = jnp.concatenate([near, shift(near, "core", 1), far, shift(far, "core", 1)], axis=0)

    order = [(d, z, 0) for d in (0, 1, 3) for z in (0, 1)] + [(d, z, 1) for d in (0, 1, 3) for z in (0, 1)]
    order += [(2, z, c) for c in (0, 1) for z in (0, 1)]
    blocks = jnp.stack([((((y + d) % 4) * 2 + (zh ^ z)) * 2 + (core ^ c)) * 8 + col_here for d, z, c in order])
    right_grade = jnp.concatenate([right_grade[(d * 2 + z) * 2 + c][None] for d, z, c in order], axis=0)
    both = (pattern + pattern.T).astype(jnp.float32)
    home = lax.dynamic_slice_in_dim(both, row_here * 8, 8, 0)
    picked = (lax.broadcasted_iota(jnp.int32, (128, 16), 0) == blocks[None, :]).astype(jnp.float32)
    tiles = jnp.dot(home, picked, preferred_element_type=jnp.float32)
    active = (tiles.reshape(4, 2, 8, 2).sum(axis=(1, 3)) > 0).astype(jnp.int32)
    half = tiles * (smoothing_divisor / B)
    weight = jnp.repeat(half.reshape(8, 8, 2).transpose(1, 0, 2), B, axis=2)

    norm_high, norm_low = split_two(own_norm)
    extra = jnp.concatenate([norm_high, norm_low]).astype(jnp.float32)
    extra = jnp.broadcast_to(extra[None], (8, 256))
    sums = pair_pass(active, weight, left_grade, right_grade.reshape(8, 1, 256), extra, left, right)
    back = lax.all_to_all(sums, COL, 0, 0, tiled=True)

    grads = jnp.sum(back[:, :1024].astype(jnp.float32), axis=0)
    tail = back[:, 1024:].astype(jnp.float32)
    inner_prod = jnp.sum(tail[:, 0:4] + tail[:, 4:8], axis=0).reshape(1024)
    row_norms = (tail[:, 8, :B] + tail[:, 8, B:]).reshape(1024)
    unit_rows = projected.astype(jnp.float32) / row_norms[:, None]
    pre_grad = ((grads - unit_rows * inner_prod[:, None]) / row_norms[:, None]).astype(jnp.bfloat16)
    weight_part = lax.dot_general(
        hidden, pre_grad, (((0,), (0,)), ((), ())), preferred_element_type=jnp.float32
    ).reshape(8, 2, 224, 256)
    keep = lax.dynamic_index_in_dim(weight_part, core, 1, False)
    give = lax.dynamic_index_in_dim(weight_part, 1 - core, 1, False)
    chip = (keep + shift(give, "core", 1)).astype(jnp.bfloat16)
    gathered = lax.all_to_all(chip, ("y", "zh"), 0, 0, tiled=True)
    weight_grad = jnp.sum(gathered.astype(jnp.float32), axis=0)
    return grads, weight_grad


def solution(mesh):
    fine = Mesh(np.asarray(mesh.devices).reshape(SIZES), AXES)
    return jax.shard_map(
        shards,
        mesh=fine,
        in_specs=(P(ROW, None), P(None, COL), P(ROW + COL), P()),
        out_specs=(P(ROW, COL), P(ROW, COL)),
        check_vma=False,
    )
```

```python
import functools

import jax
import jax.numpy as jnp
import numpy as np
from jax import lax
from jax.experimental import pallas as pl
from jax.experimental.pallas import tpu as pltpu
from jax.sharding import Mesh, PartitionSpec as P

smoothing_divisor = 64.0
epsilon = 1e-06
AXES = ("y", "zh", "core", "x", "zl")
SIZES = (4, 2, 2, 4, 2)
ROW = ("y", "zh", "core")
COL = ("x", "zl")
B = 128
PAIR = 2 * B
QUAD = 4 * B
WIDTH = 2048
ANY = pl.BlockSpec(memory_space=pltpu.HBM)
SMEM = pl.BlockSpec(memory_space=pltpu.SMEM)

LEFT = (0, 1, 3, 2)
RIGHT = ((0, 0), (0, 1), (1, 0), (3, 0), (1, 1), (3, 1), (2, 0), (2, 1))


def shift(value, axis, by):
    size = SIZES[AXES.index(axis)]
    return lax.ppermute(value, axis, [(i, (i + by) % size) for i in range(size)])


def whole(*shape):
    return pl.BlockSpec(shape, lambda *_: (0,) * len(shape))


def fetch(parts, buffer, sems):
    for k, pieces in enumerate(parts):
        row = 0
        for ref, first, rows in pieces:
            pltpu.make_async_copy(ref.at[pl.ds(first, rows)], buffer.at[k, pl.ds(row, rows)], sems.at[k]).start()
            row += rows


def visit(slot, right_slot, left_buf, right_buf, weight_ref, left_grade_ref, right_grade_ref, acc, inner):
    right = right_buf[right_slot]
    scores = lax.dot_general(left_buf[slot], right, (((1,), (1,)), ((), ())), preferred_element_type=jnp.float32)
    label = jnp.clip(left_grade_ref[slot] - right_grade_ref[right_slot], -1.0, 1.0)
    weight = weight_ref[right_slot, slot]
    weight = jnp.concatenate(
        [jnp.broadcast_to(weight[0:1], (B, QUAD)), jnp.broadcast_to(weight[1:2], (B, QUAD))], axis=0
    )
    grown = jnp.exp(label * scores)
    slopes = (label * weight / (1.0 + grown)).astype(jnp.bfloat16)
    terms = slopes.astype(jnp.float32) * scores
    inner[slot] += (terms[:, :B] + terms[:, B:PAIR]) + (terms[:, PAIR : 3 * B] + terms[:, 3 * B :])
    acc[slot] += jnp.dot(slopes, right, preferred_element_type=jnp.float32)


def sweep(lefts, rights, active_ref, left_buf, right_buf, left_sem, right_sem, body):
    fetch(lefts, left_buf, left_sem)
    fetch(rights, right_buf, right_sem)
    for k in range(len(lefts)):
        pltpu.make_async_copy(left_buf.at[k], left_buf.at[k], left_sem.at[k]).wait()

    def one(right_slot, carry):
        pltpu.make_async_copy(right_buf.at[right_slot], right_buf.at[right_slot], right_sem.at[right_slot]).wait()
        for slot in range(len(lefts)):

            @pl.when(active_ref[slot, right_slot] > 0)
            def _(slot=slot):
                body(slot, right_slot)

        return carry

    lax.fori_loop(0, len(rights), one, 0)


def group(refs, layout):
    return [[(refs[place], first, rows) for place, first, rows in pieces] for pieces in layout]


def near_kernel(lefts, rights, count, *refs):
    active_ref, weight_ref, left_grade_ref, right_grade_ref = refs[:4]
    arrays = refs[4 : 4 + count]
    acc, inner, left_buf, right_buf, left_sem, right_sem = refs[4 + count :]
    acc[...] = jnp.zeros_like(acc)
    inner[...] = jnp.zeros_like(inner)
    body = lambda s, r: visit(
        s, r, left_buf, right_buf, weight_ref, left_grade_ref, right_grade_ref, acc, inner
    )
    sweep(group(arrays, lefts), group(arrays, rights), active_ref, left_buf, right_buf, left_sem, right_sem, body)


def far_kernel(lefts, rights, count, *refs):
    place_ref, active_ref, weight_ref, left_grade_ref, right_grade_ref, extra_ref, near_acc, near_inner = refs[:8]
    arrays = refs[8 : 8 + count]
    out_ref, acc, inner, lines, left_buf, right_buf, left_sem, right_sem, acc_sem = refs[8 + count :]
    acc_copy = pltpu.make_async_copy(near_acc, acc.at[pl.ds(0, 3)], acc_sem)
    acc_copy.start()
    inner[:3] = near_inner[...]
    inner[3] = jnp.zeros((PAIR, B), jnp.float32)
    acc[3] = jnp.zeros((PAIR, WIDTH), jnp.float32)
    acc_copy.wait()
    body = lambda s, r: visit(
        s, r, left_buf, right_buf, weight_ref, left_grade_ref, right_grade_ref, acc, inner
    )
    sweep(group(arrays, lefts), group(arrays, rights), active_ref, left_buf, right_buf, left_sem, right_sem, body)
    for slot in range(4):
        place = place_ref[slot]
        at = pl.ds(pl.multiple_of(place * PAIR, PAIR), PAIR)
        for chunk in range(8):
            source = (chunk + 4) % 8
            values = acc[slot, :, source * PAIR : (source + 1) * PAIR]
            out_ref[chunk, at, :] = (values if chunk < 4 else -values).astype(jnp.bfloat16)
        lines[place] = jnp.sum(inner[slot].T, axis=0, keepdims=True) * (1.0 / smoothing_divisor)
    total = jnp.concatenate([lines[k] for k in range(4)], axis=0)
    high = total.astype(jnp.bfloat16).astype(jnp.float32)
    tail = jnp.concatenate([high, total - high, extra_ref[...]], axis=0).astype(jnp.bfloat16)
    for chunk in range(8):
        out_ref[chunk, 1024:, :] = tail


def near_pass(active, weight, left_grade, right_grade, arrays, lefts, rights):
    shapes = ((3, PAIR, WIDTH), (3, PAIR, B))
    return pl.pallas_call(
        functools.partial(near_kernel, lefts, rights, len(arrays)),
        in_specs=[SMEM, whole(*weight.shape), whole(*left_grade.shape), whole(*right_grade.shape)] + [ANY] * len(arrays),
        out_specs=[whole(*s) for s in shapes],
        out_shape=[jax.ShapeDtypeStruct(s, jnp.float32) for s in shapes],
        scratch_shapes=[
            pltpu.VMEM((3, PAIR, WIDTH), jnp.bfloat16),
            pltpu.VMEM((3, QUAD, WIDTH), jnp.bfloat16),
            pltpu.SemaphoreType.DMA((3,)),
            pltpu.SemaphoreType.DMA((3,)),
        ],
        compiler_params=pltpu.CompilerParams(vmem_limit_bytes=60 * 2**20),
        cost_estimate=pl.CostEstimate(flops=9 * 10**9, bytes_accessed=16 * 2**20, transcendentals=2**21),
        name="near_tiles",
    )(active, weight, left_grade, right_grade, *arrays)


def far_pass(place, active, weight, left_grade, right_grade, extra, near_acc, near_inner, arrays, lefts, rights):
    return pl.pallas_call(
        functools.partial(far_kernel, lefts, rights, len(arrays)),
        in_specs=[SMEM, SMEM, whole(*weight.shape), whole(*left_grade.shape), whole(*right_grade.shape)]
        + [whole(*extra.shape), ANY, whole(*near_inner.shape)]
        + [ANY] * len(arrays),
        out_specs=whole(8, 1040, PAIR),
        out_shape=jax.ShapeDtypeStruct((8, 1040, PAIR), jnp.bfloat16),
        scratch_shapes=[
            pltpu.VMEM((4, PAIR, WIDTH), jnp.float32),
            pltpu.VMEM((4, PAIR, B), jnp.float32),
            pltpu.VMEM((4, 1, PAIR), jnp.float32),
            pltpu.VMEM((4, PAIR, WIDTH), jnp.bfloat16),
            pltpu.VMEM((4, QUAD, WIDTH), jnp.bfloat16),
            pltpu.SemaphoreType.DMA((4,)),
            pltpu.SemaphoreType.DMA((4,)),
            pltpu.SemaphoreType.DMA,
        ],
        compiler_params=pltpu.CompilerParams(vmem_limit_bytes=60 * 2**20),
        cost_estimate=pl.CostEstimate(flops=8 * 10**9, bytes_accessed=24 * 2**20, transcendentals=2**21),
        name="far_tiles",
    )(place, active, weight, left_grade, right_grade, extra, near_acc, near_inner, *arrays)


def across(line, rows):
    column = jnp.broadcast_to(line, (B, rows)).T
    return jnp.concatenate([column, column], axis=1)


def weight_kernel(core_ref, back_ref, projected_ref, hidden_ref, grads_ref, give_ref, keep_ref, pre):
    @pl.when(pl.program_id(0) == 0)
    def _():
        tail = back_ref[:, 1024:, :].astype(jnp.float32)
        inner = jnp.sum(tail[:, 0:4] + tail[:, 4:8], axis=0)
        for part in range(8):
            at = pl.ds(part * B, B)
            grads = back_ref[0, at, :].astype(jnp.float32)
            for source in range(1, 8):
                grads += back_ref[source, at, :].astype(jnp.float32)
            grads_ref[at, :] = grads
            norm = across(tail[part, 8:9, :B] + tail[part, 8:9, B:], B)
            half = part % 2 * B
            product = across(inner[part // 2 : part // 2 + 1, half : half + B], B)
            unit = projected_ref[at, :].astype(jnp.float32) / norm
            pre[at, :] = ((grads - unit * product) / norm).astype(jnp.bfloat16)

    product = lax.dot_general(
        hidden_ref[...], pre[...], (((0,), (0,)), ((), ())), preferred_element_type=jnp.float32
    )
    core = core_ref[0]
    for k in range(2):
        even = product[2 * k * 224 : (2 * k + 1) * 224].astype(jnp.bfloat16)
        odd = product[(2 * k + 1) * 224 : (2 * k + 2) * 224].astype(jnp.bfloat16)
        mine = core == 0
        keep_ref[k] = jnp.where(mine, even, odd)
        give_ref[k] = jnp.where(mine, odd, even)


def weight_pass(core, back, projected, hidden):
    halves = pl.BlockSpec((2, 224, PAIR), lambda s: (s, 0, 0))
    return pl.pallas_call(
        weight_kernel,
        grid=(4,),
        in_specs=[
            SMEM,
            whole(8, 1040, PAIR),
            whole(1024, PAIR),
            pl.BlockSpec((1024, 896), lambda s: (0, s)),
        ],
        out_specs=[whole(1024, PAIR), halves, halves],
        out_shape=[
            jax.ShapeDtypeStruct((1024, PAIR), jnp.float32),
            jax.ShapeDtypeStruct((8, 224, PAIR), jnp.bfloat16),
            jax.ShapeDtypeStruct((8, 224, PAIR), jnp.bfloat16),
        ],
        scratch_shapes=[pltpu.VMEM((1024, PAIR), jnp.bfloat16)],
        compiler_params=pltpu.CompilerParams(vmem_limit_bytes=32 * 2**20),
        cost_estimate=pl.CostEstimate(flops=2 * 10**9, bytes_accessed=15 * 2**20, transcendentals=0),
        name="weight_terms",
    )(core, back, projected, hidden)


def split_two(values):
    high = values.astype(jnp.bfloat16)
    return high, (values - high.astype(jnp.float32)).astype(jnp.bfloat16)


def shards(hidden, projection, grades, pattern):
    y, zh, core, x, zl = (lax.axis_index(a) for a in AXES)
    col_here = x * 2 + zl
    grade_mine = grades.astype(jnp.bfloat16)

    projected = jnp.dot(hidden, projection, preferred_element_type=jnp.float32).astype(jnp.bfloat16)
    grade_rows = jnp.broadcast_to(jnp.tile(grade_mine, 2), (4, 2, 16, PAIR))
    pairs = jnp.broadcast_to(projected.reshape(4, 1, PAIR, PAIR), (4, 2, PAIR, PAIR))
    sent = jnp.concatenate([pairs, grade_rows], axis=2).reshape(8, PAIR + 16, PAIR)
    came = lax.all_to_all(sent, COL, 0, 0, tiled=True)
    left_grade = came[:, PAIR, :B].astype(jnp.float32).reshape(4, PAIR)
    rows = jnp.concatenate([came[k, :PAIR] for k in range(8)], axis=1).astype(jnp.float32)
    norms = jnp.sqrt(jnp.sum(rows * rows, axis=1) + epsilon)
    unit_pair = (rows / norms[:, None]).astype(jnp.bfloat16)
    own_norm = lax.dynamic_slice_in_dim(norms, zl * B, B, 0)
    unit = lax.dynamic_slice_in_dim(unit_pair, zl * B, B, 0)
    grade_lines = jnp.pad(grade_mine[None], ((0, 7), (0, WIDTH - B)))
    unit = jnp.concatenate([unit, grade_lines], axis=0)
    scaled = unit_pair * jnp.bfloat16(smoothing_divisor)
    turned = jnp.concatenate([-scaled[:, 1024:], scaled[:, :1024]], axis=1)

    below0 = shift(turned[:B], "x", 1)
    above1 = shift(turned[B:], "x", -1)
    y_below = shift(unit, "y", 1)
    y_above = shift(unit, "y", -1)
    unit_z = shift(unit, "zh", 1)
    below0, above1, y_below, y_above, unit_z, turned, unit = lax.optimization_barrier(
        (below0, above1, y_below, y_above, unit_z, turned, unit)
    )
    below1 = shift(turned[B:], "x", 1)
    above0 = shift(turned[:B], "x", -1)
    z_below = shift(unit_z, "y", 1)
    z_above = shift(unit_z, "y", -1)
    other0 = shift(jnp.concatenate([unit[:B], unit_z[:B], unit[B:], unit_z[B:]], axis=0), "core", 1)
    below0, above1, y_below, z_above, below1, above0, z_below, other0 = lax.optimization_barrier(
        (below0, above1, y_below, z_above, below1, above0, z_below, other0)
    )
    far0 = shift(below0, "x", 1)
    far1 = shift(above1, "x", -1)
    y_far = shift(y_below, "y", 1)
    z_far = shift(z_above, "y", -1)
    ring = (y_above, z_above, y_below, z_below)
    other1 = shift(jnp.concatenate([r[:B] for r in ring] + [r[B:] for r in ring], axis=0), "core", 1)

    def grade_quad(*pieces):
        return jnp.concatenate([array[row, :B] for array, row in pieces])

    right_grade = jnp.stack(
        [
            grade_quad((unit, B), (unit_z, B), (other0, 2 * B), (other0, 2 * B + 8)),
            grade_quad(*((r, B) for r in ring)),
            grade_quad(*((other1, 4 * B + 8 * k) for k in range(4))),
        ]
    ).astype(jnp.float32)[:, None]
    both = (pattern + pattern.T).astype(jnp.float32)
    row_here = ((y * 2 + zh) * 2 + core) * 8
    left_ids = jnp.stack([row_here + (x + d) % 4 * 2 + k for d in LEFT for k in (0, 1)])
    right_ids = jnp.stack(
        [((((y + d) % 4) * 2 + (zh ^ z)) * 2 + (core ^ c)) * 8 + col_here for d, c in RIGHT for z in (0, 1)]
    )
    left_pick = (left_ids[:, None] == jnp.arange(128)[None]).astype(jnp.float32)
    right_pick = (jnp.arange(128)[:, None] == right_ids[None]).astype(jnp.float32)
    tiles = jnp.dot(
        jnp.dot(left_pick, both, preferred_element_type=jnp.float32), right_pick, preferred_element_type=jnp.float32
    )
    tiles = tiles.reshape(4, 2, 4, 4)
    active = (tiles.sum(axis=(1, 3)) > 0).astype(jnp.int32)
    steps = tiles * (-smoothing_divisor / B)
    weight = jnp.repeat(steps.transpose(2, 0, 1, 3), B, axis=3)
    place = jnp.stack([(x + d) % 4 for d in LEFT]).astype(jnp.int32)
    twice = jnp.concatenate([left_grade, left_grade], axis=0)
    turned_grade = lax.dynamic_slice_in_dim(twice, x, 4, 0)
    left_grade = jnp.stack([turned_grade[d] for d in LEFT])[:, :, None]

    norm_high, norm_low = split_two(own_norm)
    extra = jnp.concatenate([norm_high, norm_low]).astype(jnp.float32)
    extra = jnp.broadcast_to(extra[None], (8, PAIR))

    one = lambda place, first=0: (place, first, B)
    lefts = [[(0, 0, PAIR)], [one(1), one(2)], [one(3), one(4)]]
    rights = [[one(5), one(6), (7, 0, PAIR)], [one(8), one(9), one(10), one(11)], [(12, 0, QUAD)]]
    arrays = [turned, above0, above1, below0, below1, unit, unit_z, other0, *ring, other1]
    near_active = active[:3, :3]
    near_acc, near_inner = near_pass(
        near_active, weight[:3, :3], left_grade[:3], right_grade, arrays, lefts, rights
    )
    y_far, z_far, far0, far1, near_acc, near_inner = lax.optimization_barrier(
        (y_far, z_far, far0, far1, near_acc, near_inner)
    )
    other2 = shift(y_far, "core", 1)
    other3 = shift(z_far, "core", 1)
    far_grade = grade_quad((y_far, B), (z_far, B), (other2, B), (other3, B)).astype(jnp.float32)[None, None]
    count = len(arrays)
    lefts = lefts + [[one(count), one(count + 1)]]
    rights = rights + [[one(count + k) for k in (2, 3, 4, 5)]]
    arrays = arrays + [far0, far1, y_far, z_far, other2, other3]
    left_over = active * jnp.asarray(np.maximum(*np.indices((4, 4))) == 3, jnp.int32)
    sums = far_pass(
        place,
        left_over,
        weight,
        left_grade,
        jnp.concatenate([right_grade, far_grade], axis=0),
        extra,
        near_acc,
        near_inner,
        arrays,
        lefts,
        rights,
    )
    back = lax.all_to_all(sums, COL, 0, 0, tiled=True)

    grads, give, keep = weight_pass(core.astype(jnp.int32).reshape(1), back, projected, hidden)
    chip = (keep.astype(jnp.float32) + shift(give, "core", 1).astype(jnp.float32)).astype(jnp.bfloat16)
    gathered = lax.all_to_all(chip, ("y", "zh"), 0, 0, tiled=True)
    weight_grad = jnp.sum(gathered.astype(jnp.float32), axis=0)
    return grads, weight_grad


def solution(mesh):
    fine = Mesh(np.asarray(mesh.devices).reshape(SIZES), AXES)
    return jax.shard_map(
        shards,
        mesh=fine,
        in_specs=(P(ROW, None), P(None, COL), P(ROW + COL), P()),
        out_specs=(P(ROW, COL), P(ROW, COL)),
        check_vma=False,
    )
```

```python
import functools

import jax
import jax.numpy as jnp
import numpy as np
from jax import lax
from jax.experimental import pallas as pl
from jax.experimental.pallas import tpu as pltpu
from jax.sharding import Mesh, PartitionSpec as P

smoothing_divisor = 64.0
epsilon = 1e-06
AXES = ("y", "zh", "core", "x", "zl")
SIZES = (4, 2, 2, 4, 2)
ROW = ("y", "zh", "core")
COL = ("x", "zl")
B = 128
PAIR = 2 * B
QUAD = 4 * B
WIDTH = 2048
ANY = pl.BlockSpec(memory_space=pltpu.HBM)
SMEM = pl.BlockSpec(memory_space=pltpu.SMEM)

LEFT = (0, 1, 3, 2)
RIGHT = ((0, 0), (0, 1), (1, 0), (3, 0), (1, 1), (3, 1), (2, 0), (2, 1))


def shift(value, axis, by):
    size = SIZES[AXES.index(axis)]
    return lax.ppermute(value, axis, [(i, (i + by) % size) for i in range(size)])


def whole(*shape):
    return pl.BlockSpec(shape, lambda *_: (0,) * len(shape))


def fetch(pieces, buffer, sem):
    row = 0
    for ref in pieces:
        pltpu.make_async_copy(ref, buffer.at[pl.ds(row, ref.shape[0])], sem).start()
        row += ref.shape[0]


def filled(buffer, sem):
    pltpu.make_async_copy(buffer, buffer, sem).wait()


def tile(slot, quad, left_buf, right_buf, weight_ref, left_grade_ref, right_grade_ref, acc, inner):
    right = right_buf[quad]
    scores = lax.dot_general(left_buf[slot], right, (((1,), (1,)), ((), ())), preferred_element_type=jnp.float32)
    label = jnp.clip(left_grade_ref[slot] - right_grade_ref[quad], -1.0, 1.0)
    weight = weight_ref[quad, slot]
    weight = jnp.concatenate(
        [jnp.broadcast_to(weight[0:1], (B, QUAD)), jnp.broadcast_to(weight[1:2], (B, QUAD))], axis=0
    )
    grown = jnp.exp(label * scores)
    slopes = (label * weight / (1.0 + grown)).astype(jnp.bfloat16)
    terms = slopes.astype(jnp.float32) * scores
    inner[slot] += (terms[:, :B] + terms[:, B:PAIR]) + (terms[:, PAIR : 3 * B] + terms[:, 3 * B :])
    acc[slot] += jnp.dot(slopes, right, preferred_element_type=jnp.float32)


def near_kernel(active_ref, weight_ref, left_grade_ref, right_grade_ref, *refs):
    lefts = (refs[0:2], refs[2:4], refs[4:6])
    rights = (refs[6:9], refs[9:13], refs[13:14])
    acc_out, inner, acc, left_buf, right_buf, left_sem, right_sem, acc_sem = refs[14:]
    for k in range(3):
        fetch(lefts[k], left_buf.at[k], left_sem.at[k])
        fetch(rights[k], right_buf.at[k], right_sem.at[k])
    acc[...] = jnp.zeros_like(acc)
    inner[...] = jnp.zeros_like(inner)

    def one(quad, carry):
        filled(right_buf.at[quad], right_sem.at[quad])
        for slot in range(3):

            @pl.when(quad == 0)
            def _(slot=slot):
                filled(left_buf.at[slot], left_sem.at[slot])

            @pl.when(active_ref[slot, quad] > 0)
            def _(slot=slot):
                tile(slot, quad, left_buf, right_buf, weight_ref, left_grade_ref, right_grade_ref, acc, inner)

            @pl.when(quad == 2)
            def _(slot=slot):
                pltpu.make_async_copy(acc.at[slot], acc_out.at[slot], acc_sem.at[slot]).start()

        return carry

    lax.fori_loop(0, 3, one, 0)
    for slot in range(3):
        pltpu.make_async_copy(acc.at[slot], acc_out.at[slot], acc_sem.at[slot]).wait()


def far_kernel(place_ref, active_ref, weight_ref, left_grade_ref, right_grade_ref, extra_ref, near_inner, near_acc, *refs):
    lefts = (refs[0:2], refs[2:4], refs[4:6], refs[6:8])
    rights = (refs[8:11], refs[11:15], refs[15:16], refs[16:20])
    out_ref, acc, inner, lines, sent, tail, left_buf, right_buf, left_sem, right_sem, acc_sem, sent_sem, tail_sem = refs[20:]
    fetch(rights[3], right_buf.at[3], right_sem.at[3])
    for k in range(3):
        fetch(lefts[k], left_buf.at[k], left_sem.at[k])
        pltpu.make_async_copy(near_acc.at[k], acc.at[k], acc_sem.at[k]).start()
    fetch(lefts[3], left_buf.at[3], left_sem.at[3])
    for k in range(3):
        fetch(rights[k], right_buf.at[k], right_sem.at[k])
    inner[:3] = near_inner[...]
    inner[3] = jnp.zeros((PAIR, B), jnp.float32)
    acc[3] = jnp.zeros((PAIR, WIDTH), jnp.float32)

    def run(slot, quad):
        @pl.when(active_ref[slot, quad] > 0)
        def _():
            tile(slot, quad, left_buf, right_buf, weight_ref, left_grade_ref, right_grade_ref, acc, inner)

    def home(slot):
        at = pl.ds(pl.multiple_of(place_ref[slot] * PAIR, PAIR), PAIR)
        return pltpu.make_async_copy(sent.at[slot], out_ref.at[:, at, :], sent_sem.at[slot])

    def finish(slot):
        for chunk in range(8):
            source = (chunk + 4) % 8
            values = acc[slot, :, source * PAIR : (source + 1) * PAIR]
            sent[slot, chunk] = (values if chunk < 4 else -values).astype(jnp.bfloat16)
        home(slot).start()
        lines[place_ref[slot]] = jnp.sum(inner[slot].T, axis=0, keepdims=True) * (1.0 / smoothing_divisor)

    filled(right_buf.at[3], right_sem.at[3])
    for slot in range(3):
        filled(left_buf.at[slot], left_sem.at[slot])
        filled(acc.at[slot], acc_sem.at[slot])
        run(slot, 3)
        finish(slot)
    filled(left_buf.at[3], left_sem.at[3])

    def one(quad, carry):
        @pl.when(quad < 3)
        def _():
            filled(right_buf.at[quad], right_sem.at[quad])

        run(3, quad)
        return carry

    lax.fori_loop(0, 4, one, 0)
    finish(3)
    total = jnp.concatenate([lines[k] for k in range(4)], axis=0)
    high = total.astype(jnp.bfloat16).astype(jnp.float32)
    last = jnp.concatenate([high, total - high, extra_ref[...]], axis=0).astype(jnp.bfloat16)
    for chunk in range(8):
        tail[chunk] = last
    tail_copy = pltpu.make_async_copy(tail, out_ref.at[:, pl.ds(1024, 16), :], tail_sem)
    tail_copy.start()
    for slot in range(4):
        home(slot).wait()
    tail_copy.wait()


def near_pass(active, weight, left_grade, right_grade, lefts, rights):
    arrays = [a for group in (lefts, rights) for pieces in group for a in pieces]
    return pl.pallas_call(
        near_kernel,
        in_specs=[SMEM, whole(*weight.shape), whole(*left_grade.shape), whole(*right_grade.shape)] + [ANY] * len(arrays),
        out_specs=[ANY, whole(3, PAIR, B)],
        out_shape=[
            jax.ShapeDtypeStruct((3, PAIR, WIDTH), jnp.float32),
            jax.ShapeDtypeStruct((3, PAIR, B), jnp.float32),
        ],
        scratch_shapes=[
            pltpu.VMEM((3, PAIR, WIDTH), jnp.float32),
            pltpu.VMEM((3, PAIR, WIDTH), jnp.bfloat16),
            pltpu.VMEM((3, QUAD, WIDTH), jnp.bfloat16),
            pltpu.SemaphoreType.DMA((3,)),
            pltpu.SemaphoreType.DMA((3,)),
            pltpu.SemaphoreType.DMA((3,)),
        ],
        compiler_params=pltpu.CompilerParams(vmem_limit_bytes=60 * 2**20),
        cost_estimate=pl.CostEstimate(flops=9 * 10**9, bytes_accessed=16 * 2**20, transcendentals=2**21),
        name="near_tiles",
    )(active, weight, left_grade, right_grade, *arrays)


def far_pass(place, active, weight, left_grade, right_grade, extra, near_inner, near_acc, lefts, rights):
    arrays = [a for group in (lefts, rights) for pieces in group for a in pieces]
    return pl.pallas_call(
        far_kernel,
        in_specs=[SMEM, SMEM, whole(*weight.shape), whole(*left_grade.shape), whole(*right_grade.shape)]
        + [whole(*extra.shape), whole(*near_inner.shape), ANY]
        + [ANY] * len(arrays),
        out_specs=ANY,
        out_shape=jax.ShapeDtypeStruct((8, 1040, PAIR), jnp.bfloat16),
        scratch_shapes=[
            pltpu.VMEM((4, PAIR, WIDTH), jnp.float32),
            pltpu.VMEM((4, PAIR, B), jnp.float32),
            pltpu.VMEM((4, 1, PAIR), jnp.float32),
            pltpu.VMEM((4, 8, PAIR, PAIR), jnp.bfloat16),
            pltpu.VMEM((8, 16, PAIR), jnp.bfloat16),
            pltpu.VMEM((4, PAIR, WIDTH), jnp.bfloat16),
            pltpu.VMEM((4, QUAD, WIDTH), jnp.bfloat16),
            pltpu.SemaphoreType.DMA((4,)),
            pltpu.SemaphoreType.DMA((4,)),
            pltpu.SemaphoreType.DMA((3,)),
            pltpu.SemaphoreType.DMA((4,)),
            pltpu.SemaphoreType.DMA,
        ],
        compiler_params=pltpu.CompilerParams(vmem_limit_bytes=60 * 2**20),
        cost_estimate=pl.CostEstimate(flops=8 * 10**9, bytes_accessed=24 * 2**20, transcendentals=2**21),
        name="far_tiles",
    )(place, active, weight, left_grade, right_grade, extra, near_inner, near_acc, *arrays)


def across(line, rows):
    column = jnp.broadcast_to(line, (B, rows)).T
    return jnp.concatenate([column, column], axis=1)


def weight_kernel(core_ref, back_ref, projected_ref, hidden_ref, grads_ref, give_ref, keep_ref, pre):
    @pl.when(pl.program_id(0) == 0)
    def _():
        tail = back_ref[:, 1024:, :].astype(jnp.float32)
        inner = jnp.sum(tail[:, 0:4] + tail[:, 4:8], axis=0)
        for part in range(8):
            at = pl.ds(part * B, B)
            grads = back_ref[0, at, :].astype(jnp.float32)
            for source in range(1, 8):
                grads += back_ref[source, at, :].astype(jnp.float32)
            grads_ref[at, :] = grads
            norm = across(tail[part, 8:9, :B] + tail[part, 8:9, B:], B)
            half = part % 2 * B
            product = across(inner[part // 2 : part // 2 + 1, half : half + B], B)
            unit = projected_ref[at, :].astype(jnp.float32) / norm
            pre[at, :] = ((grads - unit * product) / norm).astype(jnp.bfloat16)

    product = lax.dot_general(
        hidden_ref[...], pre[...], (((0,), (0,)), ((), ())), preferred_element_type=jnp.float32
    )
    core = core_ref[0]
    for k in range(2):
        even = product[2 * k * 224 : (2 * k + 1) * 224].astype(jnp.bfloat16)
        odd = product[(2 * k + 1) * 224 : (2 * k + 2) * 224].astype(jnp.bfloat16)
        mine = core == 0
        keep_ref[k] = jnp.where(mine, even, odd)
        give_ref[k] = jnp.where(mine, odd, even)


def weight_pass(core, back, projected, hidden):
    halves = pl.BlockSpec((2, 224, PAIR), lambda s: (s, 0, 0))
    return pl.pallas_call(
        weight_kernel,
        grid=(4,),
        in_specs=[
            SMEM,
            whole(8, 1040, PAIR),
            whole(1024, PAIR),
            pl.BlockSpec((1024, 896), lambda s: (0, s)),
        ],
        out_specs=[whole(1024, PAIR), halves, halves],
        out_shape=[
            jax.ShapeDtypeStruct((1024, PAIR), jnp.float32),
            jax.ShapeDtypeStruct((8, 224, PAIR), jnp.bfloat16),
            jax.ShapeDtypeStruct((8, 224, PAIR), jnp.bfloat16),
        ],
        scratch_shapes=[pltpu.VMEM((1024, PAIR), jnp.bfloat16)],
        compiler_params=pltpu.CompilerParams(vmem_limit_bytes=60 * 2**20),
        cost_estimate=pl.CostEstimate(flops=2 * 10**9, bytes_accessed=15 * 2**20, transcendentals=0),
        name="weight_terms",
    )(core, back, projected, hidden)


def split_two(values):
    high = values.astype(jnp.bfloat16)
    return high, (values - high.astype(jnp.float32)).astype(jnp.bfloat16)


def shards(hidden, projection, grades, pattern):
    y, zh, core, x, zl = (lax.axis_index(a) for a in AXES)
    col_here = x * 2 + zl

    projected = jnp.dot(hidden, projection, preferred_element_type=jnp.float32).astype(jnp.bfloat16)
    grade_rows = jnp.broadcast_to(jnp.tile(grades.astype(jnp.bfloat16), 2), (4, 2, 16, PAIR))
    pairs = jnp.broadcast_to(projected.reshape(4, 1, PAIR, PAIR), (4, 2, PAIR, PAIR))
    sent = jnp.concatenate([pairs, grade_rows], axis=2).reshape(8, PAIR + 16, PAIR)
    came = lax.all_to_all(sent, COL, 0, 0, tiled=True)

    grade_mine = grades.astype(jnp.float32).reshape(1, B)
    two = jnp.concatenate([grade_mine, shift(grade_mine, "core", 1)], axis=0)
    four = jnp.concatenate([two, shift(two, "zh", 1)], axis=0)
    spread = jnp.stack([four] + [shift(four, "y", -d) for d in (1, 2, 3)]).reshape(4, 2, 2, 1, B)
    right_grade = jnp.stack(
        [
            jnp.concatenate([spread[d, z, c] for d, c in RIGHT[2 * q : 2 * q + 2] for z in (0, 1)], axis=1)
            for q in range(4)
        ]
    )
    both = (pattern + pattern.T).astype(jnp.float32)
    row_here = ((y * 2 + zh) * 2 + core) * 8
    left_ids = jnp.stack([row_here + (x + d) % 4 * 2 + k for d in LEFT for k in (0, 1)])
    right_ids = jnp.stack(
        [((((y + d) % 4) * 2 + (zh ^ z)) * 2 + (core ^ c)) * 8 + col_here for d, c in RIGHT for z in (0, 1)]
    )
    left_pick = (left_ids[:, None] == jnp.arange(128)[None]).astype(jnp.float32)
    right_pick = (jnp.arange(128)[:, None] == right_ids[None]).astype(jnp.float32)
    tiles = jnp.dot(
        jnp.dot(left_pick, both, preferred_element_type=jnp.float32), right_pick, preferred_element_type=jnp.float32
    ).reshape(4, 2, 4, 4)
    active = (tiles.sum(axis=(1, 3)) > 0).astype(jnp.int32)
    weight = jnp.repeat((tiles * (-smoothing_divisor / B)).transpose(2, 0, 1, 3), B, axis=3)
    place = jnp.stack([(x + d) % 4 for d in LEFT]).astype(jnp.int32)
    came, right_grade, active, weight, place = lax.optimization_barrier((came, right_grade, active, weight, place))

    halves = [
        jnp.concatenate([came[k, h * B : (h + 1) * B] for k in range(8)], axis=1).astype(jnp.float32) for h in (0, 1)
    ]
    norms = [jnp.sqrt(jnp.sum(rows * rows, axis=1) + epsilon) for rows in halves]
    units = [(rows / norm[:, None]).astype(jnp.bfloat16) for rows, norm in zip(halves, norms)]
    unit = jnp.where(zl == 0, units[0], units[1])
    own_norm = jnp.where(zl == 0, norms[0], norms[1])
    scaled = [u * jnp.bfloat16(smoothing_divisor) for u in units]
    turned0, turned1 = [jnp.concatenate([-u[:, 1024:], u[:, :1024]], axis=1) for u in scaled]

    left_grade = came[:, PAIR, :B].astype(jnp.float32).reshape(4, PAIR)
    twice = jnp.concatenate([left_grade, left_grade], axis=0)
    turned_grade = lax.dynamic_slice_in_dim(twice, x, 4, 0)
    left_grade = jnp.stack([turned_grade[d] for d in LEFT])[:, :, None]
    norm_high, norm_low = split_two(own_norm)
    extra = jnp.concatenate([norm_high, norm_low]).astype(jnp.float32)
    extra = jnp.broadcast_to(extra[None], (8, PAIR))

    below0 = shift(turned0, "x", 1)
    above1 = shift(turned1, "x", -1)
    y_below = shift(unit, "y", 1)
    y_above = shift(unit, "y", -1)
    unit_z = shift(unit, "zh", 1)
    below0, above1, y_below, y_above, unit_z, turned0, turned1, unit, left_grade, extra = lax.optimization_barrier(
        (below0, above1, y_below, y_above, unit_z, turned0, turned1, unit, left_grade, extra)
    )
    below1 = shift(turned1, "x", 1)
    above0 = shift(turned0, "x", -1)
    z_below = shift(unit_z, "y", 1)
    z_above = shift(unit_z, "y", -1)
    other = shift(jnp.concatenate([unit, unit_z], axis=0), "core", 1)
    below0, above1, y_below, z_above, below1, above0, z_below, y_above, other = lax.optimization_barrier(
        (below0, above1, y_below, z_above, below1, above0, z_below, y_above, other)
    )
    ring = (y_above, z_above, y_below, z_below)
    other_ring = shift(jnp.concatenate(ring, axis=0), "core", 1)
    far0 = shift(below0, "x", 1)
    far1 = shift(above1, "x", -1)
    y_far = shift(y_below, "y", 1)
    z_far = shift(z_above, "y", -1)

    lefts = [(turned0, turned1), (above0, above1), (below0, below1)]
    rights = [(unit, unit_z, other), ring, (other_ring,)]
    near_acc, near_inner = near_pass(active, weight, left_grade, right_grade, lefts, rights)
    y_far, z_far, far0, far1, near_acc, near_inner = lax.optimization_barrier(
        (y_far, z_far, far0, far1, near_acc, near_inner)
    )
    lefts = lefts + [(far0, far1)]
    rights = rights + [(y_far, z_far, shift(y_far, "core", 1), shift(z_far, "core", 1))]
    sums = far_pass(place, active, weight, left_grade, right_grade, extra, near_inner, near_acc, lefts, rights)
    back = lax.all_to_all(sums, COL, 0, 0, tiled=True)

    grads, give, keep = weight_pass(core.astype(jnp.int32).reshape(1), back, projected, hidden)
    chip = (keep.astype(jnp.float32) + shift(give, "core", 1).astype(jnp.float32)).astype(jnp.bfloat16)
    gathered = lax.all_to_all(chip, ("y", "zh"), 0, 0, tiled=True)
    weight_grad = jnp.sum(gathered.astype(jnp.float32), axis=0)
    return grads, weight_grad


def solution(mesh):
    fine = Mesh(np.asarray(mesh.devices).reshape(SIZES), AXES)
    return jax.shard_map(
        shards,
        mesh=fine,
        in_specs=(P(ROW, None), P(None, COL), P(ROW + COL), P()),
        out_specs=(P(ROW, COL), P(ROW, COL)),
        check_vma=False,
    )
```

```python
import functools

import jax
import jax.numpy as jnp
import numpy as np
from jax import lax
from jax.experimental import pallas as pl
from jax.experimental.pallas import tpu as pltpu
from jax.sharding import Mesh, PartitionSpec as P

smoothing_divisor = 64.0
epsilon = 1e-06
AXES = ("y", "zh", "core", "x", "zl")
SIZES = (4, 2, 2, 4, 2)
ROW = ("y", "zh", "core")
COL = ("x", "zl")
B = 128
PAIR = 2 * B
QUAD = 4 * B
WIDTH = 2048
ANY = pl.BlockSpec(memory_space=pltpu.HBM)
SMEM = pl.BlockSpec(memory_space=pltpu.SMEM)

LEFT = (0, 1, 3, 2)
RIGHT = [(0, z, c) for c in (0, 1) for z in (0, 1)]
RIGHT += [(d, z, c) for z in (0, 1) for c in (0, 1) for d in (1, 3)]
RIGHT += [(2, z, c) for c in (0, 1) for z in (0, 1)]


def shift(value, axis, by):
    size = SIZES[AXES.index(axis)]
    return lax.ppermute(value, axis, [(i, (i + by) % size) for i in range(size)])


def whole(*shape):
    return pl.BlockSpec(shape, lambda *_: (0,) * len(shape))


def fetch(pieces, buffer, sem):
    row = 0
    for ref in pieces:
        pltpu.make_async_copy(ref, buffer.at[pl.ds(row, ref.shape[0])], sem).start()
        row += ref.shape[0]


def filled(buffer, sem):
    pltpu.make_async_copy(buffer, buffer, sem).wait()


def tile(slot, quad, left_buf, right_buf, weight_ref, left_grade_ref, right_grade_ref, acc, inner):
    right = right_buf[quad]
    scores = lax.dot_general(left_buf[slot], right, (((1,), (1,)), ((), ())), preferred_element_type=jnp.float32)
    label = jnp.clip(left_grade_ref[slot] - right_grade_ref[quad], -1.0, 1.0)
    weight = weight_ref[quad, slot]
    weight = jnp.concatenate(
        [jnp.broadcast_to(weight[0:1], (B, QUAD)), jnp.broadcast_to(weight[1:2], (B, QUAD))], axis=0
    )
    grown = jnp.exp(label * scores)
    slopes = (label * weight * pltpu.reciprocal(1.0 + grown, approx=True)).astype(jnp.bfloat16)
    terms = slopes.astype(jnp.float32) * scores
    inner[slot] += (terms[:, :B] + terms[:, B:PAIR]) + (terms[:, PAIR : 3 * B] + terms[:, 3 * B :])
    acc[slot] += jnp.dot(slopes, right, preferred_element_type=jnp.float32)


def near_kernel(active_ref, weight_ref, left_grade_ref, right_grade_ref, *refs):
    lefts = (refs[0:1], refs[1:2], refs[2:3])
    rights = (refs[3:6], refs[6:9], refs[9:12])
    acc_out, inner, acc, left_buf, right_buf, left_sem, right_sem, acc_sem = refs[12:]
    fetch(rights[0], right_buf.at[0], right_sem.at[0])
    for k in range(3):
        fetch(lefts[k], left_buf.at[k], left_sem.at[k])
    acc[...] = jnp.zeros_like(acc)
    inner[...] = jnp.zeros_like(inner)

    def one(quad, carry):
        filled(right_buf.at[quad], right_sem.at[quad])
        for slot in range(3):

            @pl.when(quad == 0)
            def _(slot=slot):
                filled(left_buf.at[slot], left_sem.at[slot])
                if slot < 2:
                    fetch(rights[slot + 1], right_buf.at[slot + 1], right_sem.at[slot + 1])

            @pl.when(active_ref[slot, quad] > 0)
            def _(slot=slot):
                tile(slot, quad, left_buf, right_buf, weight_ref, left_grade_ref, right_grade_ref, acc, inner)

            @pl.when(quad == 2)
            def _(slot=slot):
                pltpu.make_async_copy(acc.at[slot], acc_out.at[slot], acc_sem.at[slot]).start()

        return carry

    lax.fori_loop(0, 3, one, 0)
    for slot in range(3):
        pltpu.make_async_copy(acc.at[slot], acc_out.at[slot], acc_sem.at[slot]).wait()


def far_kernel(place_ref, active_ref, weight_ref, left_grade_ref, right_grade_ref, extra_ref, near_inner, near_acc, *refs):
    lefts = (refs[0:1], refs[1:2], refs[2:3], refs[3:5])
    rights = (refs[5:8], refs[8:11], refs[11:14], refs[14:18])
    out_ref, acc, inner, lines, sent, tail, left_buf, right_buf, left_sem, right_sem, acc_sem, sent_sem, tail_sem = refs[18:]
    acc_in = lambda k: pltpu.make_async_copy(near_acc.at[k], acc.at[k], acc_sem.at[k])
    fetch(rights[3], right_buf.at[3], right_sem.at[3])
    for k in range(2):
        fetch(lefts[k], left_buf.at[k], left_sem.at[k])
        acc_in(k).start()
    inner[:3] = near_inner[...]
    inner[3] = jnp.zeros((PAIR, B), jnp.float32)
    acc[3] = jnp.zeros((PAIR, WIDTH), jnp.float32)

    def run(slot, quad):
        @pl.when(active_ref[slot, quad] > 0)
        def _():
            tile(slot, quad, left_buf, right_buf, weight_ref, left_grade_ref, right_grade_ref, acc, inner)

    def home(slot):
        at = pl.ds(pl.multiple_of(place_ref[slot] * PAIR, PAIR), PAIR)
        return pltpu.make_async_copy(sent.at[slot], out_ref.at[:, at, :], sent_sem.at[slot])

    def finish(slot):
        for chunk in range(8):
            source = (chunk + 4) % 8
            values = acc[slot, :, source * PAIR : (source + 1) * PAIR]
            sent[slot, chunk] = (values if chunk < 4 else -values).astype(jnp.bfloat16)
        home(slot).start()
        lines[place_ref[slot]] = jnp.sum(inner[slot].T, axis=0, keepdims=True) * (1.0 / smoothing_divisor)

    filled(right_buf.at[3], right_sem.at[3])
    for slot in range(3):
        filled(left_buf.at[slot], left_sem.at[slot])
        acc_in(slot).wait()
        if slot == 0:
            fetch(lefts[2], left_buf.at[2], left_sem.at[2])
            acc_in(2).start()
            fetch(lefts[3], left_buf.at[3], left_sem.at[3])
            fetch(rights[0], right_buf.at[0], right_sem.at[0])
        if slot == 1:
            fetch(rights[1], right_buf.at[1], right_sem.at[1])
            fetch(rights[2], right_buf.at[2], right_sem.at[2])
        run(slot, 3)
        finish(slot)
    filled(left_buf.at[3], left_sem.at[3])

    def one(quad, carry):
        @pl.when(quad < 3)
        def _():
            filled(right_buf.at[quad], right_sem.at[quad])

        run(3, quad)
        return carry

    lax.fori_loop(0, 4, one, 0)
    finish(3)
    total = jnp.concatenate([lines[k] for k in range(4)], axis=0)
    high = total.astype(jnp.bfloat16).astype(jnp.float32)
    last = jnp.concatenate([high, total - high, extra_ref[...]], axis=0).astype(jnp.bfloat16)
    for chunk in range(8):
        tail[chunk] = last
    tail_copy = pltpu.make_async_copy(tail, out_ref.at[:, pl.ds(1024, 16), :], tail_sem)
    tail_copy.start()
    for slot in range(4):
        home(slot).wait()
    tail_copy.wait()


def near_pass(active, weight, left_grade, right_grade, lefts, rights):
    arrays = [a for group in (lefts, rights) for pieces in group for a in pieces]
    return pl.pallas_call(
        near_kernel,
        in_specs=[SMEM, whole(*weight.shape), whole(*left_grade.shape), whole(*right_grade.shape)] + [ANY] * len(arrays),
        out_specs=[ANY, whole(3, PAIR, B)],
        out_shape=[
            jax.ShapeDtypeStruct((3, PAIR, WIDTH), jnp.float32),
            jax.ShapeDtypeStruct((3, PAIR, B), jnp.float32),
        ],
        scratch_shapes=[
            pltpu.VMEM((3, PAIR, WIDTH), jnp.float32),
            pltpu.VMEM((3, PAIR, WIDTH), jnp.bfloat16),
            pltpu.VMEM((3, QUAD, WIDTH), jnp.bfloat16),
            pltpu.SemaphoreType.DMA((3,)),
            pltpu.SemaphoreType.DMA((3,)),
            pltpu.SemaphoreType.DMA((3,)),
        ],
        compiler_params=pltpu.CompilerParams(vmem_limit_bytes=60 * 2**20),
        cost_estimate=pl.CostEstimate(flops=9 * 10**9, bytes_accessed=16 * 2**20, transcendentals=2**21),
        name="near_tiles",
    )(active, weight, left_grade, right_grade, *arrays)


def far_pass(place, active, weight, left_grade, right_grade, extra, near_inner, near_acc, lefts, rights):
    arrays = [a for group in (lefts, rights) for pieces in group for a in pieces]
    return pl.pallas_call(
        far_kernel,
        in_specs=[SMEM, SMEM, whole(*weight.shape), whole(*left_grade.shape), whole(*right_grade.shape)]
        + [whole(*extra.shape), whole(*near_inner.shape), ANY]
        + [ANY] * len(arrays),
        out_specs=ANY,
        out_shape=jax.ShapeDtypeStruct((8, 1040, PAIR), jnp.bfloat16),
        scratch_shapes=[
            pltpu.VMEM((4, PAIR, WIDTH), jnp.float32),
            pltpu.VMEM((4, PAIR, B), jnp.float32),
            pltpu.VMEM((4, 1, PAIR), jnp.float32),
            pltpu.VMEM((4, 8, PAIR, PAIR), jnp.bfloat16),
            pltpu.VMEM((8, 16, PAIR), jnp.bfloat16),
            pltpu.VMEM((4, PAIR, WIDTH), jnp.bfloat16),
            pltpu.VMEM((4, QUAD, WIDTH), jnp.bfloat16),
            pltpu.SemaphoreType.DMA((4,)),
            pltpu.SemaphoreType.DMA((4,)),
            pltpu.SemaphoreType.DMA((3,)),
            pltpu.SemaphoreType.DMA((4,)),
            pltpu.SemaphoreType.DMA,
        ],
        compiler_params=pltpu.CompilerParams(vmem_limit_bytes=60 * 2**20),
        cost_estimate=pl.CostEstimate(flops=8 * 10**9, bytes_accessed=24 * 2**20, transcendentals=2**21),
        name="far_tiles",
    )(place, active, weight, left_grade, right_grade, extra, near_inner, near_acc, *arrays)


def across(line, rows):
    column = jnp.broadcast_to(line, (B, rows)).T
    return jnp.concatenate([column, column], axis=1)


def weight_kernel(core_ref, projected_ref, back_ref, hidden_ref, grads_out, give_out, keep_out, *scratch):
    tail, parts, cols, grads, give, keep, pre, tail_sem, part_sem, col_sem, out_sem = scratch
    tail_in = pltpu.make_async_copy(back_ref.at[:, pl.ds(1024, 16), :], tail, tail_sem)
    part_in = [
        pltpu.make_async_copy(back_ref.at[:, pl.ds(k * B, B), :], parts.at[k], part_sem.at[k]) for k in range(8)
    ]
    cols_in = [
        pltpu.make_async_copy(hidden_ref.at[:, pl.ds(k * 896, 896)], cols.at[k], col_sem.at[k]) for k in range(4)
    ]
    tail_in.start()
    for k in range(8):
        part_in[k].start()
    tail_in.wait()
    ends = tail[...].astype(jnp.float32)
    inner = jnp.sum(ends[:, 0:4] + ends[:, 4:8], axis=0)
    for k in range(8):
        part_in[k].wait()
        if k < 4:
            cols_in[k].start()
        at = pl.ds(k * B, B)
        total = parts[k, 0].astype(jnp.float32)
        for source in range(1, 8):
            total += parts[k, source].astype(jnp.float32)
        grads[at, :] = total
        norm = across(ends[k, 8:9, :B] + ends[k, 8:9, B:], B)
        half = k % 2 * B
        product = across(inner[k // 2 : k // 2 + 1, half : half + B], B)
        unit = projected_ref[at, :].astype(jnp.float32) / norm
        pre[at, :] = ((total - unit * product) / norm).astype(jnp.bfloat16)
    grads_copy = pltpu.make_async_copy(grads, grads_out, out_sem.at[0])
    grads_copy.start()
    mine = core_ref[0] == 0
    copies = [grads_copy]
    for k in range(4):
        cols_in[k].wait()
        product = lax.dot_general(cols[k], pre[...], (((0,), (0,)), ((), ())), preferred_element_type=jnp.float32)
        for j in range(2):
            even = product[2 * j * 224 : (2 * j + 1) * 224].astype(jnp.bfloat16)
            odd = product[(2 * j + 1) * 224 : (2 * j + 2) * 224].astype(jnp.bfloat16)
            keep[2 * k + j] = jnp.where(mine, even, odd)
            give[2 * k + j] = jnp.where(mine, odd, even)
        two = pl.ds(2 * k, 2)
        copies.append(pltpu.make_async_copy(give.at[two], give_out.at[two], out_sem.at[1 + 2 * k]))
        copies.append(pltpu.make_async_copy(keep.at[two], keep_out.at[two], out_sem.at[2 + 2 * k]))
        copies[-2].start()
        copies[-1].start()
    for copy in copies:
        copy.wait()


def weight_pass(core, back, projected, hidden):
    chip = jax.ShapeDtypeStruct((8, 224, PAIR), jnp.bfloat16)
    return pl.pallas_call(
        weight_kernel,
        in_specs=[SMEM, whole(1024, PAIR), ANY, ANY],
        out_specs=[ANY, ANY, ANY],
        out_shape=[jax.ShapeDtypeStruct((1024, PAIR), jnp.float32), chip, chip],
        scratch_shapes=[
            pltpu.VMEM((8, 16, PAIR), jnp.bfloat16),
            pltpu.VMEM((8, 8, B, PAIR), jnp.bfloat16),
            pltpu.VMEM((4, 1024, 896), jnp.bfloat16),
            pltpu.VMEM((1024, PAIR), jnp.float32),
            pltpu.VMEM((8, 224, PAIR), jnp.bfloat16),
            pltpu.VMEM((8, 224, PAIR), jnp.bfloat16),
            pltpu.VMEM((1024, PAIR), jnp.bfloat16),
            pltpu.SemaphoreType.DMA,
            pltpu.SemaphoreType.DMA((8,)),
            pltpu.SemaphoreType.DMA((4,)),
            pltpu.SemaphoreType.DMA((9,)),
        ],
        compiler_params=pltpu.CompilerParams(vmem_limit_bytes=60 * 2**20),
        cost_estimate=pl.CostEstimate(flops=2 * 10**9, bytes_accessed=15 * 2**20, transcendentals=0),
        name="weight_terms",
    )(core, projected, back, hidden)


def split_two(values):
    high = values.astype(jnp.bfloat16)
    return high, (values - high.astype(jnp.float32)).astype(jnp.bfloat16)


def shards(hidden, projection, grades, pattern):
    y, zh, core, x, zl = (lax.axis_index(a) for a in AXES)
    col_here = x * 2 + zl

    grade_mine = grades.astype(jnp.float32).reshape(1, B)
    two = jnp.concatenate([grade_mine, shift(grade_mine, "core", 1)], axis=0)
    hidden, two = lax.optimization_barrier((hidden, two))
    four = jnp.concatenate([two, shift(two, "zh", 1)], axis=0)
    projected = jnp.dot(hidden, projection, preferred_element_type=jnp.float32).astype(jnp.bfloat16)
    projected, four = lax.optimization_barrier((projected, four))
    grade_rows = jnp.broadcast_to(jnp.tile(grades.astype(jnp.bfloat16), 2), (4, 2, 16, PAIR))
    pairs = jnp.broadcast_to(projected.reshape(4, 1, PAIR, PAIR), (4, 2, PAIR, PAIR))
    sent = jnp.concatenate([pairs, grade_rows], axis=2).reshape(8, PAIR + 16, PAIR)
    came = lax.all_to_all(sent, COL, 0, 0, tiled=True)

    spread = jnp.stack([four] + [shift(four, "y", -d) for d in (1, 2, 3)]).reshape(4, 2, 2, 1, B)
    right_grade = jnp.stack(
        [
            jnp.concatenate([spread[place] for place in RIGHT[4 * q : 4 * q + 4]], axis=1)
            for q in range(4)
        ]
    )
    both = (pattern + pattern.T).astype(jnp.float32)
    row_here = ((y * 2 + zh) * 2 + core) * 8
    left_ids = jnp.stack([row_here + (x + d) % 4 * 2 + k for d in LEFT for k in (0, 1)])
    right_ids = jnp.stack(
        [((((y + d) % 4) * 2 + (zh ^ z)) * 2 + (core ^ c)) * 8 + col_here for d, z, c in RIGHT]
    )
    left_pick = (left_ids[:, None] == jnp.arange(128)[None]).astype(jnp.float32)
    right_pick = (jnp.arange(128)[:, None] == right_ids[None]).astype(jnp.float32)
    tiles = jnp.dot(
        jnp.dot(left_pick, both, preferred_element_type=jnp.float32), right_pick, preferred_element_type=jnp.float32
    ).reshape(4, 2, 4, 4)
    active = (tiles.sum(axis=(1, 3)) > 0).astype(jnp.int32)
    weight = jnp.repeat((tiles * (-smoothing_divisor / B)).transpose(2, 0, 1, 3), B, axis=3)
    place = jnp.stack([(x + d) % 4 for d in LEFT]).astype(jnp.int32)
    came, right_grade, active, weight, place = lax.optimization_barrier((came, right_grade, active, weight, place))

    rows = jnp.concatenate([came[k, :PAIR] for k in range(8)], axis=1).astype(jnp.float32)
    norms = jnp.sqrt(jnp.sum(rows * rows, axis=1) + epsilon)
    units = (rows / norms[:, None]).astype(jnp.bfloat16)
    unit = jnp.where(zl == 0, units[:B], units[B:])
    own_norm = jnp.where(zl == 0, norms[:B], norms[B:])
    scaled = units * jnp.bfloat16(smoothing_divisor)
    turned = jnp.concatenate([-scaled[:, 1024:], scaled[:, :1024]], axis=1)

    left_grade = came[:, PAIR, :B].astype(jnp.float32).reshape(4, PAIR)
    twice = jnp.concatenate([left_grade, left_grade], axis=0)
    turned_grade = lax.dynamic_slice_in_dim(twice, x, 4, 0)
    left_grade = jnp.stack([turned_grade[d] for d in LEFT])[:, :, None]
    norm_high, norm_low = split_two(own_norm)
    extra = jnp.concatenate([norm_high, norm_low]).astype(jnp.float32)
    extra = jnp.broadcast_to(extra[None], (8, PAIR))

    below = shift(turned, "x", 1)
    above = shift(turned, "x", -1)
    y_below = shift(unit, "y", 1)
    y_above = shift(unit, "y", -1)
    unit_z = shift(unit, "zh", 1)
    y_below, y_above, unit_z, unit, left_grade, extra = lax.optimization_barrier(
        (y_below, y_above, unit_z, unit, left_grade, extra)
    )
    z_below = shift(unit_z, "y", 1)
    z_above = shift(unit_z, "y", -1)
    other = shift(jnp.concatenate([unit, unit_z], axis=0), "core", 1)
    y_both = jnp.concatenate([y_above, y_below], axis=0)
    below, above, y_below, z_above, z_below, y_above, other, y_both = lax.optimization_barrier(
        (below, above, y_below, z_above, z_below, y_above, other, y_both)
    )
    y_other = shift(y_both, "core", 1)
    z_other = shift(jnp.concatenate([z_above, z_below], axis=0), "core", 1)
    far0 = shift(below[:B], "x", 1)
    far1 = shift(above[B:], "x", -1)
    y_far = shift(y_below, "y", 1)
    z_far = shift(z_above, "y", -1)

    lefts = [(turned,), (above,), (below,)]
    rights = [(unit, unit_z, other), (y_above, y_below, y_other), (z_above, z_below, z_other)]
    near_acc, near_inner = near_pass(active, weight, left_grade, right_grade, lefts, rights)
    y_far, z_far, far0, far1, near_acc, near_inner = lax.optimization_barrier(
        (y_far, z_far, far0, far1, near_acc, near_inner)
    )
    lefts = lefts + [(far0, far1)]
    rights = rights + [(y_far, z_far, shift(y_far, "core", 1), shift(z_far, "core", 1))]
    sums = far_pass(place, active, weight, left_grade, right_grade, extra, near_inner, near_acc, lefts, rights)
    back = lax.all_to_all(sums, COL, 0, 0, tiled=True)

    grads, give, keep = weight_pass(core.astype(jnp.int32).reshape(1), back, projected, hidden)
    chip = (keep.astype(jnp.float32) + shift(give, "core", 1).astype(jnp.float32)).astype(jnp.bfloat16)
    gathered = lax.all_to_all(chip, ("y", "zh"), 0, 0, tiled=True)
    weight_grad = jnp.sum(gathered.astype(jnp.float32), axis=0)
    return grads, weight_grad


def solution(mesh):
    fine = Mesh(np.asarray(mesh.devices).reshape(SIZES), AXES)
    return jax.shard_map(
        shards,
        mesh=fine,
        in_specs=(P(ROW, None), P(None, COL), P(ROW + COL), P()),
        out_specs=(P(ROW, COL), P(ROW, COL)),
        check_vma=False,
    )
```

```python
import functools

import jax
import jax.numpy as jnp
import numpy as np
from jax import lax
from jax.experimental import pallas as pl
from jax.experimental.pallas import tpu as pltpu
from jax.sharding import Mesh, PartitionSpec as P

smoothing_divisor = 64.0
epsilon = 1e-06
AXES = ("y", "zh", "core", "x", "zl")
SIZES = (4, 2, 2, 4, 2)
ROW = ("y", "zh", "core")
COL = ("x", "zl")
B = 128
PAIR = 2 * B
QUAD = 4 * B
LONG = B + 16
WIDTH = 2048
ANY = pl.BlockSpec(memory_space=pltpu.HBM)
SMEM = pl.BlockSpec(memory_space=pltpu.SMEM)

LEFT = (0, 1, 3, 2)
RIGHT = [(0, z, c) for c in (0, 1) for z in (0, 1)]
RIGHT += [(d, z, c) for z in (0, 1) for c in (0, 1) for d in (1, 3)]
RIGHT += [(2, z, c) for c in (0, 1) for z in (0, 1)]


def shift(value, axis, by):
    size = SIZES[AXES.index(axis)]
    return lax.ppermute(value, axis, [(i, (i + by) % size) for i in range(size)])


def whole(*shape):
    return pl.BlockSpec(shape, lambda *_: (0,) * len(shape))


def fetch(pieces, buffer, sem):
    row = 0
    for ref in pieces:
        rows = ref.shape[0]
        blocks = [(k, B) for k in range(0, rows, LONG)] if rows % LONG == 0 else [(0, rows)]
        for first, rows in blocks:
            pltpu.make_async_copy(ref.at[pl.ds(first, rows)], buffer.at[pl.ds(row, rows)], sem).start()
            row += rows


def filled(buffer, sem):
    pltpu.make_async_copy(buffer, buffer, sem).wait()


def columns(left_grade_ref, grade_cols, slots):
    for slot in slots:
        grade_cols[slot] = jnp.broadcast_to(left_grade_ref[slot], (B, PAIR)).T


def tile(slot, quad, left_buf, right_buf, weight_ref, grade_cols, right_grade_ref, acc, inner, scores, slopes):
    right = right_buf[quad]
    scores[...] = lax.dot_general(
        left_buf[slot], right, (((1,), (1,)), ((), ())), preferred_element_type=jnp.float32
    )
    for part in range(4):
        rows = slice(part * 64, part * 64 + 64)
        here = grade_cols[slot, rows, :]
        total = jnp.zeros((64, B), jnp.float32)
        for lane in range(4):
            lanes = slice(lane * B, lane * B + B)
            score = scores[rows, lanes]
            label = jnp.clip(here - right_grade_ref[quad, :, lanes], -1.0, 1.0)
            step = label * weight_ref[quad, slot, part // 2 : part // 2 + 1, lanes]
            grown = jnp.exp(label * score)
            slope = (step * pltpu.reciprocal(1.0 + grown, approx=True)).astype(jnp.bfloat16)
            slopes[rows, lanes] = slope
            total += slope.astype(jnp.float32) * score
        inner[slot, rows, :] += total
    acc[slot] += jnp.dot(slopes[...], right, preferred_element_type=jnp.float32)


def near_kernel(active_ref, weight_ref, left_grade_ref, right_grade_ref, *refs):
    lefts = (refs[0:1], refs[1:2], refs[2:3])
    rights = (refs[3:6], refs[6:9], refs[9:12])
    acc_out, inner, acc, left_buf, right_buf, grade_cols, scores, slopes, left_sem, right_sem, acc_sem = refs[12:]
    fetch(rights[0], right_buf.at[0], right_sem.at[0])
    for k in range(3):
        fetch(lefts[k], left_buf.at[k], left_sem.at[k])
    acc[...] = jnp.zeros_like(acc)
    inner[...] = jnp.zeros_like(inner)
    columns(left_grade_ref, grade_cols, range(3))

    def one(quad, carry):
        filled(right_buf.at[quad], right_sem.at[quad])
        for slot in range(3):

            @pl.when(quad == 0)
            def _(slot=slot):
                filled(left_buf.at[slot], left_sem.at[slot])
                if slot < 2:
                    fetch(rights[slot + 1], right_buf.at[slot + 1], right_sem.at[slot + 1])

            @pl.when(active_ref[slot, quad] > 0)
            def _(slot=slot):
                tile(slot, quad, left_buf, right_buf, weight_ref, grade_cols, right_grade_ref, acc, inner, scores, slopes)

            @pl.when(quad == 2)
            def _(slot=slot):
                pltpu.make_async_copy(acc.at[slot], acc_out.at[slot], acc_sem.at[slot]).start()

        return carry

    lax.fori_loop(0, 3, one, 0)
    for slot in range(3):
        pltpu.make_async_copy(acc.at[slot], acc_out.at[slot], acc_sem.at[slot]).wait()


def far_kernel(
    place_ref, active_ref, weight_ref, left_grade_ref, near_grade_ref, far_grade_ref, extra_ref, near_inner, near_acc, *refs
):
    lefts = (refs[0:1], refs[1:2], refs[2:3], refs[3:5])
    rights = (refs[5:8], refs[8:11], refs[11:14], refs[14:18])
    out_ref, acc, inner, lines, sent, tail, left_buf, right_buf = refs[18:26]
    grade_cols, right_grade_ref, scores, slopes, left_sem, right_sem, acc_sem, sent_sem, tail_sem = refs[26:]
    acc_in = lambda k: pltpu.make_async_copy(near_acc.at[k], acc.at[k], acc_sem.at[k])
    fetch(rights[3], right_buf.at[3], right_sem.at[3])
    for k in range(2):
        fetch(lefts[k], left_buf.at[k], left_sem.at[k])
        acc_in(k).start()
    columns(left_grade_ref, grade_cols, range(4))
    right_grade_ref[:3] = near_grade_ref[...]
    right_grade_ref[3:] = far_grade_ref[...]
    inner[:3] = near_inner[...]
    inner[3] = jnp.zeros((PAIR, B), jnp.float32)
    acc[3] = jnp.zeros((PAIR, WIDTH), jnp.float32)

    def run(slot, quad):
        @pl.when(active_ref[slot, quad] > 0)
        def _():
            tile(slot, quad, left_buf, right_buf, weight_ref, grade_cols, right_grade_ref, acc, inner, scores, slopes)

    def home(slot):
        at = pl.ds(pl.multiple_of(place_ref[slot] * PAIR, PAIR), PAIR)
        return pltpu.make_async_copy(sent.at[slot], out_ref.at[:, at, :], sent_sem.at[slot])

    def finish(slot):
        for chunk in range(8):
            source = (chunk + 4) % 8
            values = acc[slot, :, source * PAIR : (source + 1) * PAIR]
            sent[slot, chunk] = (values if chunk < 4 else -values).astype(jnp.bfloat16)
        home(slot).start()
        lines[place_ref[slot]] = jnp.sum(inner[slot].T, axis=0, keepdims=True) * (1.0 / smoothing_divisor)

    filled(right_buf.at[3], right_sem.at[3])
    for slot in range(3):
        filled(left_buf.at[slot], left_sem.at[slot])
        acc_in(slot).wait()
        if slot == 0:
            fetch(lefts[2], left_buf.at[2], left_sem.at[2])
            acc_in(2).start()
            fetch(lefts[3], left_buf.at[3], left_sem.at[3])
            fetch(rights[0], right_buf.at[0], right_sem.at[0])
        if slot == 1:
            fetch(rights[1], right_buf.at[1], right_sem.at[1])
            fetch(rights[2], right_buf.at[2], right_sem.at[2])
        run(slot, 3)
        finish(slot)
    filled(left_buf.at[3], left_sem.at[3])

    def one(quad, carry):
        @pl.when(quad < 3)
        def _():
            filled(right_buf.at[quad], right_sem.at[quad])

        run(3, quad)
        return carry

    lax.fori_loop(0, 4, one, 0)
    finish(3)
    total = jnp.concatenate([lines[k] for k in range(4)], axis=0)
    high = total.astype(jnp.bfloat16).astype(jnp.float32)
    last = jnp.concatenate([high, total - high, extra_ref[...]], axis=0).astype(jnp.bfloat16)
    for chunk in range(8):
        tail[chunk] = last
    tail_copy = pltpu.make_async_copy(tail, out_ref.at[:, pl.ds(1024, 16), :], tail_sem)
    tail_copy.start()
    for slot in range(4):
        home(slot).wait()
    tail_copy.wait()


def near_pass(active, weight, left_grade, right_grade, lefts, rights):
    arrays = [a for group in (lefts, rights) for pieces in group for a in pieces]
    return pl.pallas_call(
        near_kernel,
        in_specs=[SMEM, whole(*weight.shape), whole(*left_grade.shape), whole(*right_grade.shape)] + [ANY] * len(arrays),
        out_specs=[ANY, whole(3, PAIR, B)],
        out_shape=[
            jax.ShapeDtypeStruct((3, PAIR, WIDTH), jnp.float32),
            jax.ShapeDtypeStruct((3, PAIR, B), jnp.float32),
        ],
        scratch_shapes=[
            pltpu.VMEM((3, PAIR, WIDTH), jnp.float32),
            pltpu.VMEM((3, PAIR, WIDTH), jnp.bfloat16),
            pltpu.VMEM((3, QUAD, WIDTH), jnp.bfloat16),
            pltpu.VMEM((3, PAIR, B), jnp.float32),
            pltpu.VMEM((PAIR, QUAD), jnp.float32),
            pltpu.VMEM((PAIR, QUAD), jnp.bfloat16),
            pltpu.SemaphoreType.DMA((3,)),
            pltpu.SemaphoreType.DMA((3,)),
            pltpu.SemaphoreType.DMA((3,)),
        ],
        compiler_params=pltpu.CompilerParams(vmem_limit_bytes=60 * 2**20),
        cost_estimate=pl.CostEstimate(flops=9 * 10**9, bytes_accessed=16 * 2**20, transcendentals=2**21),
        name="near_tiles",
    )(active, weight, left_grade, right_grade, *arrays)


def far_pass(place, active, weight, left_grade, near_grade, far_grade, extra, near_inner, near_acc, lefts, rights):
    arrays = [a for group in (lefts, rights) for pieces in group for a in pieces]
    return pl.pallas_call(
        far_kernel,
        in_specs=[SMEM, SMEM]
        + [whole(*a.shape) for a in (weight, left_grade, near_grade, far_grade, extra, near_inner)]
        + [ANY]
        + [ANY] * len(arrays),
        out_specs=ANY,
        out_shape=jax.ShapeDtypeStruct((8, 1040, PAIR), jnp.bfloat16),
        scratch_shapes=[
            pltpu.VMEM((4, PAIR, WIDTH), jnp.float32),
            pltpu.VMEM((4, PAIR, B), jnp.float32),
            pltpu.VMEM((4, 1, PAIR), jnp.float32),
            pltpu.VMEM((4, 8, PAIR, PAIR), jnp.bfloat16),
            pltpu.VMEM((8, 16, PAIR), jnp.bfloat16),
            pltpu.VMEM((4, PAIR, WIDTH), jnp.bfloat16),
            pltpu.VMEM((4, QUAD, WIDTH), jnp.bfloat16),
            pltpu.VMEM((4, PAIR, B), jnp.float32),
            pltpu.VMEM((4, 1, QUAD), jnp.float32),
            pltpu.VMEM((PAIR, QUAD), jnp.float32),
            pltpu.VMEM((PAIR, QUAD), jnp.bfloat16),
            pltpu.SemaphoreType.DMA((4,)),
            pltpu.SemaphoreType.DMA((4,)),
            pltpu.SemaphoreType.DMA((3,)),
            pltpu.SemaphoreType.DMA((4,)),
            pltpu.SemaphoreType.DMA,
        ],
        compiler_params=pltpu.CompilerParams(vmem_limit_bytes=60 * 2**20),
        cost_estimate=pl.CostEstimate(flops=8 * 10**9, bytes_accessed=24 * 2**20, transcendentals=2**21),
        name="far_tiles",
    )(place, active, weight, left_grade, near_grade, far_grade, extra, near_inner, near_acc, *arrays)


def across(line, rows):
    column = jnp.broadcast_to(line, (B, rows)).T
    return jnp.concatenate([column, column], axis=1)


def weight_kernel(core_ref, back_ref, projected_ref, hidden_ref, grads_ref, give_ref, keep_ref, pre):
    @pl.when(pl.program_id(0) == 0)
    def _():
        tail = back_ref[:, 1024:, :].astype(jnp.float32)
        inner = jnp.sum(tail[:, 0:4] + tail[:, 4:8], axis=0)
        for part in range(8):
            at = pl.ds(part * B, B)
            grads = back_ref[0, at, :].astype(jnp.float32)
            for source in range(1, 8):
                grads += back_ref[source, at, :].astype(jnp.float32)
            grads_ref[at, :] = grads
            norm = across(tail[part, 8:9, :B] + tail[part, 8:9, B:], B)
            half = part % 2 * B
            product = across(inner[part // 2 : part // 2 + 1, half : half + B], B)
            unit = projected_ref[at, :].astype(jnp.float32) / norm
            pre[at, :] = ((grads - unit * product) / norm).astype(jnp.bfloat16)

    product = lax.dot_general(
        hidden_ref[...], pre[...], (((0,), (0,)), ((), ())), preferred_element_type=jnp.float32
    )
    core = core_ref[0]
    for k in range(2):
        even = product[2 * k * 224 : (2 * k + 1) * 224].astype(jnp.bfloat16)
        odd = product[(2 * k + 1) * 224 : (2 * k + 2) * 224].astype(jnp.bfloat16)
        mine = core == 0
        keep_ref[k] = jnp.where(mine, even, odd)
        give_ref[k] = jnp.where(mine, odd, even)


def weight_pass(core, back, projected, hidden):
    halves = pl.BlockSpec((2, 224, PAIR), lambda s: (s, 0, 0))
    return pl.pallas_call(
        weight_kernel,
        grid=(4,),
        in_specs=[
            SMEM,
            whole(8, 1040, PAIR),
            whole(1024, PAIR),
            pl.BlockSpec((1024, 896), lambda s: (0, s)),
        ],
        out_specs=[whole(1024, PAIR), halves, halves],
        out_shape=[
            jax.ShapeDtypeStruct((1024, PAIR), jnp.float32),
            jax.ShapeDtypeStruct((8, 224, PAIR), jnp.bfloat16),
            jax.ShapeDtypeStruct((8, 224, PAIR), jnp.bfloat16),
        ],
        scratch_shapes=[pltpu.VMEM((1024, PAIR), jnp.bfloat16)],
        compiler_params=pltpu.CompilerParams(vmem_limit_bytes=32 * 2**20),
        cost_estimate=pl.CostEstimate(flops=2 * 10**9, bytes_accessed=15 * 2**20, transcendentals=0),
        name="weight_terms",
    )(core, back, projected, hidden)


def split_two(values):
    high = values.astype(jnp.bfloat16)
    return high, (values - high.astype(jnp.float32)).astype(jnp.bfloat16)


def grade_quads(*arrays):
    lines = jnp.concatenate([a[B:, :B] for a in arrays], axis=0).astype(jnp.float32)
    lines = lines.reshape(len(arrays) // 2, 2, LONG - B, B)[:, :, :2]
    return lines.transpose(0, 2, 1, 3).reshape(-1, 1, QUAD)


def shards(hidden, projection, grades, pattern):
    y, zh, core, x, zl = (lax.axis_index(a) for a in AXES)
    col_here = x * 2 + zl

    grade_mine = grades.astype(jnp.bfloat16).reshape(1, B)
    two = jnp.concatenate([grade_mine, shift(grade_mine, "core", 1)], axis=0)
    projected = jnp.dot(hidden, projection, preferred_element_type=jnp.float32).astype(jnp.bfloat16)
    grade_rows = jnp.broadcast_to(jnp.tile(grades.astype(jnp.bfloat16), 2), (4, 2, 16, PAIR))
    pairs = jnp.broadcast_to(projected.reshape(4, 1, PAIR, PAIR), (4, 2, PAIR, PAIR))
    sent = jnp.concatenate([pairs, grade_rows], axis=2).reshape(8, PAIR + 16, PAIR)
    came = lax.all_to_all(sent, COL, 0, 0, tiled=True)

    both = (pattern + pattern.T).astype(jnp.float32)
    row_here = ((y * 2 + zh) * 2 + core) * 8
    left_ids = jnp.stack([row_here + (x + d) % 4 * 2 + k for d in LEFT for k in (0, 1)])
    right_ids = jnp.stack(
        [((((y + d) % 4) * 2 + (zh ^ z)) * 2 + (core ^ c)) * 8 + col_here for d, z, c in RIGHT]
    )
    left_pick = (left_ids[:, None] == jnp.arange(128)[None]).astype(jnp.float32)
    right_pick = (jnp.arange(128)[:, None] == right_ids[None]).astype(jnp.float32)
    tiles = jnp.dot(
        jnp.dot(left_pick, both, preferred_element_type=jnp.float32), right_pick, preferred_element_type=jnp.float32
    ).reshape(4, 2, 4, 4)
    active = (tiles.sum(axis=(1, 3)) > 0).astype(jnp.int32)
    weight = jnp.repeat((tiles * (-smoothing_divisor / B)).transpose(2, 0, 1, 3), B, axis=3)
    place = jnp.stack([(x + d) % 4 for d in LEFT]).astype(jnp.int32)
    came, two, active, weight, place = lax.optimization_barrier((came, two, active, weight, place))

    rows = jnp.concatenate([came[k, :PAIR] for k in range(8)], axis=1).astype(jnp.float32)
    norms = jnp.sqrt(jnp.sum(rows * rows, axis=1) + epsilon)
    units = (rows / norms[:, None]).astype(jnp.bfloat16)
    unit = jnp.where(zl == 0, units[:B], units[B:])
    unit = jnp.concatenate([unit, jnp.pad(two, ((0, LONG - B - 2), (0, WIDTH - B)))], axis=0)
    own_norm = jnp.where(zl == 0, norms[:B], norms[B:])
    scaled = units * jnp.bfloat16(smoothing_divisor)
    turned = jnp.concatenate([-scaled[:, 1024:], scaled[:, :1024]], axis=1)

    left_grade = came[:, PAIR, :B].astype(jnp.float32).reshape(4, PAIR)
    twice = jnp.concatenate([left_grade, left_grade], axis=0)
    turned_grade = lax.dynamic_slice_in_dim(twice, x, 4, 0)
    left_grade = jnp.stack([turned_grade[d] for d in LEFT])[:, None]
    norm_high, norm_low = split_two(own_norm)
    extra = jnp.concatenate([norm_high, norm_low]).astype(jnp.float32)
    extra = jnp.broadcast_to(extra[None], (8, PAIR))

    below = shift(turned, "x", 1)
    above = shift(turned, "x", -1)
    y_below = shift(unit, "y", 1)
    y_above = shift(unit, "y", -1)
    unit_z = shift(unit, "zh", 1)
    y_below, y_above, unit_z, unit, left_grade, extra = lax.optimization_barrier(
        (y_below, y_above, unit_z, unit, left_grade, extra)
    )
    z_below = shift(unit_z, "y", 1)
    z_above = shift(unit_z, "y", -1)
    other = shift(jnp.concatenate([unit, unit_z], axis=0), "core", 1)
    y_both = jnp.concatenate([y_above, y_below], axis=0)
    below, above, y_below, z_above, z_below, y_above, y_both = lax.optimization_barrier(
        (below, above, y_below, z_above, z_below, y_above, y_both)
    )
    y_other = shift(y_both, "core", 1)
    z_other = shift(jnp.concatenate([z_above, z_below], axis=0), "core", 1)
    far0 = shift(below[:B], "x", 1)
    far1 = shift(above[B:], "x", -1)
    y_far = shift(y_below, "y", 1)
    z_far = shift(z_above, "y", -1)

    lefts = [(turned,), (above,), (below,)]
    rights = [(unit, unit_z, other), (y_above, y_below, y_other), (z_above, z_below, z_other)]
    near_grade = grade_quads(unit, unit_z, y_above, y_below, z_above, z_below)
    near_acc, near_inner = near_pass(active, weight, left_grade, near_grade, lefts, rights)
    y_far, z_far, far0, far1, near_acc, near_inner = lax.optimization_barrier(
        (y_far, z_far, far0, far1, near_acc, near_inner)
    )
    lefts = lefts + [(far0, far1)]
    rights = rights + [(y_far, z_far, shift(y_far, "core", 1), shift(z_far, "core", 1))]
    far_grade = grade_quads(y_far, z_far)
    sums = far_pass(
        place, active, weight, left_grade, near_grade, far_grade, extra, near_inner, near_acc, lefts, rights
    )
    back = lax.all_to_all(sums, COL, 0, 0, tiled=True)

    grads, give, keep = weight_pass(core.astype(jnp.int32).reshape(1), back, projected, hidden)
    chip = (keep.astype(jnp.float32) + shift(give, "core", 1).astype(jnp.float32)).astype(jnp.bfloat16)
    gathered = lax.all_to_all(chip, ("y", "zh"), 0, 0, tiled=True)
    weight_grad = jnp.sum(gathered.astype(jnp.float32), axis=0)
    return grads, weight_grad


def solution(mesh):
    fine = Mesh(np.asarray(mesh.devices).reshape(SIZES), AXES)
    return jax.shard_map(
        shards,
        mesh=fine,
        in_specs=(P(ROW, None), P(None, COL), P(ROW + COL), P()),
        out_specs=(P(ROW, COL), P(ROW, COL)),
        check_vma=False,
    )
```

```python
import functools

import jax
import jax.numpy as jnp
import numpy as np
from jax import lax
from jax.experimental import pallas as pl
from jax.experimental.pallas import tpu as pltpu
from jax.sharding import Mesh, PartitionSpec as P

smoothing_divisor = 64.0
epsilon = 1e-06
AXES = ("y", "zh", "core", "x", "zl")
SIZES = (4, 2, 2, 4, 2)
ROW = ("y", "zh", "core")
COL = ("x", "zl")
B = 128
PAIR = 2 * B
QUAD = 4 * B
LONG = B + 16
HALF = 1024
TAIL = 32
WIDTH = 2048
ANY = pl.BlockSpec(memory_space=pltpu.HBM)
SMEM = pl.BlockSpec(memory_space=pltpu.SMEM)

LEFT = (0, 1, 3, 2)
RIGHT = [(0, z, c) for c in (0, 1) for z in (0, 1)]
RIGHT += [(d, z, c) for z in (0, 1) for c in (0, 1) for d in (1, 3)]
RIGHT += [(2, z, c) for c in (0, 1) for z in (0, 1)]


def shift(value, axis, by):
    size = SIZES[AXES.index(axis)]
    return lax.ppermute(value, axis, [(i, (i + by) % size) for i in range(size)])


def whole(*shape):
    return pl.BlockSpec(shape, lambda *_: (0,) * len(shape))


def fetch(pieces, buffer, sem, first_column=0, columns=WIDTH):
    row = 0
    lanes = pl.ds(first_column, columns)
    for ref in pieces:
        rows = ref.shape[0]
        blocks = [(k, B) for k in range(0, rows, LONG)] if rows % LONG == 0 else [(0, rows)]
        for first, rows in blocks:
            pltpu.make_async_copy(ref.at[pl.ds(first, rows), lanes], buffer.at[pl.ds(row, rows)], sem).start()
            row += rows


def filled(buffer, sem):
    pltpu.make_async_copy(buffer, buffer, sem).wait()


def columns(left_grade_ref, grade_cols, slots):
    for slot in slots:
        grade_cols[slot] = jnp.broadcast_to(left_grade_ref[slot], (B, PAIR)).T


def tile(slot, quad, left_buf, right_buf, weight_ref, grade_cols, right_grade_ref, acc, inner, scores, slopes):
    right = right_buf[quad]
    scores[...] = lax.dot_general(
        left_buf[slot], right, (((1,), (1,)), ((), ())), preferred_element_type=jnp.float32
    )
    for part in range(4):
        rows = slice(part * 64, part * 64 + 64)
        here = grade_cols[slot, rows, :]
        total = jnp.zeros((64, B), jnp.float32)
        for lane in range(4):
            lanes = slice(lane * B, lane * B + B)
            score = scores[rows, lanes]
            label = jnp.clip(here - right_grade_ref[quad, :, lanes], -1.0, 1.0)
            step = label * weight_ref[quad, slot, part // 2 : part // 2 + 1, lanes]
            grown = jnp.exp(label * score)
            slope = (step * pltpu.reciprocal(1.0 + grown, approx=True)).astype(jnp.bfloat16)
            slopes[rows, lanes] = slope
            total += slope.astype(jnp.float32) * score
        inner[slot, rows, :] += total
    acc[slot] += jnp.dot(slopes[...], right_buf[quad, :, :HALF], preferred_element_type=jnp.float32)


def near_kernel(active_ref, weight_ref, left_grade_ref, right_grade_ref, *refs):
    lefts = (refs[0:1], refs[1:2], refs[2:3])
    rights = (refs[3:6], refs[6:9], refs[9:12])
    acc_out, slopes_out, inner, acc, left_buf, right_buf, grade_cols, scores, slopes = refs[12:21]
    left_sem, right_sem, acc_sem, slopes_sem = refs[21:]
    fetch(rights[0], right_buf.at[0], right_sem.at[0])
    for k in range(3):
        fetch(lefts[k], left_buf.at[k], left_sem.at[k])
    acc[...] = jnp.zeros_like(acc)
    inner[...] = jnp.zeros_like(inner)
    columns(left_grade_ref, grade_cols, range(3))
    acc_copy = lambda slot: pltpu.make_async_copy(acc.at[slot], acc_out.at[slot], acc_sem.at[slot])
    slopes_copy = lambda slot: pltpu.make_async_copy(slopes.at[slot], slopes_out.at[slot], slopes_sem.at[slot])

    def one(quad, carry):
        filled(right_buf.at[quad], right_sem.at[quad])
        for slot in range(3):

            @pl.when(quad == 0)
            def _(slot=slot):
                filled(left_buf.at[slot], left_sem.at[slot])
                if slot < 2:
                    fetch(rights[slot + 1], right_buf.at[slot + 1], right_sem.at[slot + 1])

            @pl.when(active_ref[slot, quad] > 0)
            def _(slot=slot):
                tile(
                    slot, quad, left_buf, right_buf, weight_ref, grade_cols, right_grade_ref, acc, inner, scores,
                    slopes.at[slot, quad],
                )

            @pl.when(quad == 2)
            def _(slot=slot):
                acc_copy(slot).start()
                slopes_copy(slot).start()

        return carry

    lax.fori_loop(0, 3, one, 0)
    for slot in range(3):
        acc_copy(slot).wait()
        slopes_copy(slot).wait()


def halves_of(values, sent, slot):
    for chunk in range(8):
        source = (chunk + 4) % 8
        part = values[:, source * B : (source + 1) * B]
        sent[slot, chunk] = (part if chunk < 4 else -part).astype(jnp.bfloat16)


def far_kernel(
    place_ref, active_ref, weight_ref, left_grade_ref, near_grade_ref, far_grade_ref, extra_ref, near_inner, near_acc, *refs
):
    lefts = (refs[0:1], refs[1:2], refs[2:3], refs[3:5])
    rights = (refs[5:8], refs[8:11], refs[11:14], refs[14:18])
    out_ref, slopes_out, acc, inner, lines, sent, tail, left_buf, right_buf = refs[18:27]
    grade_cols, right_grade_ref, scores, slopes = refs[27:31]
    left_sem, right_sem, acc_sem, sent_sem, tail_sem, slopes_sem = refs[31:]
    acc_in = lambda k: pltpu.make_async_copy(near_acc.at[k], acc.at[k], acc_sem.at[k])
    fetch(rights[3], right_buf.at[3], right_sem.at[3])
    for k in range(2):
        fetch(lefts[k], left_buf.at[k], left_sem.at[k])
        acc_in(k).start()
    columns(left_grade_ref, grade_cols, range(4))
    right_grade_ref[:3] = near_grade_ref[...]
    right_grade_ref[3:] = far_grade_ref[...]
    inner[:3] = near_inner[...]
    inner[3] = jnp.zeros((PAIR, B), jnp.float32)
    acc[3] = jnp.zeros((PAIR, HALF), jnp.float32)

    def run(slot, quad, place):
        @pl.when(active_ref[slot, quad] > 0)
        def _():
            tile(
                slot, quad, left_buf, right_buf, weight_ref, grade_cols, right_grade_ref, acc, inner, scores,
                slopes.at[place],
            )

    def home(slot):
        at = pl.ds(pl.multiple_of(place_ref[slot] * PAIR, PAIR), PAIR)
        return pltpu.make_async_copy(sent.at[slot], out_ref.at[:, at, :], sent_sem.at[slot])

    def finish(slot):
        halves_of(acc[slot], sent, slot)
        home(slot).start()
        line = jnp.sum(inner[slot].T, axis=0, keepdims=True) * (1.0 / smoothing_divisor)
        lines[2 * place_ref[slot]] = line[:, :B]
        lines[2 * place_ref[slot] + 1] = line[:, B:]

    filled(right_buf.at[3], right_sem.at[3])
    for slot in range(3):
        filled(left_buf.at[slot], left_sem.at[slot])
        acc_in(slot).wait()
        if slot == 0:
            fetch(lefts[2], left_buf.at[2], left_sem.at[2])
            acc_in(2).start()
            fetch(lefts[3], left_buf.at[3], left_sem.at[3])
            fetch(rights[0], right_buf.at[0], right_sem.at[0])
        if slot == 1:
            fetch(rights[1], right_buf.at[1], right_sem.at[1])
            fetch(rights[2], right_buf.at[2], right_sem.at[2])
        run(slot, 3, slot)
        finish(slot)
    filled(left_buf.at[3], left_sem.at[3])

    def one(quad, carry):
        @pl.when(quad < 3)
        def _():
            filled(right_buf.at[quad], right_sem.at[quad])

        run(3, quad, jnp.where(quad < 3, quad + 4, 3))
        return carry

    lax.fori_loop(0, 4, one, 0)
    slopes_copy = pltpu.make_async_copy(slopes, slopes_out, slopes_sem)
    slopes_copy.start()
    finish(3)
    total = jnp.concatenate([lines[k] for k in range(8)], axis=0)
    high = total.astype(jnp.bfloat16).astype(jnp.float32)
    last = jnp.concatenate([high, total - high, extra_ref[...]], axis=0).astype(jnp.bfloat16)
    for chunk in range(8):
        tail[chunk] = last
    tail_copy = pltpu.make_async_copy(tail, out_ref.at[:, pl.ds(1024, TAIL), :], tail_sem)
    tail_copy.start()
    for slot in range(4):
        home(slot).wait()
    tail_copy.wait()
    slopes_copy.wait()


def rest_kernel(place_ref, active_ref, near_slopes, far_slopes, *refs):
    rights = (refs[0:3], refs[3:6], refs[6:9], refs[9:13])
    out_ref, acc, sent, right_buf, slopes, right_sem, slopes_sem, sent_sem = refs[13:]
    for quad in range(4):
        fetch(rights[quad], right_buf.at[quad], right_sem.at[quad], HALF, HALF)
    for slot in range(4):
        for quad in range(4):
            if slot < 3 and quad < 3:
                source = near_slopes.at[slot, quad]
            else:
                source = far_slopes.at[slot if quad == 3 else 4 + quad]
            pltpu.make_async_copy(source, slopes.at[slot, quad], slopes_sem.at[slot]).start()
    for quad in range(4):
        filled(right_buf.at[quad], right_sem.at[quad])
    for slot in range(4):
        filled(slopes.at[slot], slopes_sem.at[slot])

    def home(slot):
        at = pl.ds(pl.multiple_of(place_ref[slot] * PAIR, PAIR), PAIR)
        return pltpu.make_async_copy(sent.at[slot], out_ref.at[:, at, :], sent_sem.at[slot])

    def one(slot, carry):
        acc[...] = jnp.zeros_like(acc)
        for quad in range(4):

            @pl.when(active_ref[slot, quad] > 0)
            def _(quad=quad):
                acc[...] += jnp.dot(slopes[slot, quad], right_buf[quad], preferred_element_type=jnp.float32)

        halves_of(acc[...], sent, slot)
        home(slot).start()
        return carry

    lax.fori_loop(0, 4, one, 0)
    for slot in range(4):
        home(slot).wait()


def near_pass(active, weight, left_grade, right_grade, lefts, rights):
    arrays = [a for group in (lefts, rights) for pieces in group for a in pieces]
    return pl.pallas_call(
        near_kernel,
        in_specs=[SMEM, whole(*weight.shape), whole(*left_grade.shape), whole(*right_grade.shape)] + [ANY] * len(arrays),
        out_specs=[ANY, ANY, whole(3, PAIR, B)],
        out_shape=[
            jax.ShapeDtypeStruct((3, PAIR, HALF), jnp.float32),
            jax.ShapeDtypeStruct((3, 3, PAIR, QUAD), jnp.bfloat16),
            jax.ShapeDtypeStruct((3, PAIR, B), jnp.float32),
        ],
        scratch_shapes=[
            pltpu.VMEM((3, PAIR, HALF), jnp.float32),
            pltpu.VMEM((3, PAIR, WIDTH), jnp.bfloat16),
            pltpu.VMEM((3, QUAD, WIDTH), jnp.bfloat16),
            pltpu.VMEM((3, PAIR, B), jnp.float32),
            pltpu.VMEM((PAIR, QUAD), jnp.float32),
            pltpu.VMEM((3, 3, PAIR, QUAD), jnp.bfloat16),
            pltpu.SemaphoreType.DMA((3,)),
            pltpu.SemaphoreType.DMA((3,)),
            pltpu.SemaphoreType.DMA((3,)),
            pltpu.SemaphoreType.DMA((3,)),
        ],
        compiler_params=pltpu.CompilerParams(vmem_limit_bytes=60 * 2**20),
        cost_estimate=pl.CostEstimate(flops=8 * 10**9, bytes_accessed=16 * 2**20, transcendentals=2**21),
        name="near_tiles",
    )(active, weight, left_grade, right_grade, *arrays)


def far_pass(place, active, weight, left_grade, near_grade, far_grade, extra, near_inner, near_acc, lefts, rights):
    arrays = [a for group in (lefts, rights) for pieces in group for a in pieces]
    return pl.pallas_call(
        far_kernel,
        in_specs=[SMEM, SMEM]
        + [whole(*a.shape) for a in (weight, left_grade, near_grade, far_grade, extra, near_inner)]
        + [ANY]
        + [ANY] * len(arrays),
        out_specs=[ANY, ANY],
        out_shape=[
            jax.ShapeDtypeStruct((8, 1024 + TAIL, B), jnp.bfloat16),
            jax.ShapeDtypeStruct((7, PAIR, QUAD), jnp.bfloat16),
        ],
        scratch_shapes=[
            pltpu.VMEM((4, PAIR, HALF), jnp.float32),
            pltpu.VMEM((4, PAIR, B), jnp.float32),
            pltpu.VMEM((8, 1, B), jnp.float32),
            pltpu.VMEM((4, 8, PAIR, B), jnp.bfloat16),
            pltpu.VMEM((8, TAIL, B), jnp.bfloat16),
            pltpu.VMEM((4, PAIR, WIDTH), jnp.bfloat16),
            pltpu.VMEM((4, QUAD, WIDTH), jnp.bfloat16),
            pltpu.VMEM((4, PAIR, B), jnp.float32),
            pltpu.VMEM((4, 1, QUAD), jnp.float32),
            pltpu.VMEM((PAIR, QUAD), jnp.float32),
            pltpu.VMEM((7, PAIR, QUAD), jnp.bfloat16),
            pltpu.SemaphoreType.DMA((4,)),
            pltpu.SemaphoreType.DMA((4,)),
            pltpu.SemaphoreType.DMA((3,)),
            pltpu.SemaphoreType.DMA((4,)),
            pltpu.SemaphoreType.DMA,
            pltpu.SemaphoreType.DMA,
        ],
        compiler_params=pltpu.CompilerParams(vmem_limit_bytes=60 * 2**20),
        cost_estimate=pl.CostEstimate(flops=6 * 10**9, bytes_accessed=24 * 2**20, transcendentals=2**21),
        name="far_tiles",
    )(place, active, weight, left_grade, near_grade, far_grade, extra, near_inner, near_acc, *arrays)


def rest_pass(place, active, near_slopes, far_slopes, rights):
    arrays = [a for pieces in rights for a in pieces]
    return pl.pallas_call(
        rest_kernel,
        in_specs=[SMEM, SMEM, ANY, ANY] + [ANY] * len(arrays),
        out_specs=ANY,
        out_shape=jax.ShapeDtypeStruct((8, 1024, B), jnp.bfloat16),
        scratch_shapes=[
            pltpu.VMEM((PAIR, HALF), jnp.float32),
            pltpu.VMEM((4, 8, PAIR, B), jnp.bfloat16),
            pltpu.VMEM((4, QUAD, HALF), jnp.bfloat16),
            pltpu.VMEM((4, 4, PAIR, QUAD), jnp.bfloat16),
            pltpu.SemaphoreType.DMA((4,)),
            pltpu.SemaphoreType.DMA((4,)),
            pltpu.SemaphoreType.DMA((4,)),
        ],
        compiler_params=pltpu.CompilerParams(vmem_limit_bytes=40 * 2**20),
        cost_estimate=pl.CostEstimate(flops=5 * 10**9, bytes_accessed=10 * 2**20, transcendentals=0),
        name="rest_tiles",
    )(place, active, near_slopes, far_slopes, *arrays)


def weight_kernel(half, core_ref, tail_ref, back_ref, projected_ref, hidden_ref, *refs):
    pre = refs[-1]
    grads_ref, give_ref, keep_ref = refs[-4:-1]

    @pl.when(pl.program_id(0) == 0)
    def _():
        tail = tail_ref[...].astype(jnp.float32)
        inner = jnp.sum(tail[:, 0:8] + tail[:, 8:16], axis=0)
        for part in range(8):
            at = pl.ds(part * B, B)
            grads = back_ref[0, at, :].astype(jnp.float32)
            for source in range(1, 8):
                grads += back_ref[source, at, :].astype(jnp.float32)
            if half == 0:
                grads_ref[at, :] = grads
            else:
                grads_ref[at, :B] = refs[0][at, :]
                grads_ref[at, B:] = grads
            norm = jnp.broadcast_to(tail[part, 16:17] + tail[part, 17:18], (B, B)).T
            product = jnp.broadcast_to(inner[part : part + 1], (B, B)).T
            unit = projected_ref[at, half * B : half * B + B].astype(jnp.float32) / norm
            pre[at, :] = ((grads - unit * product) / norm).astype(jnp.bfloat16)

    product = lax.dot_general(
        hidden_ref[...], pre[...], (((0,), (0,)), ((), ())), preferred_element_type=jnp.float32
    )
    mine = core_ref[0] == 0
    for k in range(2):
        even = product[2 * k * 224 : (2 * k + 1) * 224].astype(jnp.bfloat16)
        odd = product[(2 * k + 1) * 224 : (2 * k + 2) * 224].astype(jnp.bfloat16)
        keep_ref[k] = jnp.where(mine, even, odd)
        give_ref[k] = jnp.where(mine, odd, even)


def weight_pass(half, core, back_tail, back, projected, hidden, grads=None):
    chip = jax.ShapeDtypeStruct((8, 224, B), jnp.bfloat16)
    pieces = pl.BlockSpec((2, 224, B), lambda s: (s, 0, 0))
    width = B if half == 0 else PAIR
    return pl.pallas_call(
        functools.partial(weight_kernel, half),
        grid=(4,),
        in_specs=[
            SMEM,
            pl.BlockSpec((8, TAIL, B), lambda s: (0, 1024 // TAIL, 0)),
            pl.BlockSpec((8, 1024, B), lambda s: (0, 0, 0)),
            whole(1024, PAIR),
            pl.BlockSpec((1024, 896), lambda s: (0, s)),
        ]
        + ([] if grads is None else [whole(1024, B)]),
        out_specs=[whole(1024, width), pieces, pieces],
        out_shape=[jax.ShapeDtypeStruct((1024, width), jnp.float32), chip, chip],
        scratch_shapes=[pltpu.VMEM((1024, B), jnp.bfloat16)],
        compiler_params=pltpu.CompilerParams(vmem_limit_bytes=32 * 2**20),
        cost_estimate=pl.CostEstimate(flops=2 * 10**9, bytes_accessed=12 * 2**20, transcendentals=0),
        name="weight_terms",
    )(core, back_tail, back, projected, hidden, *([] if grads is None else [grads]))


def on_chip(give, keep):
    return (keep.astype(jnp.float32) + shift(give, "core", 1).astype(jnp.float32)).astype(jnp.bfloat16)


def spread_sum(chip, y, zh):
    total = None
    for dy in range(4):
        for dz in range(2):
            piece = lax.dynamic_index_in_dim(chip, (y + dy) % 4 * 2 + (zh ^ dz), 0, False)
            if dy or dz:
                pairs = [(a * 2 + b, (a + dy) % 4 * 2 + (b ^ dz)) for a in range(4) for b in range(2)]
                piece = lax.ppermute(piece, ("y", "zh"), pairs)
            piece = piece.astype(jnp.float32)
            total = piece if total is None else total + piece
    return total


def split_two(values):
    high = values.astype(jnp.bfloat16)
    return high, (values - high.astype(jnp.float32)).astype(jnp.bfloat16)


def grade_quads(*arrays):
    lines = jnp.concatenate([a[B:, :B] for a in arrays], axis=0).astype(jnp.float32)
    lines = lines.reshape(len(arrays) // 2, 2, LONG - B, B)[:, :, :2]
    return lines.transpose(0, 2, 1, 3).reshape(-1, 1, QUAD)


def shards(hidden, projection, grades, pattern):
    y, zh, core, x, zl = (lax.axis_index(a) for a in AXES)
    col_here = x * 2 + zl

    grade_mine = grades.astype(jnp.bfloat16).reshape(1, B)
    two = jnp.concatenate([grade_mine, shift(grade_mine, "core", 1)], axis=0)
    projected = jnp.dot(hidden, projection, preferred_element_type=jnp.float32).astype(jnp.bfloat16)
    grade_rows = jnp.broadcast_to(jnp.tile(grades.astype(jnp.bfloat16), 2), (4, 2, 16, PAIR))
    pairs = jnp.broadcast_to(projected.reshape(4, 1, PAIR, PAIR), (4, 2, PAIR, PAIR))
    sent = jnp.concatenate([pairs, grade_rows], axis=2).reshape(8, PAIR + 16, PAIR)
    came = lax.all_to_all(sent, COL, 0, 0, tiled=True)

    both = (pattern + pattern.T).astype(jnp.float32)
    row_here = ((y * 2 + zh) * 2 + core) * 8
    left_ids = jnp.stack([row_here + (x + d) % 4 * 2 + k for d in LEFT for k in (0, 1)])
    right_ids = jnp.stack(
        [((((y + d) % 4) * 2 + (zh ^ z)) * 2 + (core ^ c)) * 8 + col_here for d, z, c in RIGHT]
    )
    left_pick = (left_ids[:, None] == jnp.arange(128)[None]).astype(jnp.float32)
    right_pick = (jnp.arange(128)[:, None] == right_ids[None]).astype(jnp.float32)
    tiles = jnp.dot(
        jnp.dot(left_pick, both, preferred_element_type=jnp.float32), right_pick, preferred_element_type=jnp.float32
    ).reshape(4, 2, 4, 4)
    active = (tiles.sum(axis=(1, 3)) > 0).astype(jnp.int32)
    weight = jnp.repeat((tiles * (-smoothing_divisor / B)).transpose(2, 0, 1, 3), B, axis=3)
    place = jnp.stack([(x + d) % 4 for d in LEFT]).astype(jnp.int32)
    came, two, active, weight, place = lax.optimization_barrier((came, two, active, weight, place))

    rows = [came[k, :PAIR, h : h + B] for h in (0, B) for k in range(8)]
    rows = jnp.concatenate(rows, axis=1).astype(jnp.float32)
    norms = jnp.sqrt(jnp.sum(rows * rows, axis=1) + epsilon)
    units = (rows / norms[:, None]).astype(jnp.bfloat16)
    unit = jnp.where(zl == 0, units[:B], units[B:])
    unit = jnp.concatenate([unit, jnp.pad(two, ((0, LONG - B - 2), (0, WIDTH - B)))], axis=0)
    own_norm = jnp.where(zl == 0, norms[:B], norms[B:])
    scaled = units * jnp.bfloat16(smoothing_divisor)
    quarter = [scaled[:, k * 512 : (k + 1) * 512] for k in range(4)]
    turned = jnp.concatenate([-quarter[1], quarter[0], -quarter[3], quarter[2]], axis=1)

    left_grade = came[:, PAIR, :B].astype(jnp.float32).reshape(4, PAIR)
    twice = jnp.concatenate([left_grade, left_grade], axis=0)
    turned_grade = lax.dynamic_slice_in_dim(twice, x, 4, 0)
    left_grade = jnp.stack([turned_grade[d] for d in LEFT])[:, None]
    extra = jnp.stack([part.astype(jnp.float32) for part in split_two(own_norm)])
    extra = jnp.pad(extra, ((0, TAIL - 18), (0, 0)))

    below = shift(turned, "x", 1)
    above = shift(turned, "x", -1)
    y_below = shift(unit, "y", 1)
    y_above = shift(unit, "y", -1)
    unit_z = shift(unit, "zh", 1)
    y_below, y_above, unit_z, unit, left_grade, extra = lax.optimization_barrier(
        (y_below, y_above, unit_z, unit, left_grade, extra)
    )
    z_below = shift(unit_z, "y", 1)
    z_above = shift(unit_z, "y", -1)
    other = shift(jnp.concatenate([unit, unit_z], axis=0), "core", 1)
    y_both = jnp.concatenate([y_above, y_below], axis=0)
    below, above, y_below, z_above, z_below, y_above, y_both = lax.optimization_barrier(
        (below, above, y_below, z_above, z_below, y_above, y_both)
    )
    y_other = shift(y_both, "core", 1)
    z_other = shift(jnp.concatenate([z_above, z_below], axis=0), "core", 1)
    far0 = shift(below[:B], "x", 1)
    far1 = shift(above[B:], "x", -1)
    y_far = shift(y_below, "y", 1)
    z_far = shift(z_above, "y", -1)

    lefts = [(turned,), (above,), (below,)]
    rights = [(unit, unit_z, other), (y_above, y_below, y_other), (z_above, z_below, z_other)]
    near_grade = grade_quads(unit, unit_z, y_above, y_below, z_above, z_below)
    near_acc, near_slopes, near_inner = near_pass(active, weight, left_grade, near_grade, lefts, rights)
    y_far, z_far, far0, far1, near_acc, near_inner = lax.optimization_barrier(
        (y_far, z_far, far0, far1, near_acc, near_inner)
    )
    lefts = lefts + [(far0, far1)]
    rights = rights + [(y_far, z_far, shift(y_far, "core", 1), shift(z_far, "core", 1))]
    far_grade = grade_quads(y_far, z_far)
    sums, far_slopes = far_pass(
        place, active, weight, left_grade, near_grade, far_grade, extra, near_inner, near_acc, lefts, rights
    )
    back = lax.all_to_all(sums, COL, 0, 0, tiled=True)
    others = rest_pass(place, active, near_slopes, far_slopes, rights)
    other_back = lax.all_to_all(others, COL, 0, 0, tiled=True)
    core_here = core.astype(jnp.int32).reshape(1)
    half_grads, give, keep = weight_pass(0, core_here, back, back, projected, hidden)
    half_weight = spread_sum(on_chip(give, keep), y, zh)
    other_back, half_weight = lax.optimization_barrier((other_back, half_weight))
    grads, give, keep = weight_pass(1, core_here, back, other_back, projected, hidden, half_grads)
    gathered = lax.all_to_all(on_chip(give, keep), ("y", "zh"), 0, 0, tiled=True)
    other_weight = jnp.sum(gathered.astype(jnp.float32), axis=0)
    return grads, jnp.concatenate([half_weight, other_weight], axis=1)


def solution(mesh):
    fine = Mesh(np.asarray(mesh.devices).reshape(SIZES), AXES)
    return jax.shard_map(
        shards,
        mesh=fine,
        in_specs=(P(ROW, None), P(None, COL), P(ROW + COL), P()),
        out_specs=(P(ROW, COL), P(ROW, COL)),
        check_vma=False,
    )
```

```python
import functools

import jax
import jax.numpy as jnp
import numpy as np
from jax import lax
from jax.experimental import pallas as pl
from jax.experimental.pallas import tpu as pltpu
from jax.sharding import Mesh, PartitionSpec as P

smoothing_divisor = 64.0
epsilon = 1e-06
AXES = ("y", "zh", "core", "x", "zl")
SIZES = (4, 2, 2, 4, 2)
ROW = ("y", "zh", "core")
COL = ("x", "zl")
B = 128
PAIR = 2 * B
QUAD = 4 * B
LONG = B + 16
WIDTH = 2048
ANY = pl.BlockSpec(memory_space=pltpu.HBM)
SMEM = pl.BlockSpec(memory_space=pltpu.SMEM)

LEFT = (0, 1, 3, 2)
RIGHT = [(0, z, c) for c in (0, 1) for z in (0, 1)]
RIGHT += [(d, z, c) for z in (0, 1) for c in (0, 1) for d in (1, 3)]
RIGHT += [(2, z, c) for c in (0, 1) for z in (0, 1)]


def shift(value, axis, by):
    size = SIZES[AXES.index(axis)]
    return lax.ppermute(value, axis, [(i, (i + by) % size) for i in range(size)])


def whole(*shape):
    return pl.BlockSpec(shape, lambda *_: (0,) * len(shape))


def fetch(pieces, buffer, sem):
    row = 0
    for ref, first, rows in pieces:
        pltpu.make_async_copy(ref.at[pl.ds(first, rows)], buffer.at[pl.ds(row, rows)], sem).start()
        row += rows


def blocks(ref, first=0, count=1):
    return [(ref, k * LONG, B) for k in range(first, first + count)]


def quads(refs):
    unit, unit_z, y_above, y_below, z_above, z_below, other, y_other, z_other = refs
    return (
        blocks(unit) + blocks(unit_z) + blocks(other, 0, 2),
        blocks(y_above) + blocks(y_below) + blocks(y_other, 0, 2),
        blocks(z_above) + blocks(z_below) + blocks(z_other, 0, 2),
    )


def filled(buffer, sem):
    pltpu.make_async_copy(buffer, buffer, sem).wait()


def columns(left_grade_ref, grade_cols, slots):
    for slot in slots:
        grade_cols[slot] = jnp.broadcast_to(left_grade_ref[slot], (B, PAIR)).T


def run_tiles(tiles, left_buf, right_buf, weight_ref, grade_cols, right_grade_ref, acc, inner, scores, slopes):
    def score(k):
        slot, quad = tiles[k]
        scores[k % 2] = lax.dot_general(
            left_buf[slot], right_buf[quad], (((1,), (1,)), ((), ())), preferred_element_type=jnp.float32
        )

    score(0)
    for k, (slot, quad) in enumerate(tiles):
        if k + 1 < len(tiles):
            score(k + 1)
        for part in range(4):
            rows = slice(part * 64, part * 64 + 64)
            here = grade_cols[slot, rows, :]
            total = jnp.zeros((64, B), jnp.float32)
            for lane in range(4):
                lanes = slice(lane * B, lane * B + B)
                value = scores[k % 2, rows, lanes]
                label = jnp.clip(here - right_grade_ref[quad, :, lanes], -1.0, 1.0)
                step = label * weight_ref[quad, slot, part // 2 : part // 2 + 1, lanes]
                grown = jnp.exp(label * value)
                slope = (step * pltpu.reciprocal(1.0 + grown, approx=True)).astype(jnp.bfloat16)
                slopes[k % 2, rows, lanes] = slope
                total += slope.astype(jnp.float32) * value
            inner[slot, rows, :] += total
        acc[slot] += jnp.dot(slopes[k % 2], right_buf[quad], preferred_element_type=jnp.float32)


def near_kernel(active_ref, weight_ref, left_grade_ref, right_grade_ref, *refs):
    lefts = [[(ref, 0, PAIR)] for ref in refs[:3]]
    rights = quads(refs[3:12])
    acc_out, inner, acc, left_buf, right_buf, grade_cols, scores, slopes, left_sem, right_sem, acc_sem = refs[12:]
    fetch(rights[0], right_buf.at[0], right_sem.at[0])
    for k in range(3):
        fetch(lefts[k], left_buf.at[k], left_sem.at[k])
    acc[...] = jnp.zeros_like(acc)
    inner[...] = jnp.zeros_like(inner)
    columns(left_grade_ref, grade_cols, range(3))
    acc_copy = lambda slot: pltpu.make_async_copy(acc.at[slot], acc_out.at[slot], acc_sem.at[slot])
    for k in range(3):
        filled(left_buf.at[k], left_sem.at[k])
    for k in (1, 2):
        fetch(rights[k], right_buf.at[k], right_sem.at[k])

    def one(quad, carry):
        filled(right_buf.at[quad], right_sem.at[quad])

        @pl.when(active_ref[0, quad] + active_ref[1, quad] + active_ref[2, quad] > 0)
        def _():
            run_tiles(
                [(0, quad), (1, quad), (2, quad)],
                left_buf, right_buf, weight_ref, grade_cols, right_grade_ref, acc, inner, scores, slopes,
            )

        return carry

    lax.fori_loop(0, 3, one, 0)
    for slot in range(3):
        acc_copy(slot).start()
    for slot in range(3):
        acc_copy(slot).wait()


def far_kernel(
    place_ref, active_ref, weight_ref, left_grade_ref, near_grade_ref, far_grade_ref, extra_ref, near_inner, near_acc, *refs
):
    lefts = [[(ref, 0, PAIR)] for ref in refs[:3]] + [[(refs[3], 0, B), (refs[4], 0, B)]]
    rights = quads(refs[5:14]) + (sum((blocks(ref) for ref in refs[14:18]), []),)
    out_ref, acc, inner, lines, sent, tail, left_buf, right_buf = refs[18:26]
    grade_cols, right_grade_ref, scores, slopes, left_sem, right_sem, acc_sem, sent_sem, tail_sem = refs[26:]
    acc_in = lambda k: pltpu.make_async_copy(near_acc.at[k], acc.at[k], acc_sem.at[k])
    fetch(rights[3], right_buf.at[3], right_sem.at[3])
    for k in range(2):
        fetch(lefts[k], left_buf.at[k], left_sem.at[k])
        acc_in(k).start()
    columns(left_grade_ref, grade_cols, range(4))
    right_grade_ref[:3] = near_grade_ref[...]
    right_grade_ref[3:] = far_grade_ref[...]
    inner[:3] = near_inner[...]
    inner[3] = jnp.zeros((PAIR, B), jnp.float32)
    acc[3] = jnp.zeros((PAIR, WIDTH), jnp.float32)

    def run(tiles):
        @pl.when(sum(active_ref[slot, quad] for slot, quad in tiles) > 0)
        def _():
            run_tiles(
                tiles, left_buf, right_buf, weight_ref, grade_cols, right_grade_ref, acc, inner, scores, slopes
            )

    def home(slot):
        at = pl.ds(pl.multiple_of(place_ref[slot] * PAIR, PAIR), PAIR)
        return pltpu.make_async_copy(sent.at[slot], out_ref.at[:, at, :], sent_sem.at[slot])

    def finish(slot):
        for chunk in range(8):
            source = (chunk + 4) % 8
            values = acc[slot, :, source * PAIR : (source + 1) * PAIR]
            sent[slot, chunk] = (values if chunk < 4 else -values).astype(jnp.bfloat16)
        home(slot).start()
        lines[place_ref[slot]] = jnp.sum(inner[slot].T, axis=0, keepdims=True) * (1.0 / smoothing_divisor)

    filled(right_buf.at[3], right_sem.at[3])
    for slot in range(2):
        filled(left_buf.at[slot], left_sem.at[slot])
        acc_in(slot).wait()
    fetch(lefts[2], left_buf.at[2], left_sem.at[2])
    acc_in(2).start()
    fetch(lefts[3], left_buf.at[3], left_sem.at[3])
    for k in range(3):
        fetch(rights[k], right_buf.at[k], right_sem.at[k])
    run([(0, 3), (1, 3)])
    finish(0)
    finish(1)
    for slot in (2, 3):
        filled(left_buf.at[slot], left_sem.at[slot])
    acc_in(2).wait()
    run([(2, 3), (3, 3)])
    finish(2)
    for quad in range(3):
        filled(right_buf.at[quad], right_sem.at[quad])
    run([(3, 0), (3, 1), (3, 2)])
    finish(3)
    total = jnp.concatenate([lines[k] for k in range(4)], axis=0)
    high = total.astype(jnp.bfloat16).astype(jnp.float32)
    last = jnp.concatenate([high, total - high, extra_ref[...]], axis=0).astype(jnp.bfloat16)
    for chunk in range(8):
        tail[chunk] = last
    tail_copy = pltpu.make_async_copy(tail, out_ref.at[:, pl.ds(1024, 16), :], tail_sem)
    tail_copy.start()
    for slot in range(4):
        home(slot).wait()
    tail_copy.wait()


def near_pass(active, weight, left_grade, right_grade, arrays):
    return pl.pallas_call(
        near_kernel,
        in_specs=[SMEM, whole(*weight.shape), whole(*left_grade.shape), whole(*right_grade.shape)] + [ANY] * len(arrays),
        out_specs=[ANY, whole(3, PAIR, B)],
        out_shape=[
            jax.ShapeDtypeStruct((3, PAIR, WIDTH), jnp.float32),
            jax.ShapeDtypeStruct((3, PAIR, B), jnp.float32),
        ],
        scratch_shapes=[
            pltpu.VMEM((3, PAIR, WIDTH), jnp.float32),
            pltpu.VMEM((3, PAIR, WIDTH), jnp.bfloat16),
            pltpu.VMEM((3, QUAD, WIDTH), jnp.bfloat16),
            pltpu.VMEM((3, PAIR, B), jnp.float32),
            pltpu.VMEM((2, PAIR, QUAD), jnp.float32),
            pltpu.VMEM((2, PAIR, QUAD), jnp.bfloat16),
            pltpu.SemaphoreType.DMA((3,)),
            pltpu.SemaphoreType.DMA((3,)),
            pltpu.SemaphoreType.DMA((3,)),
        ],
        compiler_params=pltpu.CompilerParams(vmem_limit_bytes=60 * 2**20),
        cost_estimate=pl.CostEstimate(flops=9 * 10**9, bytes_accessed=16 * 2**20, transcendentals=2**21),
        name="near_tiles",
    )(active, weight, left_grade, right_grade, *arrays)


def far_pass(place, active, weight, left_grade, near_grade, far_grade, extra, near_inner, near_acc, arrays):
    return pl.pallas_call(
        far_kernel,
        in_specs=[SMEM, SMEM]
        + [whole(*a.shape) for a in (weight, left_grade, near_grade, far_grade, extra, near_inner)]
        + [ANY]
        + [ANY] * len(arrays),
        out_specs=ANY,
        out_shape=jax.ShapeDtypeStruct((8, 1040, PAIR), jnp.bfloat16),
        scratch_shapes=[
            pltpu.VMEM((4, PAIR, WIDTH), jnp.float32),
            pltpu.VMEM((4, PAIR, B), jnp.float32),
            pltpu.VMEM((4, 1, PAIR), jnp.float32),
            pltpu.VMEM((4, 8, PAIR, PAIR), jnp.bfloat16),
            pltpu.VMEM((8, 16, PAIR), jnp.bfloat16),
            pltpu.VMEM((4, PAIR, WIDTH), jnp.bfloat16),
            pltpu.VMEM((4, QUAD, WIDTH), jnp.bfloat16),
            pltpu.VMEM((4, PAIR, B), jnp.float32),
            pltpu.VMEM((4, 1, QUAD), jnp.float32),
            pltpu.VMEM((2, PAIR, QUAD), jnp.float32),
            pltpu.VMEM((2, PAIR, QUAD), jnp.bfloat16),
            pltpu.SemaphoreType.DMA((4,)),
            pltpu.SemaphoreType.DMA((4,)),
            pltpu.SemaphoreType.DMA((3,)),
            pltpu.SemaphoreType.DMA((4,)),
            pltpu.SemaphoreType.DMA,
        ],
        compiler_params=pltpu.CompilerParams(vmem_limit_bytes=60 * 2**20),
        cost_estimate=pl.CostEstimate(flops=8 * 10**9, bytes_accessed=24 * 2**20, transcendentals=2**21),
        name="far_tiles",
    )(place, active, weight, left_grade, near_grade, far_grade, extra, near_inner, near_acc, *arrays)


def across(line, rows):
    column = jnp.broadcast_to(line, (B, rows)).T
    return jnp.concatenate([column, column], axis=1)


def weight_kernel(core_ref, back_ref, projected_ref, hidden_ref, grads_ref, give_ref, keep_ref, pre):
    @pl.when(pl.program_id(0) == 0)
    def _():
        tail = back_ref[:, 1024:, :].astype(jnp.float32)
        inner = jnp.sum(tail[:, 0:4] + tail[:, 4:8], axis=0)
        for part in range(8):
            at = pl.ds(part * B, B)
            grads = back_ref[0, at, :].astype(jnp.float32)
            for source in range(1, 8):
                grads += back_ref[source, at, :].astype(jnp.float32)
            grads_ref[at, :] = grads
            norm = across(tail[part, 8:9, :B] + tail[part, 8:9, B:], B)
            half = part % 2 * B
            product = across(inner[part // 2 : part // 2 + 1, half : half + B], B)
            unit = projected_ref[at, :].astype(jnp.float32) / norm
            pre[at, :] = ((grads - unit * product) / norm).astype(jnp.bfloat16)

    product = lax.dot_general(
        hidden_ref[...], pre[...], (((0,), (0,)), ((), ())), preferred_element_type=jnp.float32
    )
    core = core_ref[0]
    for k in range(2):
        even = product[2 * k * 224 : (2 * k + 1) * 224].astype(jnp.bfloat16)
        odd = product[(2 * k + 1) * 224 : (2 * k + 2) * 224].astype(jnp.bfloat16)
        mine = core == 0
        keep_ref[k] = jnp.where(mine, even, odd)
        give_ref[k] = jnp.where(mine, odd, even)


def weight_pass(core, back, projected, hidden):
    halves = pl.BlockSpec((2, 224, PAIR), lambda s: (s, 0, 0))
    return pl.pallas_call(
        weight_kernel,
        grid=(4,),
        in_specs=[
            SMEM,
            whole(8, 1040, PAIR),
            whole(1024, PAIR),
            pl.BlockSpec((1024, 896), lambda s: (0, s)),
        ],
        out_specs=[whole(1024, PAIR), halves, halves],
        out_shape=[
            jax.ShapeDtypeStruct((1024, PAIR), jnp.float32),
            jax.ShapeDtypeStruct((8, 224, PAIR), jnp.bfloat16),
            jax.ShapeDtypeStruct((8, 224, PAIR), jnp.bfloat16),
        ],
        scratch_shapes=[pltpu.VMEM((1024, PAIR), jnp.bfloat16)],
        compiler_params=pltpu.CompilerParams(vmem_limit_bytes=32 * 2**20),
        cost_estimate=pl.CostEstimate(flops=2 * 10**9, bytes_accessed=15 * 2**20, transcendentals=0),
        name="weight_terms",
    )(core, back, projected, hidden)


def split_two(values):
    high = values.astype(jnp.bfloat16)
    return high, (values - high.astype(jnp.float32)).astype(jnp.bfloat16)


def grade_quads(*arrays):
    lines = jnp.concatenate([a[B:, :B] for a in arrays], axis=0).astype(jnp.float32)
    lines = lines.reshape(len(arrays) // 2, 2, LONG - B, B)[:, :, :2]
    return lines.transpose(0, 2, 1, 3).reshape(-1, 1, QUAD)


def shards(hidden, projection, grades, pattern):
    y, zh, core, x, zl = (lax.axis_index(a) for a in AXES)
    col_here = x * 2 + zl

    grade_mine = grades.astype(jnp.bfloat16).reshape(1, B)
    two = jnp.concatenate([grade_mine, shift(grade_mine, "core", 1)], axis=0)
    projected = jnp.dot(hidden, projection, preferred_element_type=jnp.float32).astype(jnp.bfloat16)
    grade_rows = jnp.broadcast_to(jnp.tile(grades.astype(jnp.bfloat16), 2), (4, 2, 16, PAIR))
    pairs = jnp.broadcast_to(projected.reshape(4, 1, PAIR, PAIR), (4, 2, PAIR, PAIR))
    sent = jnp.concatenate([pairs, grade_rows], axis=2).reshape(8, PAIR + 16, PAIR)
    came = lax.all_to_all(sent, COL, 0, 0, tiled=True)

    both = (pattern + pattern.T).astype(jnp.float32)
    row_here = ((y * 2 + zh) * 2 + core) * 8
    left_ids = jnp.stack([row_here + (x + d) % 4 * 2 + k for d in LEFT for k in (0, 1)])
    right_ids = jnp.stack(
        [((((y + d) % 4) * 2 + (zh ^ z)) * 2 + (core ^ c)) * 8 + col_here for d, z, c in RIGHT]
    )
    left_pick = (left_ids[:, None] == jnp.arange(128)[None]).astype(jnp.float32)
    right_pick = (jnp.arange(128)[:, None] == right_ids[None]).astype(jnp.float32)
    tiles = jnp.dot(
        jnp.dot(left_pick, both, preferred_element_type=jnp.float32), right_pick, preferred_element_type=jnp.float32
    ).reshape(4, 2, 4, 4)
    active = (tiles.sum(axis=(1, 3)) > 0).astype(jnp.int32)
    weight = jnp.repeat((tiles * (-smoothing_divisor / B)).transpose(2, 0, 1, 3), B, axis=3)
    place = jnp.stack([(x + d) % 4 for d in LEFT]).astype(jnp.int32)
    came, two, active, weight, place = lax.optimization_barrier((came, two, active, weight, place))

    rows = jnp.concatenate([came[k, :PAIR] for k in range(8)], axis=1).astype(jnp.float32)
    norms = jnp.sqrt(jnp.sum(rows * rows, axis=1) + epsilon)
    units = (rows / norms[:, None]).astype(jnp.bfloat16)
    unit = jnp.where(zl == 0, units[:B], units[B:])
    unit = jnp.concatenate([unit, jnp.pad(two, ((0, LONG - B - 2), (0, WIDTH - B)))], axis=0)
    own_norm = jnp.where(zl == 0, norms[:B], norms[B:])
    scaled = units * jnp.bfloat16(smoothing_divisor)
    turned = jnp.concatenate([-scaled[:, 1024:], scaled[:, :1024]], axis=1)

    left_grade = came[:, PAIR, :B].astype(jnp.float32).reshape(4, PAIR)
    twice = jnp.concatenate([left_grade, left_grade], axis=0)
    turned_grade = lax.dynamic_slice_in_dim(twice, x, 4, 0)
    left_grade = jnp.stack([turned_grade[d] for d in LEFT])[:, None]
    norm_high, norm_low = split_two(own_norm)
    extra = jnp.concatenate([norm_high, norm_low]).astype(jnp.float32)
    extra = jnp.broadcast_to(extra[None], (8, PAIR))

    below = shift(turned, "x", 1)
    above = shift(turned, "x", -1)
    y_below = shift(unit, "y", 1)
    y_above = shift(unit, "y", -1)
    unit_z = shift(unit, "zh", 1)
    y_below, y_above, unit_z, unit, left_grade, extra = lax.optimization_barrier(
        (y_below, y_above, unit_z, unit, left_grade, extra)
    )
    z_below = shift(unit_z, "y", 1)
    z_above = shift(unit_z, "y", -1)
    other = shift(jnp.concatenate([unit, unit_z], axis=0), "core", 1)
    y_both = jnp.concatenate([y_above, y_below], axis=0)
    below, above, y_below, z_above, z_below, y_above, y_both = lax.optimization_barrier(
        (below, above, y_below, z_above, z_below, y_above, y_both)
    )
    y_other = shift(y_both, "core", 1)
    z_other = shift(jnp.concatenate([z_above, z_below], axis=0), "core", 1)
    far0 = shift(below[:B], "x", 1)
    far1 = shift(above[B:], "x", -1)
    y_far = shift(y_below, "y", 1)
    z_far = shift(z_above, "y", -1)

    nearby = [unit, unit_z, y_above, y_below, z_above, z_below, other, y_other, z_other]
    near_grade = grade_quads(unit, unit_z, y_above, y_below, z_above, z_below)
    near_acc, near_inner = near_pass(
        active, weight, left_grade, near_grade, [turned, above, below] + nearby
    )
    y_far, z_far, far0, far1, near_acc, near_inner = lax.optimization_barrier(
        (y_far, z_far, far0, far1, near_acc, near_inner)
    )
    beyond = [y_far, z_far, shift(y_far, "core", 1), shift(z_far, "core", 1)]
    far_grade = grade_quads(y_far, z_far)
    sums = far_pass(
        place, active, weight, left_grade, near_grade, far_grade, extra, near_inner, near_acc,
        [turned, above, below, far0, far1] + nearby + beyond,
    )
    back = lax.all_to_all(sums, COL, 0, 0, tiled=True)

    grads, give, keep = weight_pass(core.astype(jnp.int32).reshape(1), back, projected, hidden)
    chip = (keep.astype(jnp.float32) + shift(give, "core", 1).astype(jnp.float32)).astype(jnp.bfloat16)
    gathered = lax.all_to_all(chip, ("y", "zh"), 0, 0, tiled=True)
    weight_grad = jnp.sum(gathered.astype(jnp.float32), axis=0)
    return grads, weight_grad


def solution(mesh):
    fine = Mesh(np.asarray(mesh.devices).reshape(SIZES), AXES)
    return jax.shard_map(
        shards,
        mesh=fine,
        in_specs=(P(ROW, None), P(None, COL), P(ROW + COL), P()),
        out_specs=(P(ROW, COL), P(ROW, COL)),
        check_vma=False,
    )
```

```python
import functools

import jax
import jax.numpy as jnp
import numpy as np
from jax import lax
from jax.experimental import pallas as pl
from jax.experimental.pallas import tpu as pltpu
from jax.sharding import Mesh, PartitionSpec as P

smoothing_divisor = 64.0
epsilon = 1e-06
AXES = ("y", "zh", "core", "x", "zl")
SIZES = (4, 2, 2, 4, 2)
ROW = ("y", "zh", "core")
COL = ("x", "zl")
B = 128
PAIR = 2 * B
QUAD = 4 * B
LONG = B + 16
WIDTH = 2048
ANY = pl.BlockSpec(memory_space=pltpu.HBM)
SMEM = pl.BlockSpec(memory_space=pltpu.SMEM)

LEFT = (0, 1, 3, 2)
RIGHT = [(0, z, c) for c in (0, 1) for z in (0, 1)]
RIGHT += [(d, z, c) for z in (0, 1) for c in (0, 1) for d in (1, 3)]
RIGHT += [(2, z, c) for c in (0, 1) for z in (0, 1)]


def shift(value, axis, by):
    size = SIZES[AXES.index(axis)]
    return lax.ppermute(value, axis, [(i, (i + by) % size) for i in range(size)])


def whole(*shape):
    return pl.BlockSpec(shape, lambda *_: (0,) * len(shape))


def fetch(pieces, buffer, sem):
    row = 0
    for ref, first, rows in pieces:
        pltpu.make_async_copy(ref.at[pl.ds(first, rows)], buffer.at[pl.ds(row, rows)], sem).start()
        row += rows


def blocks(ref, first=0, count=1):
    return [(ref, k * LONG, B) for k in range(first, first + count)]


def quads(refs):
    unit, unit_z, y_above, y_below, z_above, z_below, other, y_other, z_other = refs
    return (
        blocks(unit) + blocks(unit_z) + blocks(other, 0, 2),
        blocks(y_above) + blocks(y_below) + blocks(y_other, 0, 2),
        blocks(z_above) + blocks(z_below) + blocks(z_other, 0, 2),
    )


def filled(buffer, sem):
    pltpu.make_async_copy(buffer, buffer, sem).wait()


def columns(left_grade_ref, grade_cols, slots):
    for slot in slots:
        grade_cols[slot] = jnp.broadcast_to(left_grade_ref[slot], (B, PAIR)).T


def score(left, right, scores):
    scores[...] = lax.dot_general(left[...], right[...], (((1,), (1,)), ((), ())), preferred_element_type=jnp.float32)


def slope(scores, weight, grade_cols, right_grade, slopes, inner, first):
    for part in range(4):
        rows = slice(part * 64, part * 64 + 64)
        here = grade_cols[rows, :]
        total = None
        for lane in range(4):
            lanes = slice(lane * B, lane * B + B)
            value = scores[rows, lanes]
            label = jnp.clip(here - right_grade[:, lanes], -1.0, 1.0)
            step = label * weight[part // 2 : part // 2 + 1, lanes]
            grown = jnp.exp(label * value)
            one = (step * pltpu.reciprocal(1.0 + grown, approx=True)).astype(jnp.bfloat16)
            slopes[rows, lanes] = one
            term = one.astype(jnp.float32) * value
            total = term if total is None else total + term
        inner[rows, :] = total if first else inner[rows, :] + total


def quad_rows(quad, count=1):
    return pl.ds(quad * QUAD, count * QUAD)


def near_kernel(weight_ref, left_grade_ref, right_grade_ref, *refs):
    lefts = [[(ref, 0, PAIR)] for ref in refs[:3]]
    rights = quads(refs[3:12])
    acc_out, inner, acc, left_buf, right_buf, grade_cols, scores, slopes, left_sem, right_sem, acc_sem = refs[12:]
    right_at = lambda quad: right_buf.at[quad_rows(quad)]
    for k in range(3):
        fetch(rights[k], right_at(k), right_sem.at[k])
        if k == 0:
            fetch(lefts[0], left_buf.at[0], left_sem.at[0])
    for k in (1, 2):
        fetch(lefts[k], left_buf.at[k], left_sem.at[k])
    columns(left_grade_ref, grade_cols, range(3))
    acc_copy = lambda slot: pltpu.make_async_copy(acc.at[slot], acc_out.at[slot], acc_sem.at[slot])

    def ahead(slot, quad):
        if quad == 0:
            filled(left_buf.at[slot], left_sem.at[slot])
        if slot == 0:
            filled(right_at(quad), right_sem.at[quad])
        score(left_buf.at[slot], right_at(quad), scores.at[:, quad_rows(quad)])

    def arithmetic(slot, quad):
        slope(
            scores.at[:, quad_rows(quad)], weight_ref.at[quad, slot], grade_cols.at[slot], right_grade_ref.at[quad],
            slopes.at[slot % 2, :, quad_rows(quad)], inner.at[slot], quad == 0,
        )

    ahead(0, 0)
    for slot in range(3):
        ahead(slot, 1)
        arithmetic(slot, 0)
        ahead(slot, 2)
        arithmetic(slot, 1)
        if slot < 2:
            ahead(slot + 1, 0)
        arithmetic(slot, 2)
        for chunk in range(8):
            lanes = slice(chunk * PAIR, chunk * PAIR + PAIR)
            acc[slot, :, lanes] = jnp.dot(slopes[slot % 2], right_buf[:, lanes], preferred_element_type=jnp.float32)
        acc_copy(slot).start()
    for slot in range(3):
        acc_copy(slot).wait()


def far_kernel(
    place_ref, weight_ref, left_grade_ref, near_grade_ref, far_grade_ref, extra_ref, near_inner, near_acc, *refs
):
    lefts = [[(ref, 0, PAIR)] for ref in refs[:3]] + [[(refs[3], 0, B), (refs[4], 0, B)]]
    rights = quads(refs[5:14]) + (sum((blocks(ref) for ref in refs[14:18]), []),)
    out_ref, acc, inner, lines, sent, tail, left_buf, right_buf = refs[18:26]
    grade_cols, scores, near_slopes, slopes, left_sem, right_sem, acc_sem, sent_sem, tail_sem = refs[26:]
    right_at = lambda quad: right_buf.at[quad_rows(quad)]
    acc_in = lambda k: pltpu.make_async_copy(near_acc.at[k], acc.at[k], acc_sem.at[k])
    fetch(rights[3], right_at(3), right_sem.at[3])
    for k in range(3):
        fetch(lefts[k], left_buf.at[k], left_sem.at[k])
        acc_in(k).start()
    columns(left_grade_ref, grade_cols, range(4))
    inner[:3] = near_inner[...]

    def home(slot):
        at = pl.ds(pl.multiple_of(place_ref[slot] * PAIR, PAIR), PAIR)
        return pltpu.make_async_copy(sent.at[slot], out_ref.at[:, at, :], sent_sem.at[slot])

    def ahead(slot, quad):
        if quad == 3:
            filled(left_buf.at[slot], left_sem.at[slot])
        if slot == 3 and quad < 3:
            filled(right_at(quad), right_sem.at[quad])
        part = slot if quad == 3 else quad
        score(left_buf.at[slot], right_at(quad), scores.at[:, quad_rows(part)])

    def arithmetic(slot, quad):
        part = slot if quad == 3 else quad
        out = near_slopes.at[slot] if slot < 3 else slopes.at[:, quad_rows(quad)]
        right_grade = far_grade_ref.at[0] if quad == 3 else near_grade_ref.at[quad]
        slope(
            scores.at[:, quad_rows(part)], weight_ref.at[quad, slot], grade_cols.at[slot], right_grade,
            out, inner.at[slot], slot == 3 and quad == 3,
        )

    def finish(slot):
        if slot < 3:
            acc_in(slot).wait()
        for chunk in range(8):
            source = (chunk + 4) % 8
            lanes = slice(source * PAIR, source * PAIR + PAIR)
            if slot < 3:
                part = jnp.dot(near_slopes[slot], right_buf[3 * QUAD :, lanes], preferred_element_type=jnp.float32)
                part = part + acc[slot, :, lanes]
            else:
                part = jnp.dot(slopes[...], right_buf[:, lanes], preferred_element_type=jnp.float32)
            sent[slot, chunk] = (part if chunk < 4 else -part).astype(jnp.bfloat16)
        home(slot).start()
        lines[place_ref[slot]] = jnp.sum(inner[slot].T, axis=0, keepdims=True) * (1.0 / smoothing_divisor)

    filled(right_at(3), right_sem.at[3])
    ahead(0, 3)
    fetch(lefts[3], left_buf.at[3], left_sem.at[3])
    for k in range(3):
        fetch(rights[k], right_at(k), right_sem.at[k])
    ahead(1, 3)
    arithmetic(0, 3)
    ahead(2, 3)
    arithmetic(1, 3)
    finish(0)
    ahead(3, 3)
    arithmetic(2, 3)
    finish(1)
    ahead(3, 0)
    arithmetic(3, 3)
    finish(2)
    ahead(3, 1)
    arithmetic(3, 0)
    ahead(3, 2)
    arithmetic(3, 1)
    arithmetic(3, 2)
    finish(3)
    total = jnp.concatenate([lines[k] for k in range(4)], axis=0)
    high = total.astype(jnp.bfloat16).astype(jnp.float32)
    last = jnp.concatenate([high, total - high, extra_ref[...]], axis=0).astype(jnp.bfloat16)
    for chunk in range(8):
        tail[chunk] = last
    tail_copy = pltpu.make_async_copy(tail, out_ref.at[:, pl.ds(1024, 16), :], tail_sem)
    tail_copy.start()
    for slot in range(4):
        home(slot).wait()
    tail_copy.wait()


def near_pass(weight, left_grade, right_grade, arrays):
    return pl.pallas_call(
        near_kernel,
        in_specs=[whole(*a.shape) for a in (weight, left_grade, right_grade)] + [ANY] * len(arrays),
        out_specs=[ANY, whole(3, PAIR, B)],
        out_shape=[
            jax.ShapeDtypeStruct((3, PAIR, WIDTH), jnp.float32),
            jax.ShapeDtypeStruct((3, PAIR, B), jnp.float32),
        ],
        scratch_shapes=[
            pltpu.VMEM((3, PAIR, WIDTH), jnp.float32),
            pltpu.VMEM((3, PAIR, WIDTH), jnp.bfloat16),
            pltpu.VMEM((3 * QUAD, WIDTH), jnp.bfloat16),
            pltpu.VMEM((3, PAIR, B), jnp.float32),
            pltpu.VMEM((PAIR, 3 * QUAD), jnp.float32),
            pltpu.VMEM((2, PAIR, 3 * QUAD), jnp.bfloat16),
            pltpu.SemaphoreType.DMA((3,)),
            pltpu.SemaphoreType.DMA((3,)),
            pltpu.SemaphoreType.DMA((3,)),
        ],
        compiler_params=pltpu.CompilerParams(vmem_limit_bytes=60 * 2**20),
        cost_estimate=pl.CostEstimate(flops=9 * 10**9, bytes_accessed=16 * 2**20, transcendentals=2**21),
        name="near_tiles",
    )(weight, left_grade, right_grade, *arrays)


def far_pass(place, weight, left_grade, near_grade, far_grade, extra, near_inner, near_acc, arrays):
    return pl.pallas_call(
        far_kernel,
        in_specs=[SMEM]
        + [whole(*a.shape) for a in (weight, left_grade, near_grade, far_grade, extra, near_inner)]
        + [ANY]
        + [ANY] * len(arrays),
        out_specs=ANY,
        out_shape=jax.ShapeDtypeStruct((8, 1040, PAIR), jnp.bfloat16),
        scratch_shapes=[
            pltpu.VMEM((3, PAIR, WIDTH), jnp.float32),
            pltpu.VMEM((4, PAIR, B), jnp.float32),
            pltpu.VMEM((4, 1, PAIR), jnp.float32),
            pltpu.VMEM((4, 8, PAIR, PAIR), jnp.bfloat16),
            pltpu.VMEM((8, 16, PAIR), jnp.bfloat16),
            pltpu.VMEM((4, PAIR, WIDTH), jnp.bfloat16),
            pltpu.VMEM((4 * QUAD, WIDTH), jnp.bfloat16),
            pltpu.VMEM((4, PAIR, B), jnp.float32),
            pltpu.VMEM((PAIR, 4 * QUAD), jnp.float32),
            pltpu.VMEM((3, PAIR, QUAD), jnp.bfloat16),
            pltpu.VMEM((PAIR, 4 * QUAD), jnp.bfloat16),
            pltpu.SemaphoreType.DMA((4,)),
            pltpu.SemaphoreType.DMA((4,)),
            pltpu.SemaphoreType.DMA((3,)),
            pltpu.SemaphoreType.DMA((4,)),
            pltpu.SemaphoreType.DMA,
        ],
        compiler_params=pltpu.CompilerParams(vmem_limit_bytes=60 * 2**20),
        cost_estimate=pl.CostEstimate(flops=8 * 10**9, bytes_accessed=24 * 2**20, transcendentals=2**21),
        name="far_tiles",
    )(place, weight, left_grade, near_grade, far_grade, extra, near_inner, near_acc, *arrays)


def across(line, rows):
    column = jnp.broadcast_to(line, (B, rows)).T
    return jnp.concatenate([column, column], axis=1)


def weight_kernel(core_ref, back_ref, projected_ref, hidden_ref, grads_ref, give_ref, keep_ref, pre):
    @pl.when(pl.program_id(0) == 0)
    def _():
        tail = back_ref[:, 1024:, :].astype(jnp.float32)
        inner = jnp.sum(tail[:, 0:4] + tail[:, 4:8], axis=0)
        for part in range(8):
            at = pl.ds(part * B, B)
            grads = back_ref[0, at, :].astype(jnp.float32)
            for source in range(1, 8):
                grads += back_ref[source, at, :].astype(jnp.float32)
            grads_ref[at, :] = grads
            norm = across(tail[part, 8:9, :B] + tail[part, 8:9, B:], B)
            half = part % 2 * B
            product = across(inner[part // 2 : part // 2 + 1, half : half + B], B)
            unit = projected_ref[at, :].astype(jnp.float32) / norm
            pre[at, :] = ((grads - unit * product) / norm).astype(jnp.bfloat16)

    product = lax.dot_general(
        hidden_ref[...], pre[...], (((0,), (0,)), ((), ())), preferred_element_type=jnp.float32
    )
    core = core_ref[0]
    for k in range(2):
        even = product[2 * k * 224 : (2 * k + 1) * 224].astype(jnp.bfloat16)
        odd = product[(2 * k + 1) * 224 : (2 * k + 2) * 224].astype(jnp.bfloat16)
        mine = core == 0
        keep_ref[k] = jnp.where(mine, even, odd)
        give_ref[k] = jnp.where(mine, odd, even)


def weight_pass(core, back, projected, hidden):
    halves = pl.BlockSpec((2, 224, PAIR), lambda s: (s, 0, 0))
    return pl.pallas_call(
        weight_kernel,
        grid=(4,),
        in_specs=[
            SMEM,
            whole(8, 1040, PAIR),
            whole(1024, PAIR),
            pl.BlockSpec((1024, 896), lambda s: (0, s)),
        ],
        out_specs=[whole(1024, PAIR), halves, halves],
        out_shape=[
            jax.ShapeDtypeStruct((1024, PAIR), jnp.float32),
            jax.ShapeDtypeStruct((8, 224, PAIR), jnp.bfloat16),
            jax.ShapeDtypeStruct((8, 224, PAIR), jnp.bfloat16),
        ],
        scratch_shapes=[pltpu.VMEM((1024, PAIR), jnp.bfloat16)],
        compiler_params=pltpu.CompilerParams(vmem_limit_bytes=32 * 2**20),
        cost_estimate=pl.CostEstimate(flops=2 * 10**9, bytes_accessed=15 * 2**20, transcendentals=0),
        name="weight_terms",
    )(core, back, projected, hidden)


def split_two(values):
    high = values.astype(jnp.bfloat16)
    return high, (values - high.astype(jnp.float32)).astype(jnp.bfloat16)


def grade_quads(*arrays):
    lines = jnp.concatenate([a[B:, :B] for a in arrays], axis=0).astype(jnp.float32)
    lines = lines.reshape(len(arrays) // 2, 2, LONG - B, B)[:, :, :2]
    return lines.transpose(0, 2, 1, 3).reshape(-1, 1, QUAD)


def shards(hidden, projection, grades, pattern):
    y, zh, core, x, zl = (lax.axis_index(a) for a in AXES)
    col_here = x * 2 + zl

    grade_mine = grades.astype(jnp.bfloat16).reshape(1, B)
    two = jnp.concatenate([grade_mine, shift(grade_mine, "core", 1)], axis=0)
    projected = jnp.dot(hidden, projection, preferred_element_type=jnp.float32).astype(jnp.bfloat16)
    grade_rows = jnp.broadcast_to(jnp.tile(grades.astype(jnp.bfloat16), 2), (4, 2, 16, PAIR))
    pairs = jnp.broadcast_to(projected.reshape(4, 1, PAIR, PAIR), (4, 2, PAIR, PAIR))
    sent = jnp.concatenate([pairs, grade_rows], axis=2).reshape(8, PAIR + 16, PAIR)
    came = lax.all_to_all(sent, COL, 0, 0, tiled=True)

    both = (pattern + pattern.T).astype(jnp.float32)
    row_here = ((y * 2 + zh) * 2 + core) * 8
    left_ids = jnp.stack([row_here + (x + d) % 4 * 2 + k for d in LEFT for k in (0, 1)])
    right_ids = jnp.stack(
        [((((y + d) % 4) * 2 + (zh ^ z)) * 2 + (core ^ c)) * 8 + col_here for d, z, c in RIGHT]
    )
    left_pick = (left_ids[:, None] == jnp.arange(128)[None]).astype(jnp.float32)
    right_pick = (jnp.arange(128)[:, None] == right_ids[None]).astype(jnp.float32)
    tiles = jnp.dot(
        jnp.dot(left_pick, both, preferred_element_type=jnp.float32), right_pick, preferred_element_type=jnp.float32
    ).reshape(4, 2, 4, 4)
    weight = jnp.repeat((tiles * (-smoothing_divisor / B)).transpose(2, 0, 1, 3), B, axis=3)
    place = jnp.stack([(x + d) % 4 for d in LEFT]).astype(jnp.int32)
    came, two, weight, place = lax.optimization_barrier((came, two, weight, place))

    rows = jnp.concatenate([came[k, :PAIR] for k in range(8)], axis=1).astype(jnp.float32)
    norms = jnp.sqrt(jnp.sum(rows * rows, axis=1) + epsilon)
    units = (rows / norms[:, None]).astype(jnp.bfloat16)
    unit = jnp.where(zl == 0, units[:B], units[B:])
    unit = jnp.concatenate([unit, jnp.pad(two, ((0, LONG - B - 2), (0, WIDTH - B)))], axis=0)
    own_norm = jnp.where(zl == 0, norms[:B], norms[B:])
    scaled = units * jnp.bfloat16(smoothing_divisor)
    turned = jnp.concatenate([-scaled[:, 1024:], scaled[:, :1024]], axis=1)

    left_grade = came[:, PAIR, :B].astype(jnp.float32).reshape(4, PAIR)
    twice = jnp.concatenate([left_grade, left_grade], axis=0)
    turned_grade = lax.dynamic_slice_in_dim(twice, x, 4, 0)
    left_grade = jnp.stack([turned_grade[d] for d in LEFT])[:, None]
    norm_high, norm_low = split_two(own_norm)
    extra = jnp.concatenate([norm_high, norm_low]).astype(jnp.float32)
    extra = jnp.broadcast_to(extra[None], (8, PAIR))

    below = shift(turned, "x", 1)
    above = shift(turned, "x", -1)
    y_below = shift(unit, "y", 1)
    y_above = shift(unit, "y", -1)
    unit_z = shift(unit, "zh", 1)
    y_below, y_above, unit_z, unit, left_grade, extra = lax.optimization_barrier(
        (y_below, y_above, unit_z, unit, left_grade, extra)
    )
    z_below = shift(unit_z, "y", 1)
    z_above = shift(unit_z, "y", -1)
    other = shift(jnp.concatenate([unit, unit_z], axis=0), "core", 1)
    y_both = jnp.concatenate([y_above, y_below], axis=0)
    below, above, y_below, z_above, z_below, y_above, y_both = lax.optimization_barrier(
        (below, above, y_below, z_above, z_below, y_above, y_both)
    )
    y_other = shift(y_both, "core", 1)
    z_other = shift(jnp.concatenate([z_above, z_below], axis=0), "core", 1)
    far0 = shift(below[:B], "x", 1)
    far1 = shift(above[B:], "x", -1)
    y_far = shift(y_below, "y", 1)
    z_far = shift(z_above, "y", -1)

    nearby = [unit, unit_z, y_above, y_below, z_above, z_below, other, y_other, z_other]
    near_grade = grade_quads(unit, unit_z, y_above, y_below, z_above, z_below)
    near_acc, near_inner = near_pass(
        weight, left_grade, near_grade, [turned, above, below] + nearby
    )
    y_far, z_far, far0, far1, near_acc, near_inner = lax.optimization_barrier(
        (y_far, z_far, far0, far1, near_acc, near_inner)
    )
    beyond = [y_far, z_far, shift(y_far, "core", 1), shift(z_far, "core", 1)]
    far_grade = grade_quads(y_far, z_far)
    sums = far_pass(
        place, weight, left_grade, near_grade, far_grade, extra, near_inner, near_acc,
        [turned, above, below, far0, far1] + nearby + beyond,
    )
    back = lax.all_to_all(sums, COL, 0, 0, tiled=True)

    grads, give, keep = weight_pass(core.astype(jnp.int32).reshape(1), back, projected, hidden)
    chip = (keep.astype(jnp.float32) + shift(give, "core", 1).astype(jnp.float32)).astype(jnp.bfloat16)
    gathered = lax.all_to_all(chip, ("y", "zh"), 0, 0, tiled=True)
    weight_grad = jnp.sum(gathered.astype(jnp.float32), axis=0)
    return grads, weight_grad


def solution(mesh):
    fine = Mesh(np.asarray(mesh.devices).reshape(SIZES), AXES)
    return jax.shard_map(
        shards,
        mesh=fine,
        in_specs=(P(ROW, None), P(None, COL), P(ROW + COL), P()),
        out_specs=(P(ROW, COL), P(ROW, COL)),
        check_vma=False,
    )
```

```python
import functools

import jax
import jax.numpy as jnp
import numpy as np
from jax import lax
from jax.experimental import pallas as pl
from jax.experimental.pallas import tpu as pltpu
from jax.sharding import Mesh, PartitionSpec as P

smoothing_divisor = 64.0
epsilon = 1e-06
AXES = ("y", "zh", "core", "x", "zl")
SIZES = (4, 2, 2, 4, 2)
ROW = ("y", "zh", "core")
COL = ("x", "zl")
B = 128
PAIR = 2 * B
QUAD = 4 * B
LONG = B + 16
WIDTH = 2048
ANY = pl.BlockSpec(memory_space=pltpu.HBM)
SMEM = pl.BlockSpec(memory_space=pltpu.SMEM)

LEFT = (0, 1, 3, 2)
RIGHT = [(0, z, c) for c in (0, 1) for z in (0, 1)]
RIGHT += [(d, z, c) for z in (0, 1) for c in (0, 1) for d in (1, 3)]
RIGHT += [(2, z, c) for c in (0, 1) for z in (0, 1)]


def shift(value, axis, by):
    size = SIZES[AXES.index(axis)]
    return lax.ppermute(value, axis, [(i, (i + by) % size) for i in range(size)])


def whole(*shape):
    return pl.BlockSpec(shape, lambda *_: (0,) * len(shape))


def fetch(pieces, buffer, sem):
    row = 0
    for ref, first, rows in pieces:
        pltpu.make_async_copy(ref.at[pl.ds(first, rows)], buffer.at[pl.ds(row, rows)], sem).start()
        row += rows


def blocks(ref, first=0, count=1):
    return [(ref, k * LONG, B) for k in range(first, first + count)]


def quads(refs):
    unit, unit_z, y_above, y_below, z_above, z_below, other, y_other, z_other = refs
    return (
        blocks(unit) + blocks(unit_z) + blocks(other, 0, 2),
        blocks(y_above) + blocks(y_below) + blocks(y_other, 0, 2),
        blocks(z_above) + blocks(z_below) + blocks(z_other, 0, 2),
    )


def filled(buffer, sem):
    pltpu.make_async_copy(buffer, buffer, sem).wait()


def columns(left_grade_ref, grade_cols, slots):
    for slot in slots:
        grade_cols[slot] = jnp.broadcast_to(left_grade_ref[slot], (B, PAIR)).T


def score(left, right, scores):
    scores[...] = lax.dot_general(left[...], right[...], (((1,), (1,)), ((), ())), preferred_element_type=jnp.float32)


def slope(scores, weight, grade_cols, right_grade, slopes, inner, first):
    for part in range(4):
        rows = slice(part * 64, part * 64 + 64)
        here = grade_cols[rows, :]
        total = None
        for lane in range(4):
            lanes = slice(lane * B, lane * B + B)
            value = scores[rows, lanes]
            label = jnp.clip(here - right_grade[:, lanes], -1.0, 1.0)
            step = label * weight[part // 2 : part // 2 + 1, lanes]
            grown = jnp.exp(label * value)
            one = (step * pltpu.reciprocal(1.0 + grown, approx=True)).astype(jnp.bfloat16)
            slopes[rows, lanes] = one
            term = one.astype(jnp.float32) * value
            total = term if total is None else total + term
        inner[rows, :] = total if first else inner[rows, :] + total


def quad_rows(quad, count=1):
    return pl.ds(quad * QUAD, count * QUAD)


def near_kernel(weight_ref, left_grade_ref, right_grade_ref, *refs):
    lefts = [[(ref, 0, PAIR)] for ref in refs[:3]]
    rights = quads(refs[3:12])
    acc_out, inner, acc, left_buf, right_buf, grade_cols, scores, slopes, left_sem, right_sem, acc_sem = refs[12:]
    right_at = lambda quad: right_buf.at[quad_rows(quad)]
    fetch(lefts[0], left_buf.at[0], left_sem.at[0])
    fetch(rights[0], right_at(0), right_sem.at[0])
    columns(left_grade_ref, grade_cols, range(3))

    def acc_copy(slot, half):
        lanes = pl.ds(half * (WIDTH // 2), WIDTH // 2)
        return pltpu.make_async_copy(acc.at[slot, :, lanes], acc_out.at[slot, :, lanes], acc_sem.at[2 * slot + half])


    def ahead(slot, quad):
        if quad == 0:
            filled(left_buf.at[slot], left_sem.at[slot])
        if slot == 0:
            filled(right_at(quad), right_sem.at[quad])
            if quad < 2:
                fetch(rights[quad + 1], right_at(quad + 1), right_sem.at[quad + 1])
            else:
                fetch(lefts[1], left_buf.at[1], left_sem.at[1])
                fetch(lefts[2], left_buf.at[2], left_sem.at[2])
        score(left_buf.at[slot], right_at(quad), scores.at[:, quad_rows(quad)])

    def arithmetic(slot, quad):
        slope(
            scores.at[:, quad_rows(quad)], weight_ref.at[quad, slot], grade_cols.at[slot], right_grade_ref.at[quad],
            slopes.at[slot % 2, :, quad_rows(quad)], inner.at[slot], quad == 0,
        )

    ahead(0, 0)
    for slot in range(3):
        ahead(slot, 1)
        arithmetic(slot, 0)
        ahead(slot, 2)
        arithmetic(slot, 1)
        if slot < 2:
            ahead(slot + 1, 0)
        arithmetic(slot, 2)
        for chunk in range(8):
            lanes = slice(chunk * PAIR, chunk * PAIR + PAIR)
            acc[slot, :, lanes] = jnp.dot(slopes[slot % 2], right_buf[:, lanes], preferred_element_type=jnp.float32)
            if chunk % 4 == 3:
                acc_copy(slot, chunk // 4).start()
    for slot in range(3):
        acc_copy(slot, 0).wait()
        acc_copy(slot, 1).wait()


def far_kernel(
    place_ref, weight_ref, left_grade_ref, near_grade_ref, far_grade_ref, extra_ref, near_inner, near_acc, *refs
):
    lefts = [[(ref, 0, PAIR)] for ref in refs[:3]] + [[(refs[3], 0, B), (refs[4], 0, B)]]
    rights = quads(refs[5:14]) + (sum((blocks(ref) for ref in refs[14:18]), []),)
    out_ref, acc, inner, lines, sent, tail, left_buf, right_buf = refs[18:26]
    grade_cols, scores, near_slopes, slopes, left_sem, right_sem, acc_sem, sent_sem, tail_sem = refs[26:]
    right_at = lambda quad: right_buf.at[quad_rows(quad)]
    acc_in = lambda k: pltpu.make_async_copy(near_acc.at[k], acc.at[k], acc_sem.at[k])
    fetch(rights[3], right_at(3), right_sem.at[3])
    fetch(lefts[0], left_buf.at[0], left_sem.at[0])
    fetch(lefts[1], left_buf.at[1], left_sem.at[1])
    columns(left_grade_ref, grade_cols, range(4))
    inner[:3] = near_inner[...]

    def home(slot):
        at = pl.ds(pl.multiple_of(place_ref[slot] * PAIR, PAIR), PAIR)
        return pltpu.make_async_copy(sent.at[slot], out_ref.at[:, at, :], sent_sem.at[slot])

    def ahead(slot, quad):
        if quad == 3:
            filled(left_buf.at[slot], left_sem.at[slot])
        if slot == 3 and quad < 3:
            filled(right_at(quad), right_sem.at[quad])
        part = slot if quad == 3 else quad
        score(left_buf.at[slot], right_at(quad), scores.at[:, quad_rows(part)])

    def arithmetic(slot, quad):
        part = slot if quad == 3 else quad
        out = near_slopes.at[slot] if slot < 3 else slopes.at[:, quad_rows(quad)]
        right_grade = far_grade_ref.at[0] if quad == 3 else near_grade_ref.at[quad]
        slope(
            scores.at[:, quad_rows(part)], weight_ref.at[quad, slot], grade_cols.at[slot], right_grade,
            out, inner.at[slot], slot == 3 and quad == 3,
        )

    def finish(slot):
        if slot < 3:
            acc_in(slot).wait()
        for chunk in range(8):
            source = (chunk + 4) % 8
            lanes = slice(source * PAIR, source * PAIR + PAIR)
            if slot < 3:
                part = jnp.dot(near_slopes[slot], right_buf[3 * QUAD :, lanes], preferred_element_type=jnp.float32)
                part = part + acc[slot, :, lanes]
            else:
                part = jnp.dot(slopes[...], right_buf[:, lanes], preferred_element_type=jnp.float32)
            sent[slot, chunk] = (part if chunk < 4 else -part).astype(jnp.bfloat16)
        home(slot).start()
        lines[place_ref[slot]] = jnp.sum(inner[slot].T, axis=0, keepdims=True) * (1.0 / smoothing_divisor)

    filled(right_at(3), right_sem.at[3])
    ahead(0, 3)
    acc_in(0).start()
    fetch(lefts[2], left_buf.at[2], left_sem.at[2])
    ahead(1, 3)
    arithmetic(0, 3)
    ahead(2, 3)
    fetch(lefts[3], left_buf.at[3], left_sem.at[3])
    acc_in(1).start()
    fetch(rights[0], right_at(0), right_sem.at[0])
    arithmetic(1, 3)
    finish(0)
    ahead(3, 3)
    acc_in(2).start()
    fetch(rights[1], right_at(1), right_sem.at[1])
    fetch(rights[2], right_at(2), right_sem.at[2])
    arithmetic(2, 3)
    finish(1)
    ahead(3, 0)
    arithmetic(3, 3)
    finish(2)
    ahead(3, 1)
    arithmetic(3, 0)
    ahead(3, 2)
    arithmetic(3, 1)
    arithmetic(3, 2)
    finish(3)
    total = jnp.concatenate([lines[k] for k in range(4)], axis=0)
    high = total.astype(jnp.bfloat16).astype(jnp.float32)
    last = jnp.concatenate([high, total - high, extra_ref[...]], axis=0).astype(jnp.bfloat16)
    for chunk in range(8):
        tail[chunk] = last
    tail_copy = pltpu.make_async_copy(tail, out_ref.at[:, pl.ds(1024, 16), :], tail_sem)
    tail_copy.start()
    for slot in range(4):
        home(slot).wait()
    tail_copy.wait()


def near_pass(weight, left_grade, right_grade, arrays):
    return pl.pallas_call(
        near_kernel,
        in_specs=[whole(*a.shape) for a in (weight, left_grade, right_grade)] + [ANY] * len(arrays),
        out_specs=[ANY, whole(3, PAIR, B)],
        out_shape=[
            jax.ShapeDtypeStruct((3, PAIR, WIDTH), jnp.float32),
            jax.ShapeDtypeStruct((3, PAIR, B), jnp.float32),
        ],
        scratch_shapes=[
            pltpu.VMEM((3, PAIR, WIDTH), jnp.float32),
            pltpu.VMEM((3, PAIR, WIDTH), jnp.bfloat16),
            pltpu.VMEM((3 * QUAD, WIDTH), jnp.bfloat16),
            pltpu.VMEM((3, PAIR, B), jnp.float32),
            pltpu.VMEM((PAIR, 3 * QUAD), jnp.float32),
            pltpu.VMEM((2, PAIR, 3 * QUAD), jnp.bfloat16),
            pltpu.SemaphoreType.DMA((3,)),
            pltpu.SemaphoreType.DMA((3,)),
            pltpu.SemaphoreType.DMA((6,)),
        ],
        compiler_params=pltpu.CompilerParams(vmem_limit_bytes=60 * 2**20),
        cost_estimate=pl.CostEstimate(flops=9 * 10**9, bytes_accessed=16 * 2**20, transcendentals=2**21),
        name="near_tiles",
    )(weight, left_grade, right_grade, *arrays)


def far_pass(place, weight, left_grade, near_grade, far_grade, extra, near_inner, near_acc, arrays):
    return pl.pallas_call(
        far_kernel,
        in_specs=[SMEM]
        + [whole(*a.shape) for a in (weight, left_grade, near_grade, far_grade, extra, near_inner)]
        + [ANY]
        + [ANY] * len(arrays),
        out_specs=ANY,
        out_shape=jax.ShapeDtypeStruct((8, 1040, PAIR), jnp.bfloat16),
        scratch_shapes=[
            pltpu.VMEM((3, PAIR, WIDTH), jnp.float32),
            pltpu.VMEM((4, PAIR, B), jnp.float32),
            pltpu.VMEM((4, 1, PAIR), jnp.float32),
            pltpu.VMEM((4, 8, PAIR, PAIR), jnp.bfloat16),
            pltpu.VMEM((8, 16, PAIR), jnp.bfloat16),
            pltpu.VMEM((4, PAIR, WIDTH), jnp.bfloat16),
            pltpu.VMEM((4 * QUAD, WIDTH), jnp.bfloat16),
            pltpu.VMEM((4, PAIR, B), jnp.float32),
            pltpu.VMEM((PAIR, 4 * QUAD), jnp.float32),
            pltpu.VMEM((3, PAIR, QUAD), jnp.bfloat16),
            pltpu.VMEM((PAIR, 4 * QUAD), jnp.bfloat16),
            pltpu.SemaphoreType.DMA((4,)),
            pltpu.SemaphoreType.DMA((4,)),
            pltpu.SemaphoreType.DMA((3,)),
            pltpu.SemaphoreType.DMA((4,)),
            pltpu.SemaphoreType.DMA,
        ],
        compiler_params=pltpu.CompilerParams(vmem_limit_bytes=60 * 2**20),
        cost_estimate=pl.CostEstimate(flops=8 * 10**9, bytes_accessed=24 * 2**20, transcendentals=2**21),
        name="far_tiles",
    )(place, weight, left_grade, near_grade, far_grade, extra, near_inner, near_acc, *arrays)


def across(line, rows):
    column = jnp.broadcast_to(line, (B, rows)).T
    return jnp.concatenate([column, column], axis=1)


def weight_kernel(core_ref, back_ref, projected_ref, hidden_ref, grads_ref, give_ref, keep_ref, pre):
    @pl.when(pl.program_id(0) == 0)
    def _():
        tail = back_ref[:, 1024:, :].astype(jnp.float32)
        inner = jnp.sum(tail[:, 0:4] + tail[:, 4:8], axis=0)
        for part in range(8):
            at = pl.ds(part * B, B)
            grads = back_ref[0, at, :].astype(jnp.float32)
            for source in range(1, 8):
                grads += back_ref[source, at, :].astype(jnp.float32)
            grads_ref[at, :] = grads
            norm = across(tail[part, 8:9, :B] + tail[part, 8:9, B:], B)
            half = part % 2 * B
            product = across(inner[part // 2 : part // 2 + 1, half : half + B], B)
            unit = projected_ref[at, :].astype(jnp.float32) / norm
            pre[at, :] = ((grads - unit * product) / norm).astype(jnp.bfloat16)

    product = lax.dot_general(
        hidden_ref[...], pre[...], (((0,), (0,)), ((), ())), preferred_element_type=jnp.float32
    )
    core = core_ref[0]
    for k in range(2):
        even = product[2 * k * 224 : (2 * k + 1) * 224].astype(jnp.bfloat16)
        odd = product[(2 * k + 1) * 224 : (2 * k + 2) * 224].astype(jnp.bfloat16)
        mine = core == 0
        keep_ref[k] = jnp.where(mine, even, odd)
        give_ref[k] = jnp.where(mine, odd, even)


def weight_pass(core, back, projected, hidden):
    halves = pl.BlockSpec((2, 224, PAIR), lambda s: (s, 0, 0))
    return pl.pallas_call(
        weight_kernel,
        grid=(4,),
        in_specs=[
            SMEM,
            whole(8, 1040, PAIR),
            whole(1024, PAIR),
            pl.BlockSpec((1024, 896), lambda s: (0, s)),
        ],
        out_specs=[whole(1024, PAIR), halves, halves],
        out_shape=[
            jax.ShapeDtypeStruct((1024, PAIR), jnp.float32),
            jax.ShapeDtypeStruct((8, 224, PAIR), jnp.bfloat16),
            jax.ShapeDtypeStruct((8, 224, PAIR), jnp.bfloat16),
        ],
        scratch_shapes=[pltpu.VMEM((1024, PAIR), jnp.bfloat16)],
        compiler_params=pltpu.CompilerParams(vmem_limit_bytes=32 * 2**20),
        cost_estimate=pl.CostEstimate(flops=2 * 10**9, bytes_accessed=15 * 2**20, transcendentals=0),
        name="weight_terms",
    )(core, back, projected, hidden)


def split_two(values):
    high = values.astype(jnp.bfloat16)
    return high, (values - high.astype(jnp.float32)).astype(jnp.bfloat16)


def grade_quads(*arrays):
    lines = jnp.concatenate([a[B:, :B] for a in arrays], axis=0).astype(jnp.float32)
    lines = lines.reshape(len(arrays) // 2, 2, LONG - B, B)[:, :, :2]
    return lines.transpose(0, 2, 1, 3).reshape(-1, 1, QUAD)


def shards(hidden, projection, grades, pattern):
    y, zh, core, x, zl = (lax.axis_index(a) for a in AXES)
    col_here = x * 2 + zl

    grade_mine = grades.astype(jnp.bfloat16).reshape(1, B)
    two = jnp.concatenate([grade_mine, shift(grade_mine, "core", 1)], axis=0)
    projected = jnp.dot(hidden, projection, preferred_element_type=jnp.float32).astype(jnp.bfloat16)
    grade_rows = jnp.broadcast_to(jnp.tile(grades.astype(jnp.bfloat16), 2), (4, 2, 16, PAIR))
    pairs = jnp.broadcast_to(projected.reshape(4, 1, PAIR, PAIR), (4, 2, PAIR, PAIR))
    sent = jnp.concatenate([pairs, grade_rows], axis=2).reshape(8, PAIR + 16, PAIR)
    came = lax.all_to_all(sent, COL, 0, 0, tiled=True)

    both = (pattern + pattern.T).astype(jnp.float32)
    row_here = ((y * 2 + zh) * 2 + core) * 8
    left_ids = jnp.stack([row_here + (x + d) % 4 * 2 + k for d in LEFT for k in (0, 1)])
    right_ids = jnp.stack(
        [((((y + d) % 4) * 2 + (zh ^ z)) * 2 + (core ^ c)) * 8 + col_here for d, z, c in RIGHT]
    )
    left_pick = (left_ids[:, None] == jnp.arange(128)[None]).astype(jnp.float32)
    right_pick = (jnp.arange(128)[:, None] == right_ids[None]).astype(jnp.float32)
    tiles = jnp.dot(
        jnp.dot(left_pick, both, preferred_element_type=jnp.float32), right_pick, preferred_element_type=jnp.float32
    ).reshape(4, 2, 4, 4)
    weight = jnp.repeat((tiles * (-smoothing_divisor / B)).transpose(2, 0, 1, 3), B, axis=3)
    place = jnp.stack([(x + d) % 4 for d in LEFT]).astype(jnp.int32)
    came, two, weight, place = lax.optimization_barrier((came, two, weight, place))

    rows = jnp.concatenate([came[k, :PAIR] for k in range(8)], axis=1).astype(jnp.float32)
    norms = jnp.sqrt(jnp.sum(rows * rows, axis=1) + epsilon)
    units = (rows / norms[:, None]).astype(jnp.bfloat16)
    unit = jnp.where(zl == 0, units[:B], units[B:])
    unit = jnp.concatenate([unit, jnp.pad(two, ((0, LONG - B - 2), (0, WIDTH - B)))], axis=0)
    own_norm = jnp.where(zl == 0, norms[:B], norms[B:])
    scaled = units * jnp.bfloat16(smoothing_divisor)
    turned = jnp.concatenate([-scaled[:, 1024:], scaled[:, :1024]], axis=1)

    left_grade = came[:, PAIR, :B].astype(jnp.float32).reshape(4, PAIR)
    twice = jnp.concatenate([left_grade, left_grade], axis=0)
    turned_grade = lax.dynamic_slice_in_dim(twice, x, 4, 0)
    left_grade = jnp.stack([turned_grade[d] for d in LEFT])[:, None]
    norm_high, norm_low = split_two(own_norm)
    extra = jnp.concatenate([norm_high, norm_low]).astype(jnp.float32)
    extra = jnp.broadcast_to(extra[None], (8, PAIR))

    below = shift(turned, "x", 1)
    above = shift(turned, "x", -1)
    y_below = shift(unit, "y", 1)
    y_above = shift(unit, "y", -1)
    unit_z = shift(unit, "zh", 1)
    y_below, y_above, unit_z, unit, left_grade, extra = lax.optimization_barrier(
        (y_below, y_above, unit_z, unit, left_grade, extra)
    )
    z_below = shift(unit_z, "y", 1)
    z_above = shift(unit_z, "y", -1)
    other = shift(jnp.concatenate([unit, unit_z], axis=0), "core", 1)
    y_both = jnp.concatenate([y_above, y_below], axis=0)
    below, above, y_below, z_above, z_below, y_above, y_both = lax.optimization_barrier(
        (below, above, y_below, z_above, z_below, y_above, y_both)
    )
    y_other = shift(y_both, "core", 1)
    z_other = shift(jnp.concatenate([z_above, z_below], axis=0), "core", 1)
    far0 = shift(below[:B], "x", 1)
    far1 = shift(above[B:], "x", -1)
    y_far = shift(y_below, "y", 1)
    z_far = shift(z_above, "y", -1)

    nearby = [unit, unit_z, y_above, y_below, z_above, z_below, other, y_other, z_other]
    near_grade = grade_quads(unit, unit_z, y_above, y_below, z_above, z_below)
    near_acc, near_inner = near_pass(
        weight, left_grade, near_grade, [turned, above, below] + nearby
    )
    y_far, z_far, far0, far1, near_acc, near_inner = lax.optimization_barrier(
        (y_far, z_far, far0, far1, near_acc, near_inner)
    )
    beyond = [y_far, z_far, shift(y_far, "core", 1), shift(z_far, "core", 1)]
    far_grade = grade_quads(y_far, z_far)
    sums = far_pass(
        place, weight, left_grade, near_grade, far_grade, extra, near_inner, near_acc,
        [turned, above, below, far0, far1] + nearby + beyond,
    )
    back = lax.all_to_all(sums, COL, 0, 0, tiled=True)

    grads, give, keep = weight_pass(core.astype(jnp.int32).reshape(1), back, projected, hidden)
    chip = (keep.astype(jnp.float32) + shift(give, "core", 1).astype(jnp.float32)).astype(jnp.bfloat16)
    gathered = lax.all_to_all(chip, ("y", "zh"), 0, 0, tiled=True)
    weight_grad = jnp.sum(gathered.astype(jnp.float32), axis=0)
    return grads, weight_grad


def solution(mesh):
    fine = Mesh(np.asarray(mesh.devices).reshape(SIZES), AXES)
    return jax.shard_map(
        shards,
        mesh=fine,
        in_specs=(P(ROW, None), P(None, COL), P(ROW + COL), P()),
        out_specs=(P(ROW, COL), P(ROW, COL)),
        check_vma=False,
    )
```

```python
import functools

import jax
import jax.numpy as jnp
import numpy as np
from jax import lax
from jax.experimental import pallas as pl
from jax.experimental.pallas import tpu as pltpu
from jax.sharding import Mesh, PartitionSpec as P

smoothing_divisor = 64.0
epsilon = 1e-06
AXES = ("y", "zh", "core", "x", "zl")
SIZES = (4, 2, 2, 4, 2)
ROW = ("y", "zh", "core")
COL = ("x", "zl")
B = 128
PAIR = 2 * B
QUAD = 4 * B
LONG = B + 16
WIDTH = 2048
ANY = pl.BlockSpec(memory_space=pltpu.HBM)
SMEM = pl.BlockSpec(memory_space=pltpu.SMEM)

RIGHT = ((0, 0, 0), (0, 1, 0), (1, 0, 0), (3, 0, 0), (1, 1, 0), (3, 1, 0), (0, 0, 1), (0, 1, 1))
RIGHT += ((1, 0, 1), (3, 0, 1), (1, 1, 1), (3, 1, 1), (2, 0, 0), (2, 1, 0), (2, 0, 1), (2, 1, 1))
SHARDS = ((0, 0), (0, 1), (3, 0), (3, 1), (1, 0), (1, 1), (2, 0), (2, 1))


def shift(value, axis, by):
    size = SIZES[AXES.index(axis)]
    return lax.ppermute(value, axis, [(i, (i + by) % size) for i in range(size)])


def whole(*shape):
    return pl.BlockSpec(shape, lambda *_: (0,) * len(shape))


def fetch(pieces, buffer, sem):
    row = 0
    for ref, first, rows in pieces:
        pltpu.make_async_copy(ref.at[pl.ds(first, rows)], buffer.at[pl.ds(row, rows)], sem).start()
        row += rows


def blocks(ref, first=0, count=1):
    return [(ref, k * LONG, B) for k in range(first, first + count)]


def fetch_left(spot_ref, shards, slot, buffer, sem):
    for k, ref in enumerate(shards):
        lanes = pl.ds(pl.multiple_of(spot_ref[k] * PAIR, PAIR), PAIR)
        pltpu.make_async_copy(ref.at[pl.ds(slot * PAIR, PAIR), :], buffer.at[slot, :, lanes], sem).start()


def filled(buffer, sem):
    pltpu.make_async_copy(buffer, buffer, sem).wait()


def columns(left_grade_ref, grade_cols, slots):
    for slot in slots:
        grade_cols[slot] = jnp.broadcast_to(left_grade_ref[slot], (B, PAIR)).T


def score(left, right, scores):
    scores[...] = lax.dot_general(left[...], right[...], (((1,), (1,)), ((), ())), preferred_element_type=jnp.float32)


def slope(scores, weight, grade_cols, right_grade, scale, slopes, inner, first):
    for part in range(4):
        rows = slice(part * 64, part * 64 + 64)
        here = grade_cols[rows, :]
        scaled = scale[rows, :]
        total = None
        for lane in range(4):
            lanes = slice(lane * B, lane * B + B)
            value = scores[rows, lanes] * scaled
            label = jnp.clip(here - right_grade[:, lanes], -1.0, 1.0)
            step = label * weight[part // 2 : part // 2 + 1, lanes]
            grown = jnp.exp(label * value)
            one = (step * pltpu.reciprocal(1.0 + grown, approx=True)).astype(jnp.bfloat16)
            slopes[rows, lanes] = one
            term = one.astype(jnp.float32) * value
            total = term if total is None else total + term
        inner[rows, :] = total if first else inner[rows, :] + total


def quad_rows(quad, count=1):
    return pl.ds(quad * QUAD, count * QUAD)


def pair_tiles(left_buf, right_buf, weight_ref, grade_cols, right_grade_ref, scale, scores, slopes, inner, first, begin, finish):
    def ahead(slot, quad):
        begin(slot, quad)
        score(left_buf.at[slot], right_buf.at[quad_rows(quad)], scores.at[slot % 2, :, quad_rows(quad)])

    def arithmetic(slot, quad):
        slope(
            scores.at[slot % 2, :, quad_rows(quad)], weight_ref.at[quad, slot], grade_cols.at[slot],
            right_grade_ref.at[quad], scale.at[slot], slopes.at[slot % 2, :, quad_rows(quad)], inner.at[slot],
            first and quad == 0,
        )

    ahead(0, 0)
    ahead(0, 1)
    for slot in range(4):
        arithmetic(slot, 0)
        if slot < 3:
            ahead(slot + 1, 0)
        arithmetic(slot, 1)
        if slot < 3:
            ahead(slot + 1, 1)
        finish(slot, slopes.at[slot % 2])


def near_kernel(spot_ref, weight_ref, left_grade_ref, right_grade_ref, *refs):
    shards = refs[:8]
    unit, unit_z, y_above, y_below, z_above, z_below, other = refs[8:15]
    rights = (
        blocks(unit) + blocks(unit_z) + blocks(y_above) + blocks(y_below),
        blocks(z_above) + blocks(z_below) + blocks(other, 0, 2),
    )
    acc_out, inner, scale, acc, left_buf, right_buf, grade_cols, scores, slopes, left_sem, right_sem, acc_sem = refs[15:]
    fetch_left(spot_ref, shards, 0, left_buf, left_sem.at[0])
    for k in range(2):
        fetch(rights[k], right_buf.at[quad_rows(k)], right_sem.at[k])
    for slot in (1, 2, 3):
        fetch_left(spot_ref, shards, slot, left_buf, left_sem.at[slot])
    columns(left_grade_ref, grade_cols, range(4))
    acc_copy = lambda slot: pltpu.make_async_copy(acc.at[slot], acc_out.at[slot], acc_sem.at[slot])

    def begin(slot, quad):
        if quad == 0:
            filled(left_buf.at[slot], left_sem.at[slot])
            squares = jnp.zeros((PAIR, B), jnp.float32)
            for chunk in range(16):
                part = left_buf[slot, :, chunk * B : (chunk + 1) * B].astype(jnp.float32)
                squares += part * part
            norm = jnp.sqrt(jnp.sum(squares, axis=1, keepdims=True) + epsilon)
            scale[slot] = jnp.broadcast_to(smoothing_divisor / norm, (PAIR, B))
        if slot == 0:
            filled(right_buf.at[quad_rows(quad)], right_sem.at[quad])

    def finish(slot, slopes_ref):
        for chunk in range(8):
            lanes = slice(chunk * PAIR, chunk * PAIR + PAIR)
            part = jnp.dot(slopes_ref[...], right_buf[:, lanes], preferred_element_type=jnp.float32)
            acc[slot, :, lanes] = part.astype(jnp.bfloat16)
        acc_copy(slot).start()

    pair_tiles(
        left_buf, right_buf, weight_ref, grade_cols, right_grade_ref, scale, scores, slopes, inner, True, begin, finish
    )
    for slot in range(4):
        acc_copy(slot).wait()


def far_kernel(spot_ref, weight_ref, left_grade_ref, right_grade_ref, extra_ref, scale, near_inner, near_acc, *refs):
    shards = refs[:8]
    y_other, z_other, y_far, z_far, y_far_other, z_far_other = refs[8:14]
    rights = (
        blocks(y_other, 0, 2) + blocks(z_other, 0, 2),
        blocks(y_far) + blocks(z_far) + blocks(y_far_other) + blocks(z_far_other),
    )
    out_ref, acc, inner, lines, sent, tail, left_buf, right_buf, grade_cols, scores, slopes = refs[14:25]
    left_sem, right_sem, acc_sem, sent_sem, tail_sem = refs[25:]
    acc_in = lambda k: pltpu.make_async_copy(near_acc.at[k], acc.at[k], acc_sem.at[k])
    fetch_left(spot_ref, shards, 0, left_buf, left_sem.at[0])
    for k in range(2):
        fetch(rights[k], right_buf.at[quad_rows(k)], right_sem.at[k])
    for slot in range(4):
        if slot > 0:
            fetch_left(spot_ref, shards, slot, left_buf, left_sem.at[slot])
        acc_in(slot).start()
    columns(left_grade_ref, grade_cols, range(4))
    inner[...] = near_inner[...]

    def home(slot):
        return pltpu.make_async_copy(sent.at[slot], out_ref.at[:, pl.ds(slot * PAIR, PAIR), :], sent_sem.at[slot])

    def begin(slot, quad):
        if quad == 0:
            filled(left_buf.at[slot], left_sem.at[slot])
        if slot == 0:
            filled(right_buf.at[quad_rows(quad)], right_sem.at[quad])

    def finish(slot, slopes_ref):
        acc_in(slot).wait()
        for chunk in range(8):
            source = (chunk + 4) % 8
            lanes = slice(source * PAIR, source * PAIR + PAIR)
            part = jnp.dot(slopes_ref[...], right_buf[:, lanes], preferred_element_type=jnp.float32)
            sent[slot, chunk] = (part + acc[slot, :, lanes].astype(jnp.float32)).astype(jnp.bfloat16)
        home(slot).start()
        lines[slot] = jnp.sum(inner[slot].T, axis=0, keepdims=True) * (1.0 / smoothing_divisor)

    pair_tiles(
        left_buf, right_buf, weight_ref, grade_cols, right_grade_ref, scale, scores, slopes, inner, False, begin, finish
    )
    total = jnp.concatenate([lines[k] for k in range(4)], axis=0)
    high = total.astype(jnp.bfloat16).astype(jnp.float32)
    last = jnp.concatenate([high, total - high, extra_ref[...]], axis=0).astype(jnp.bfloat16)
    for chunk in range(8):
        tail[chunk] = last
    tail_copy = pltpu.make_async_copy(tail, out_ref.at[:, pl.ds(1024, 16), :], tail_sem)
    tail_copy.start()
    for slot in range(4):
        home(slot).wait()
    tail_copy.wait()


BUFFERS = [
    pltpu.VMEM((4, PAIR, WIDTH), jnp.bfloat16),
    pltpu.VMEM((2 * QUAD, WIDTH), jnp.bfloat16),
    pltpu.VMEM((4, PAIR, B), jnp.float32),
    pltpu.VMEM((2, PAIR, 2 * QUAD), jnp.float32),
    pltpu.VMEM((2, PAIR, 2 * QUAD), jnp.bfloat16),
    pltpu.SemaphoreType.DMA((4,)),
    pltpu.SemaphoreType.DMA((2,)),
    pltpu.SemaphoreType.DMA((4,)),
]


def near_pass(spots, weight, left_grade, right_grade, arrays):
    rows = jax.ShapeDtypeStruct((4, PAIR, B), jnp.float32)
    return pl.pallas_call(
        near_kernel,
        in_specs=[SMEM] + [whole(*a.shape) for a in (weight, left_grade, right_grade)] + [ANY] * len(arrays),
        out_specs=[ANY, whole(4, PAIR, B), whole(4, PAIR, B)],
        out_shape=[jax.ShapeDtypeStruct((4, PAIR, WIDTH), jnp.bfloat16), rows, rows],
        scratch_shapes=[pltpu.VMEM((4, PAIR, WIDTH), jnp.bfloat16)] + BUFFERS,
        compiler_params=pltpu.CompilerParams(vmem_limit_bytes=60 * 2**20),
        cost_estimate=pl.CostEstimate(flops=9 * 10**9, bytes_accessed=16 * 2**20, transcendentals=2**21),
        name="near_tiles",
    )(spots, weight, left_grade, right_grade, *arrays)


def far_pass(spots, weight, left_grade, right_grade, extra, scale, near_inner, near_acc, arrays):
    return pl.pallas_call(
        far_kernel,
        in_specs=[SMEM]
        + [whole(*a.shape) for a in (weight, left_grade, right_grade, extra, scale, near_inner)]
        + [ANY]
        + [ANY] * len(arrays),
        out_specs=ANY,
        out_shape=jax.ShapeDtypeStruct((8, 1040, PAIR), jnp.bfloat16),
        scratch_shapes=[
            pltpu.VMEM((4, PAIR, WIDTH), jnp.bfloat16),
            pltpu.VMEM((4, PAIR, B), jnp.float32),
            pltpu.VMEM((4, 1, PAIR), jnp.float32),
            pltpu.VMEM((4, 8, PAIR, PAIR), jnp.bfloat16),
            pltpu.VMEM((8, 16, PAIR), jnp.bfloat16),
        ]
        + BUFFERS
        + [pltpu.SemaphoreType.DMA((4,)), pltpu.SemaphoreType.DMA],
        compiler_params=pltpu.CompilerParams(vmem_limit_bytes=60 * 2**20),
        cost_estimate=pl.CostEstimate(flops=8 * 10**9, bytes_accessed=24 * 2**20, transcendentals=2**21),
        name="far_tiles",
    )(spots, weight, left_grade, right_grade, extra, scale, near_inner, near_acc, *arrays)


def across(line, rows):
    column = jnp.broadcast_to(line, (B, rows)).T
    return jnp.concatenate([column, column], axis=1)


def weight_kernel(core_ref, back_ref, projected_ref, hidden_ref, grads_ref, give_ref, keep_ref, pre):
    @pl.when(pl.program_id(0) == 0)
    def _():
        tail = back_ref[:, 1024:, :].astype(jnp.float32)
        inner = jnp.sum(tail[:, 0:4] + tail[:, 4:8], axis=0)
        for part in range(8):
            at = pl.ds(part * B, B)
            grads = back_ref[0, at, :].astype(jnp.float32)
            for source in range(1, 8):
                grads += back_ref[source, at, :].astype(jnp.float32)
            grads_ref[at, :] = grads
            norm = across(tail[part, 8:9, :B] + tail[part, 8:9, B:], B)
            half = part % 2 * B
            product = across(inner[part // 2 : part // 2 + 1, half : half + B], B)
            unit = projected_ref[at, :].astype(jnp.float32) / norm
            pre[at, :] = ((grads - unit * product) / norm).astype(jnp.bfloat16)

    product = lax.dot_general(
        hidden_ref[...], pre[...], (((0,), (0,)), ((), ())), preferred_element_type=jnp.float32
    )
    core = core_ref[0]
    for k in range(2):
        even = product[2 * k * 224 : (2 * k + 1) * 224].astype(jnp.bfloat16)
        odd = product[(2 * k + 1) * 224 : (2 * k + 2) * 224].astype(jnp.bfloat16)
        mine = core == 0
        keep_ref[k] = jnp.where(mine, even, odd)
        give_ref[k] = jnp.where(mine, odd, even)


def weight_pass(core, back, projected, hidden):
    halves = pl.BlockSpec((2, 224, PAIR), lambda s: (s, 0, 0))
    return pl.pallas_call(
        weight_kernel,
        grid=(4,),
        in_specs=[
            SMEM,
            whole(8, 1040, PAIR),
            whole(1024, PAIR),
            pl.BlockSpec((1024, 896), lambda s: (0, s)),
        ],
        out_specs=[whole(1024, PAIR), halves, halves],
        out_shape=[
            jax.ShapeDtypeStruct((1024, PAIR), jnp.float32),
            jax.ShapeDtypeStruct((8, 224, PAIR), jnp.bfloat16),
            jax.ShapeDtypeStruct((8, 224, PAIR), jnp.bfloat16),
        ],
        scratch_shapes=[pltpu.VMEM((1024, PAIR), jnp.bfloat16)],
        compiler_params=pltpu.CompilerParams(vmem_limit_bytes=32 * 2**20),
        cost_estimate=pl.CostEstimate(flops=2 * 10**9, bytes_accessed=15 * 2**20, transcendentals=0),
        name="weight_terms",
    )(core, back, projected, hidden)


def split_two(values):
    high = values.astype(jnp.bfloat16)
    return high, (values - high.astype(jnp.float32)).astype(jnp.bfloat16)


def grade_lines(*arrays):
    lines = jnp.concatenate([a[B:, :B] for a in arrays], axis=0).astype(jnp.float32)
    lines = lines.reshape(len(arrays), LONG - B, B)
    return lines[:, 0], lines[:, 1]


def shards(hidden, projection, grades, pattern):
    y, zh, core, x, zl = (lax.axis_index(a) for a in AXES)
    col_here = x * 2 + zl

    grade_mine = grades.astype(jnp.bfloat16).reshape(1, B)
    two = jnp.concatenate([grade_mine, shift(grade_mine, "core", 1)], axis=0)
    projected = jnp.dot(hidden, projection, preferred_element_type=jnp.float32).astype(jnp.bfloat16)
    grade_rows = jnp.broadcast_to(jnp.tile(grade_mine, (1, 2)), (8, 16, PAIR))
    sent = jnp.concatenate([projected.reshape(8, B, PAIR), grade_rows], axis=1)
    came = lax.all_to_all(sent, COL, 0, 0, tiled=True)
    across_z = shift(projected, "zl", 1)
    below = shift(projected, "x", 1)
    above = shift(projected, "x", -1)

    both = (pattern + pattern.T).astype(jnp.float32)
    row_here = ((y * 2 + zh) * 2 + core) * 8
    home = lax.dynamic_slice_in_dim(both, row_here, 8, 0)
    right_ids = jnp.stack(
        [((((y + d) % 4) * 2 + (zh ^ z)) * 2 + (core ^ c)) * 8 + col_here for d, z, c in RIGHT]
    )
    right_pick = (jnp.arange(128)[:, None] == right_ids[None]).astype(jnp.float32)
    tiles = jnp.dot(home, right_pick, preferred_element_type=jnp.float32).reshape(4, 2, 4, 4)
    weight = jnp.repeat((tiles * (-smoothing_divisor / B)).transpose(2, 0, 1, 3), B, axis=3)
    spots = jnp.stack([((x + d) % 4 * 2 + (zl ^ z) + 4) % 8 for d, z in SHARDS]).astype(jnp.int32)
    came, across_z, below, above, two, weight, spots = lax.optimization_barrier(
        (came, across_z, below, above, two, weight, spots)
    )

    rows = jnp.concatenate([came[k, :B] for k in range(8)], axis=1).astype(jnp.float32)
    own_norm = jnp.sqrt(jnp.sum(rows * rows, axis=1) + epsilon)
    unit = (rows / own_norm[:, None]).astype(jnp.bfloat16)
    unit = jnp.concatenate([-unit[:, :1024], unit[:, 1024:]], axis=1)
    unit = jnp.concatenate([unit, jnp.pad(two, ((0, LONG - B - 2), (0, WIDTH - B)))], axis=0)
    left_grade = came[:, B, :B].astype(jnp.float32).reshape(4, 1, PAIR)
    norm_high, norm_low = split_two(own_norm)
    extra = jnp.concatenate([norm_high, norm_low]).astype(jnp.float32)
    extra = jnp.broadcast_to(extra[None], (8, PAIR))

    y_below = shift(unit, "y", 1)
    y_above = shift(unit, "y", -1)
    unit_z = shift(unit, "zh", 1)
    below_z = shift(across_z, "x", 1)
    above_z = shift(across_z, "x", -1)
    y_below, y_above, unit_z, unit, below, below_z, above_z, left_grade, extra = lax.optimization_barrier(
        (y_below, y_above, unit_z, unit, below, below_z, above_z, left_grade, extra)
    )
    z_below = shift(unit_z, "y", 1)
    z_above = shift(unit_z, "y", -1)
    far = shift(below, "x", 1)
    far_z = shift(above_z, "x", -1)
    other = shift(jnp.concatenate([unit, unit_z], axis=0), "core", 1)
    y_both = jnp.concatenate([y_above, y_below], axis=0)
    y_below, z_above, z_below, y_above, far, far_z, y_both = lax.optimization_barrier(
        (y_below, z_above, z_below, y_above, far, far_z, y_both)
    )
    y_far = shift(y_below, "y", 1)
    z_far = shift(z_above, "y", -1)
    y_other = shift(y_both, "core", 1)
    z_other = shift(jnp.concatenate([z_above, z_below], axis=0), "core", 1)

    left = [projected, across_z, below, below_z, above, above_z, far, far_z]
    nearby = [unit, unit_z, y_above, y_below, z_above, z_below]
    mine, others = grade_lines(*nearby)
    near_grade = jnp.concatenate([mine, others[:2]], axis=0).reshape(2, 1, QUAD)
    near_acc, near_inner, scale = near_pass(spots, weight[:2], left_grade, near_grade, left + nearby + [other])
    y_far, z_far, near_acc, near_inner = lax.optimization_barrier((y_far, z_far, near_acc, near_inner))
    far_mine, far_others = grade_lines(y_far, z_far)
    far_grade = jnp.concatenate([others[2:], far_mine, far_others], axis=0).reshape(2, 1, QUAD)
    beyond = [y_other, z_other, y_far, z_far, shift(y_far, "core", 1), shift(z_far, "core", 1)]
    sums = far_pass(
        spots, weight[2:], left_grade, far_grade, extra, scale, near_inner, near_acc, left + beyond
    )
    back = lax.all_to_all(sums, COL, 0, 0, tiled=True)

    grads, give, keep = weight_pass(core.astype(jnp.int32).reshape(1), back, projected, hidden)
    chip = (keep.astype(jnp.float32) + shift(give, "core", 1).astype(jnp.float32)).astype(jnp.bfloat16)
    gathered = lax.all_to_all(chip, ("y", "zh"), 0, 0, tiled=True)
    weight_grad = jnp.sum(gathered.astype(jnp.float32), axis=0)
    return grads, weight_grad


def solution(mesh):
    fine = Mesh(np.asarray(mesh.devices).reshape(SIZES), AXES)
    return jax.shard_map(
        shards,
        mesh=fine,
        in_specs=(P(ROW, None), P(None, COL), P(ROW + COL), P()),
        out_specs=(P(ROW, COL), P(ROW, COL)),
        check_vma=False,
    )
```

```python
import functools

import jax
import jax.numpy as jnp
import numpy as np
from jax import lax
from jax.experimental import pallas as pl
from jax.experimental.pallas import tpu as pltpu
from jax.sharding import Mesh, PartitionSpec as P

smoothing_divisor = 64.0
epsilon = 1e-06
AXES = ("y", "zh", "core", "x", "zl")
SIZES = (4, 2, 2, 4, 2)
ROW = ("y", "zh", "core")
COL = ("x", "zl")
B = 128
PAIR = 2 * B
QUAD = 4 * B
LONG = B + 16
WIDTH = 2048
ANY = pl.BlockSpec(memory_space=pltpu.HBM)
SMEM = pl.BlockSpec(memory_space=pltpu.SMEM)

RIGHT = ((0, 0, 0), (0, 1, 0), (1, 0, 0), (3, 0, 0), (1, 1, 0), (3, 1, 0), (0, 0, 1), (0, 1, 1))
RIGHT += ((1, 0, 1), (3, 0, 1), (1, 1, 1), (3, 1, 1), (2, 0, 0), (2, 1, 0), (2, 0, 1), (2, 1, 1))
SHARDS = ((0, 0), (0, 1), (3, 0), (3, 1), (1, 0), (1, 1), (2, 0), (2, 1))


def shift(value, axis, by):
    size = SIZES[AXES.index(axis)]
    return lax.ppermute(value, axis, [(i, (i + by) % size) for i in range(size)])


def whole(*shape):
    return pl.BlockSpec(shape, lambda *_: (0,) * len(shape))


def fetch(pieces, buffer, sem):
    row = 0
    for ref, first, rows in pieces:
        pltpu.make_async_copy(ref.at[pl.ds(first, rows)], buffer.at[pl.ds(row, rows)], sem).start()
        row += rows


def blocks(ref, first=0, count=1):
    return [(ref, k * LONG, B) for k in range(first, first + count)]


def fetch_left(spot_ref, shards, slot, buffer, sem):
    for k, ref in enumerate(shards):
        lanes = pl.ds(pl.multiple_of(spot_ref[k] * PAIR, PAIR), PAIR)
        pltpu.make_async_copy(ref.at[pl.ds(slot * PAIR, PAIR), :], buffer.at[slot, :, lanes], sem).start()


def filled(buffer, sem):
    pltpu.make_async_copy(buffer, buffer, sem).wait()


def columns(left_grade_ref, grade_cols, slots):
    for slot in slots:
        grade_cols[slot] = jnp.broadcast_to(left_grade_ref[slot], (B, PAIR)).T


def score(left, right, scores):
    scores[...] = lax.dot_general(left[...], right[...], (((1,), (1,)), ((), ())), preferred_element_type=jnp.float32)


def slope(scores, weight, grade_cols, right_grade, scale, slopes, inner, first):
    for part in range(4):
        rows = slice(part * 64, part * 64 + 64)
        here = grade_cols[rows, :]
        scaled = scale[rows, :]
        total = None
        for lane in range(4):
            lanes = slice(lane * B, lane * B + B)
            value = scores[rows, lanes] * scaled
            label = jnp.clip(here - right_grade[:, lanes], -1.0, 1.0)
            step = label * weight[part // 2 : part // 2 + 1, lanes]
            grown = jnp.exp(label * value)
            one = (step * pltpu.reciprocal(1.0 + grown, approx=True)).astype(jnp.bfloat16)
            slopes[rows, lanes] = one
            term = one.astype(jnp.float32) * value
            total = term if total is None else total + term
        inner[rows, :] = total if first else inner[rows, :] + total


def quad_rows(quad, count=1):
    return pl.ds(quad * QUAD, count * QUAD)


def pair_tiles(left_buf, right_buf, weight_ref, grade_cols, right_grade_ref, scale, scores, slopes, inner, first, begin, finish):
    def ahead(slot, quad):
        begin(slot, quad)
        score(left_buf.at[slot], right_buf.at[quad_rows(quad)], scores.at[slot % 2, :, quad_rows(quad)])

    def arithmetic(slot, quad):
        slope(
            scores.at[slot % 2, :, quad_rows(quad)], weight_ref.at[quad, slot], grade_cols.at[slot],
            right_grade_ref.at[quad], scale.at[slot], slopes.at[slot % 2, :, quad_rows(quad)], inner.at[slot],
            first and quad == 0,
        )

    ahead(0, 0)
    ahead(0, 1)
    for slot in range(4):
        arithmetic(slot, 0)
        if slot < 3:
            ahead(slot + 1, 0)
        arithmetic(slot, 1)
        if slot < 3:
            ahead(slot + 1, 1)
        finish(slot, slopes.at[slot % 2])


def near_kernel(spot_ref, weight_ref, left_grade_ref, right_grade_ref, *refs):
    shards = refs[:8]
    unit, unit_z, y_above, y_below, z_above, z_below, other = refs[8:15]
    rights = (
        blocks(unit) + blocks(unit_z) + blocks(y_above) + blocks(y_below),
        blocks(z_above) + blocks(z_below) + blocks(other, 0, 2),
    )
    acc_out, inner, scale, acc, left_buf, right_buf, grade_cols, scores, slopes, left_sem, right_sem, acc_sem = refs[15:]
    fetch_left(spot_ref, shards, 0, left_buf, left_sem.at[0])
    for k in range(2):
        fetch(rights[k], right_buf.at[quad_rows(k)], right_sem.at[k])
    for slot in (1, 2, 3):
        fetch_left(spot_ref, shards, slot, left_buf, left_sem.at[slot])
    columns(left_grade_ref, grade_cols, range(4))
    acc_copy = lambda slot: pltpu.make_async_copy(acc.at[slot], acc_out.at[slot], acc_sem.at[slot])

    def begin(slot, quad):
        if quad == 0:
            filled(left_buf.at[slot], left_sem.at[slot])
            squares = jnp.zeros((PAIR, B), jnp.float32)
            for chunk in range(16):
                part = left_buf[slot, :, chunk * B : (chunk + 1) * B].astype(jnp.float32)
                squares += part * part
            norm = jnp.sqrt(jnp.sum(squares, axis=1, keepdims=True) + epsilon)
            scale[slot] = jnp.broadcast_to(smoothing_divisor / norm, (PAIR, B))
        if slot == 0:
            filled(right_buf.at[quad_rows(quad)], right_sem.at[quad])

    def finish(slot, slopes_ref):
        for chunk in range(8):
            lanes = slice(chunk * PAIR, chunk * PAIR + PAIR)
            part = jnp.dot(slopes_ref[...], right_buf[:, lanes], preferred_element_type=jnp.float32)
            acc[slot, :, lanes] = part.astype(jnp.bfloat16)
        acc_copy(slot).start()

    pair_tiles(
        left_buf, right_buf, weight_ref, grade_cols, right_grade_ref, scale, scores, slopes, inner, True, begin, finish
    )
    for slot in range(4):
        acc_copy(slot).wait()


def far_kernel(spot_ref, weight_ref, left_grade_ref, right_grade_ref, extra_ref, scale, near_inner, near_acc, *refs):
    shards = refs[:8]
    y_other, z_other, y_far, z_far, y_far_other, z_far_other = refs[8:14]
    rights = (
        blocks(y_other, 0, 2) + blocks(z_other, 0, 2),
        blocks(y_far) + blocks(z_far) + blocks(y_far_other) + blocks(z_far_other),
    )
    out_ref, acc, inner, lines, sent, tail, left_buf, right_buf, grade_cols, scores, slopes = refs[14:25]
    left_sem, right_sem, acc_sem, sent_sem, tail_sem = refs[25:]
    acc_in = lambda k: pltpu.make_async_copy(near_acc.at[k], acc.at[k], acc_sem.at[k])
    fetch_left(spot_ref, shards, 0, left_buf, left_sem.at[0])
    for k in range(2):
        fetch(rights[k], right_buf.at[quad_rows(k)], right_sem.at[k])
    for slot in range(4):
        if slot > 0:
            fetch_left(spot_ref, shards, slot, left_buf, left_sem.at[slot])
        acc_in(slot).start()
    columns(left_grade_ref, grade_cols, range(4))
    inner[...] = near_inner[...]

    def home(slot):
        return pltpu.make_async_copy(sent.at[slot], out_ref.at[:, pl.ds(slot * PAIR, PAIR), :], sent_sem.at[slot])

    def begin(slot, quad):
        if quad == 0:
            filled(left_buf.at[slot], left_sem.at[slot])
        if slot == 0:
            filled(right_buf.at[quad_rows(quad)], right_sem.at[quad])

    def finish(slot, slopes_ref):
        acc_in(slot).wait()
        for chunk in range(8):
            source = (chunk + 4) % 8
            lanes = slice(source * PAIR, source * PAIR + PAIR)
            part = jnp.dot(slopes_ref[...], right_buf[:, lanes], preferred_element_type=jnp.float32)
            sent[slot, chunk] = (part + acc[slot, :, lanes].astype(jnp.float32)).astype(jnp.bfloat16)
        home(slot).start()
        lines[slot] = jnp.sum(inner[slot].T, axis=0, keepdims=True) * (1.0 / smoothing_divisor)

    pair_tiles(
        left_buf, right_buf, weight_ref, grade_cols, right_grade_ref, scale, scores, slopes, inner, False, begin, finish
    )
    total = jnp.concatenate([lines[k] for k in range(4)], axis=0)
    high = total.astype(jnp.bfloat16).astype(jnp.float32)
    last = jnp.concatenate([high, total - high, extra_ref[...]], axis=0).astype(jnp.bfloat16)
    for chunk in range(8):
        tail[chunk] = last
    tail_copy = pltpu.make_async_copy(tail, out_ref.at[:, pl.ds(1024, 16), :], tail_sem)
    tail_copy.start()
    for slot in range(4):
        home(slot).wait()
    tail_copy.wait()


BUFFERS = [
    pltpu.VMEM((4, PAIR, WIDTH), jnp.bfloat16),
    pltpu.VMEM((2 * QUAD, WIDTH), jnp.bfloat16),
    pltpu.VMEM((4, PAIR, B), jnp.float32),
    pltpu.VMEM((2, PAIR, 2 * QUAD), jnp.float32),
    pltpu.VMEM((2, PAIR, 2 * QUAD), jnp.bfloat16),
    pltpu.SemaphoreType.DMA((4,)),
    pltpu.SemaphoreType.DMA((2,)),
    pltpu.SemaphoreType.DMA((4,)),
]


def near_pass(spots, weight, left_grade, right_grade, arrays):
    rows = jax.ShapeDtypeStruct((4, PAIR, B), jnp.float32)
    return pl.pallas_call(
        near_kernel,
        in_specs=[SMEM] + [whole(*a.shape) for a in (weight, left_grade, right_grade)] + [ANY] * len(arrays),
        out_specs=[ANY, whole(4, PAIR, B), whole(4, PAIR, B)],
        out_shape=[jax.ShapeDtypeStruct((4, PAIR, WIDTH), jnp.bfloat16), rows, rows],
        scratch_shapes=[pltpu.VMEM((4, PAIR, WIDTH), jnp.bfloat16)] + BUFFERS,
        compiler_params=pltpu.CompilerParams(vmem_limit_bytes=20 * 2**20),
        cost_estimate=pl.CostEstimate(flops=9 * 10**9, bytes_accessed=16 * 2**20, transcendentals=2**21),
        name="near_tiles",
    )(spots, weight, left_grade, right_grade, *arrays)


def far_pass(spots, weight, left_grade, right_grade, extra, scale, near_inner, near_acc, arrays):
    return pl.pallas_call(
        far_kernel,
        in_specs=[SMEM]
        + [whole(*a.shape) for a in (weight, left_grade, right_grade, extra, scale, near_inner)]
        + [ANY]
        + [ANY] * len(arrays),
        out_specs=ANY,
        out_shape=jax.ShapeDtypeStruct((8, 1040, PAIR), jnp.bfloat16),
        scratch_shapes=[
            pltpu.VMEM((4, PAIR, WIDTH), jnp.bfloat16),
            pltpu.VMEM((4, PAIR, B), jnp.float32),
            pltpu.VMEM((4, 1, PAIR), jnp.float32),
            pltpu.VMEM((4, 8, PAIR, PAIR), jnp.bfloat16),
            pltpu.VMEM((8, 16, PAIR), jnp.bfloat16),
        ]
        + BUFFERS
        + [pltpu.SemaphoreType.DMA((4,)), pltpu.SemaphoreType.DMA],
        compiler_params=pltpu.CompilerParams(vmem_limit_bytes=24 * 2**20),
        cost_estimate=pl.CostEstimate(flops=8 * 10**9, bytes_accessed=24 * 2**20, transcendentals=2**21),
        name="far_tiles",
    )(spots, weight, left_grade, right_grade, extra, scale, near_inner, near_acc, *arrays)


def across(line, rows):
    column = jnp.broadcast_to(line, (B, rows)).T
    return jnp.concatenate([column, column], axis=1)


def weight_kernel(core_ref, back_ref, projected_ref, hidden_ref, grads_ref, give_ref, keep_ref, pre):
    @pl.when(pl.program_id(0) == 0)
    def _():
        tail = back_ref[:, 1024:, :].astype(jnp.float32)
        inner = jnp.sum(tail[:, 0:4] + tail[:, 4:8], axis=0)
        for part in range(8):
            at = pl.ds(part * B, B)
            grads = back_ref[0, at, :].astype(jnp.float32)
            for source in range(1, 8):
                grads += back_ref[source, at, :].astype(jnp.float32)
            grads_ref[at, :] = grads
            norm = across(tail[part, 8:9, :B] + tail[part, 8:9, B:], B)
            half = part % 2 * B
            product = across(inner[part // 2 : part // 2 + 1, half : half + B], B)
            unit = projected_ref[at, :].astype(jnp.float32) / norm
            pre[at, :] = ((grads - unit * product) / norm).astype(jnp.bfloat16)

    product = lax.dot_general(
        hidden_ref[...], pre[...], (((0,), (0,)), ((), ())), preferred_element_type=jnp.float32
    )
    core = core_ref[0]
    for k in range(2):
        even = product[2 * k * 224 : (2 * k + 1) * 224].astype(jnp.bfloat16)
        odd = product[(2 * k + 1) * 224 : (2 * k + 2) * 224].astype(jnp.bfloat16)
        mine = core == 0
        keep_ref[k] = jnp.where(mine, even, odd)
        give_ref[k] = jnp.where(mine, odd, even)


def weight_pass(core, back, projected, hidden):
    halves = pl.BlockSpec((2, 224, PAIR), lambda s: (s, 0, 0))
    return pl.pallas_call(
        weight_kernel,
        grid=(4,),
        in_specs=[
            SMEM,
            whole(8, 1040, PAIR),
            whole(1024, PAIR),
            pl.BlockSpec((1024, 896), lambda s: (0, s)),
        ],
        out_specs=[whole(1024, PAIR), halves, halves],
        out_shape=[
            jax.ShapeDtypeStruct((1024, PAIR), jnp.float32),
            jax.ShapeDtypeStruct((8, 224, PAIR), jnp.bfloat16),
            jax.ShapeDtypeStruct((8, 224, PAIR), jnp.bfloat16),
        ],
        scratch_shapes=[pltpu.VMEM((1024, PAIR), jnp.bfloat16)],
        compiler_params=pltpu.CompilerParams(vmem_limit_bytes=32 * 2**20),
        cost_estimate=pl.CostEstimate(flops=2 * 10**9, bytes_accessed=15 * 2**20, transcendentals=0),
        name="weight_terms",
    )(core, back, projected, hidden)


def split_two(values):
    high = values.astype(jnp.bfloat16)
    return high, (values - high.astype(jnp.float32)).astype(jnp.bfloat16)


def grade_lines(*arrays):
    lines = jnp.concatenate([a[B:, :B] for a in arrays], axis=0).astype(jnp.float32)
    lines = lines.reshape(len(arrays), LONG - B, B)
    return lines[:, 0], lines[:, 1]


def shards(hidden, projection, grades, pattern):
    y, zh, core, x, zl = (lax.axis_index(a) for a in AXES)
    col_here = x * 2 + zl

    grade_mine = grades.astype(jnp.bfloat16).reshape(1, B)
    two = jnp.concatenate([grade_mine, shift(grade_mine, "core", 1)], axis=0)
    projected = jnp.dot(hidden, projection, preferred_element_type=jnp.float32).astype(jnp.bfloat16)
    grade_rows = jnp.broadcast_to(jnp.tile(grade_mine, (1, 2)), (8, 16, PAIR))
    sent = jnp.concatenate([projected.reshape(8, B, PAIR), grade_rows], axis=1)
    came = lax.all_to_all(sent, COL, 0, 0, tiled=True)
    across_z = shift(projected, "zl", 1)
    below = shift(projected, "x", 1)
    above = shift(projected, "x", -1)

    both = (pattern + pattern.T).astype(jnp.float32)
    row_here = ((y * 2 + zh) * 2 + core) * 8
    home = lax.dynamic_slice_in_dim(both, row_here, 8, 0)
    right_ids = jnp.stack(
        [((((y + d) % 4) * 2 + (zh ^ z)) * 2 + (core ^ c)) * 8 + col_here for d, z, c in RIGHT]
    )
    right_pick = (jnp.arange(128)[:, None] == right_ids[None]).astype(jnp.float32)
    tiles = jnp.dot(home, right_pick, preferred_element_type=jnp.float32).reshape(4, 2, 4, 4)
    weight = jnp.repeat((tiles * (-smoothing_divisor / B)).transpose(2, 0, 1, 3), B, axis=3)
    spots = jnp.stack([((x + d) % 4 * 2 + (zl ^ z) + 4) % 8 for d, z in SHARDS]).astype(jnp.int32)
    came, across_z, below, above, two, weight, spots = lax.optimization_barrier(
        (came, across_z, below, above, two, weight, spots)
    )

    rows = jnp.concatenate([came[k, :B] for k in range(8)], axis=1).astype(jnp.float32)
    own_norm = jnp.sqrt(jnp.sum(rows * rows, axis=1) + epsilon)
    unit = (rows / own_norm[:, None]).astype(jnp.bfloat16)
    unit = jnp.concatenate([-unit[:, :1024], unit[:, 1024:]], axis=1)
    unit = jnp.concatenate([unit, jnp.pad(two, ((0, LONG - B - 2), (0, WIDTH - B)))], axis=0)
    left_grade = came[:, B, :B].astype(jnp.float32).reshape(4, 1, PAIR)
    norm_high, norm_low = split_two(own_norm)
    extra = jnp.concatenate([norm_high, norm_low]).astype(jnp.float32)
    extra = jnp.broadcast_to(extra[None], (8, PAIR))

    y_below = shift(unit, "y", 1)
    y_above = shift(unit, "y", -1)
    unit_z = shift(unit, "zh", 1)
    below_z = shift(across_z, "x", 1)
    above_z = shift(across_z, "x", -1)
    y_below, y_above, unit_z, unit, below, below_z, above_z, left_grade, extra = lax.optimization_barrier(
        (y_below, y_above, unit_z, unit, below, below_z, above_z, left_grade, extra)
    )
    z_below = shift(unit_z, "y", 1)
    z_above = shift(unit_z, "y", -1)
    far = shift(below, "x", 1)
    far_z = shift(above_z, "x", -1)
    other = shift(jnp.concatenate([unit, unit_z], axis=0), "core", 1)
    y_both = jnp.concatenate([y_above, y_below], axis=0)
    y_below, z_above, z_below, y_above, far, far_z, y_both = lax.optimization_barrier(
        (y_below, z_above, z_below, y_above, far, far_z, y_both)
    )
    y_far = shift(y_below, "y", 1)
    z_far = shift(z_above, "y", -1)
    y_other = shift(y_both, "core", 1)
    z_other = shift(jnp.concatenate([z_above, z_below], axis=0), "core", 1)

    left = [projected, across_z, below, below_z, above, above_z, far, far_z]
    nearby = [unit, unit_z, y_above, y_below, z_above, z_below]
    mine, others = grade_lines(*nearby)
    near_grade = jnp.concatenate([mine, others[:2]], axis=0).reshape(2, 1, QUAD)
    near_acc, near_inner, scale = near_pass(spots, weight[:2], left_grade, near_grade, left + nearby + [other])
    y_far, z_far, near_acc, near_inner = lax.optimization_barrier((y_far, z_far, near_acc, near_inner))
    far_mine, far_others = grade_lines(y_far, z_far)
    far_grade = jnp.concatenate([others[2:], far_mine, far_others], axis=0).reshape(2, 1, QUAD)
    beyond = [y_other, z_other, y_far, z_far, shift(y_far, "core", 1), shift(z_far, "core", 1)]
    sums = far_pass(
        spots, weight[2:], left_grade, far_grade, extra, scale, near_inner, near_acc, left + beyond
    )
    back = lax.all_to_all(sums, COL, 0, 0, tiled=True)

    grads, give, keep = weight_pass(core.astype(jnp.int32).reshape(1), back, projected, hidden)
    chip = (keep.astype(jnp.float32) + shift(give, "core", 1).astype(jnp.float32)).astype(jnp.bfloat16)
    gathered = lax.all_to_all(chip, ("y", "zh"), 0, 0, tiled=True)
    weight_grad = jnp.sum(gathered.astype(jnp.float32), axis=0)
    return grads, weight_grad


def solution(mesh):
    fine = Mesh(np.asarray(mesh.devices).reshape(SIZES), AXES)
    return jax.shard_map(
        shards,
        mesh=fine,
        in_specs=(P(ROW, None), P(None, COL), P(ROW + COL), P()),
        out_specs=(P(ROW, COL), P(ROW, COL)),
        check_vma=False,
    )
```

```python
import functools

import jax
import jax.numpy as jnp
import numpy as np
from jax import lax
from jax.experimental import pallas as pl
from jax.experimental.pallas import tpu as pltpu
from jax.sharding import Mesh, PartitionSpec as P

smoothing_divisor = 64.0
epsilon = 1e-06
AXES = ("y", "zh", "core", "x", "zl")
SIZES = (4, 2, 2, 4, 2)
ROW = ("y", "zh", "core")
COL = ("x", "zl")
B = 128
PAIR = 2 * B
QUAD = 4 * B
LONG = B + 16
WIDTH = 2048
ANY = pl.BlockSpec(memory_space=pltpu.HBM)
SMEM = pl.BlockSpec(memory_space=pltpu.SMEM)

RIGHT = ((0, 0, 0), (0, 1, 0), (1, 0, 0), (3, 0, 0), (1, 1, 0), (3, 1, 0), (0, 0, 1), (0, 1, 1))
RIGHT += ((1, 0, 1), (3, 0, 1), (1, 1, 1), (3, 1, 1), (2, 0, 0), (2, 1, 0), (2, 0, 1), (2, 1, 1))
SHARDS = ((0, 0), (0, 1), (3, 0), (3, 1), (1, 0), (1, 1), (2, 0), (2, 1))


def shift(value, axis, by):
    size = SIZES[AXES.index(axis)]
    return lax.ppermute(value, axis, [(i, (i + by) % size) for i in range(size)])


def whole(*shape):
    return pl.BlockSpec(shape, lambda *_: (0,) * len(shape))


def fetch(pieces, buffer, sem):
    row = 0
    for ref, first, rows in pieces:
        pltpu.make_async_copy(ref.at[pl.ds(first, rows)], buffer.at[pl.ds(row, rows)], sem).start()
        row += rows


def blocks(ref, first=0, count=1):
    return [(ref, k * LONG, B) for k in range(first, first + count)]


def fetch_right(rights, right_buf, right_sem, grade_rows, grade_sem):
    for k, pieces in enumerate(rights):
        fetch(pieces, right_buf.at[quad_rows(k)], right_sem.at[k])
        for j, (ref, first, rows) in enumerate(pieces):
            grades = ref.at[pl.ds(first + rows, LONG - B), pl.ds(0, B)]
            pltpu.make_async_copy(grades, grade_rows.at[k * 4 + j], grade_sem).start()


def right_grades(grade_rows, grade_sem, right_grade):
    filled(grade_rows, grade_sem)
    for k in range(8):
        lanes = slice(k % 4 * B, k % 4 * B + B)
        right_grade[k // 4, :, lanes] = grade_rows[k].astype(jnp.float32)[0:1]


def fetch_left(spot_ref, shards, slot, buffer, sem):
    for k, ref in enumerate(shards):
        lanes = pl.ds(pl.multiple_of(spot_ref[k] * PAIR, PAIR), PAIR)
        pltpu.make_async_copy(ref.at[pl.ds(slot * PAIR, PAIR), :], buffer.at[slot, :, lanes], sem).start()


def filled(buffer, sem):
    pltpu.make_async_copy(buffer, buffer, sem).wait()


def columns(left_grade_ref, grade_cols, slots):
    for slot in slots:
        grade_cols[slot] = jnp.broadcast_to(left_grade_ref[slot], (B, PAIR)).T


def score(left, right, scores):
    scores[...] = lax.dot_general(left[...], right[...], (((1,), (1,)), ((), ())), preferred_element_type=jnp.float32)


def slope(scores, weight, grade_cols, right_grade, scale, slopes, inner, first):
    for part in range(4):
        rows = slice(part * 64, part * 64 + 64)
        here = grade_cols[rows, :]
        scaled = scale[rows, :]
        total = None
        for lane in range(4):
            lanes = slice(lane * B, lane * B + B)
            value = scores[rows, lanes] * scaled
            label = jnp.clip(here - right_grade[:, lanes], -1.0, 1.0)
            step = label * weight[part // 2 : part // 2 + 1, lanes]
            grown = jnp.exp(label * value)
            one = (step * pltpu.reciprocal(1.0 + grown, approx=True)).astype(jnp.bfloat16)
            slopes[rows, lanes] = one
            term = one.astype(jnp.float32) * value
            total = term if total is None else total + term
        inner[rows, :] = total if first else inner[rows, :] + total


def quad_rows(quad, count=1):
    return pl.ds(quad * QUAD, count * QUAD)


def pair_tiles(left_buf, right_buf, weight_ref, grade_cols, right_grade_ref, scale, scores, slopes, inner, first, begin, finish):
    def ahead(slot, quad):
        begin(slot, quad)
        score(left_buf.at[slot], right_buf.at[quad_rows(quad)], scores.at[slot % 2, :, quad_rows(quad)])

    def arithmetic(slot, quad):
        slope(
            scores.at[slot % 2, :, quad_rows(quad)], weight_ref.at[quad, slot], grade_cols.at[slot],
            right_grade_ref.at[quad], scale.at[slot], slopes.at[slot % 2, :, quad_rows(quad)], inner.at[slot],
            first and quad == 0,
        )

    ahead(0, 0)
    ahead(0, 1)
    for slot in range(4):
        arithmetic(slot, 0)
        if slot < 3:
            ahead(slot + 1, 0)
        arithmetic(slot, 1)
        if slot < 3:
            ahead(slot + 1, 1)
        finish(slot, slopes.at[slot % 2])


def near_kernel(spot_ref, weight_ref, left_grade_ref, *refs):
    shards = refs[:8]
    unit, unit_z, y_above, y_below, z_above, z_below, other = refs[8:15]
    rights = (
        blocks(unit) + blocks(unit_z) + blocks(y_above) + blocks(y_below),
        blocks(z_above) + blocks(z_below) + blocks(other, 0, 2),
    )
    acc_out, inner, scale, acc, left_buf, right_buf, grade_cols, scores, slopes = refs[15:24]
    grade_rows, right_grade_ref, left_sem, right_sem, acc_sem, grade_sem = refs[24:]
    fetch_left(spot_ref, shards, 0, left_buf, left_sem.at[0])
    fetch_right(rights, right_buf, right_sem, grade_rows, grade_sem)
    for slot in (1, 2, 3):
        fetch_left(spot_ref, shards, slot, left_buf, left_sem.at[slot])
    columns(left_grade_ref, grade_cols, range(4))
    right_grades(grade_rows, grade_sem, right_grade_ref)
    acc_copy = lambda slot: pltpu.make_async_copy(acc.at[slot], acc_out.at[slot], acc_sem.at[slot])

    def begin(slot, quad):
        if quad == 0:
            filled(left_buf.at[slot], left_sem.at[slot])
            squares = jnp.zeros((PAIR, B), jnp.float32)
            for chunk in range(16):
                part = left_buf[slot, :, chunk * B : (chunk + 1) * B].astype(jnp.float32)
                squares += part * part
            norm = jnp.sqrt(jnp.sum(squares, axis=1, keepdims=True) + epsilon)
            scale[slot] = jnp.broadcast_to(smoothing_divisor / norm, (PAIR, B))
        if slot == 0:
            filled(right_buf.at[quad_rows(quad)], right_sem.at[quad])

    def finish(slot, slopes_ref):
        for chunk in range(8):
            lanes = slice(chunk * PAIR, chunk * PAIR + PAIR)
            part = jnp.dot(slopes_ref[...], right_buf[:, lanes], preferred_element_type=jnp.float32)
            acc[slot, :, lanes] = part.astype(jnp.bfloat16)
        acc_copy(slot).start()

    pair_tiles(
        left_buf, right_buf, weight_ref, grade_cols, right_grade_ref, scale, scores, slopes, inner, True, begin, finish
    )
    for slot in range(4):
        acc_copy(slot).wait()


def far_kernel(spot_ref, weight_ref, left_grade_ref, extra_ref, scale, near_inner, near_acc, *refs):
    shards = refs[:8]
    y_other, z_other, y_far, z_far, y_far_other, z_far_other = refs[8:14]
    rights = (
        blocks(y_other, 0, 2) + blocks(z_other, 0, 2),
        blocks(y_far) + blocks(z_far) + blocks(y_far_other) + blocks(z_far_other),
    )
    out_ref, acc, inner, lines, sent, tail, left_buf, right_buf, grade_cols, scores, slopes = refs[14:25]
    grade_rows, right_grade_ref, left_sem, right_sem, acc_sem, grade_sem, sent_sem, tail_sem = refs[25:]
    acc_in = lambda k: pltpu.make_async_copy(near_acc.at[k], acc.at[k], acc_sem.at[k])
    fetch_left(spot_ref, shards, 0, left_buf, left_sem.at[0])
    fetch_right(rights, right_buf, right_sem, grade_rows, grade_sem)
    for slot in range(4):
        if slot > 0:
            fetch_left(spot_ref, shards, slot, left_buf, left_sem.at[slot])
        acc_in(slot).start()
    columns(left_grade_ref, grade_cols, range(4))
    right_grades(grade_rows, grade_sem, right_grade_ref)
    inner[...] = near_inner[...]

    def home(slot):
        return pltpu.make_async_copy(sent.at[slot], out_ref.at[:, pl.ds(slot * PAIR, PAIR), :], sent_sem.at[slot])

    def begin(slot, quad):
        if quad == 0:
            filled(left_buf.at[slot], left_sem.at[slot])
        if slot == 0:
            filled(right_buf.at[quad_rows(quad)], right_sem.at[quad])

    def finish(slot, slopes_ref):
        acc_in(slot).wait()
        for chunk in range(8):
            source = (chunk + 4) % 8
            lanes = slice(source * PAIR, source * PAIR + PAIR)
            part = jnp.dot(slopes_ref[...], right_buf[:, lanes], preferred_element_type=jnp.float32)
            sent[slot, chunk] = (part + acc[slot, :, lanes].astype(jnp.float32)).astype(jnp.bfloat16)
        home(slot).start()
        lines[slot] = jnp.sum(inner[slot].T, axis=0, keepdims=True) * (1.0 / smoothing_divisor)

    pair_tiles(
        left_buf, right_buf, weight_ref, grade_cols, right_grade_ref, scale, scores, slopes, inner, False, begin, finish
    )
    total = jnp.concatenate([lines[k] for k in range(4)], axis=0)
    high = total.astype(jnp.bfloat16).astype(jnp.float32)
    last = jnp.concatenate([high, total - high, extra_ref[...]], axis=0).astype(jnp.bfloat16)
    for chunk in range(8):
        tail[chunk] = last
    tail_copy = pltpu.make_async_copy(tail, out_ref.at[:, pl.ds(1024, 16), :], tail_sem)
    tail_copy.start()
    for slot in range(4):
        home(slot).wait()
    tail_copy.wait()


BUFFERS = [
    pltpu.VMEM((4, PAIR, WIDTH), jnp.bfloat16),
    pltpu.VMEM((2 * QUAD, WIDTH), jnp.bfloat16),
    pltpu.VMEM((4, PAIR, B), jnp.float32),
    pltpu.VMEM((2, PAIR, 2 * QUAD), jnp.float32),
    pltpu.VMEM((2, PAIR, 2 * QUAD), jnp.bfloat16),
    pltpu.VMEM((8, LONG - B, B), jnp.bfloat16),
    pltpu.VMEM((2, 1, QUAD), jnp.float32),
    pltpu.SemaphoreType.DMA((4,)),
    pltpu.SemaphoreType.DMA((2,)),
    pltpu.SemaphoreType.DMA((4,)),
    pltpu.SemaphoreType.DMA,
]


def near_pass(spots, weight, left_grade, arrays):
    rows = jax.ShapeDtypeStruct((4, PAIR, B), jnp.float32)
    return pl.pallas_call(
        near_kernel,
        in_specs=[SMEM] + [whole(*a.shape) for a in (weight, left_grade)] + [ANY] * len(arrays),
        out_specs=[ANY, whole(4, PAIR, B), whole(4, PAIR, B)],
        out_shape=[jax.ShapeDtypeStruct((4, PAIR, WIDTH), jnp.bfloat16), rows, rows],
        scratch_shapes=[pltpu.VMEM((4, PAIR, WIDTH), jnp.bfloat16)] + BUFFERS,
        compiler_params=pltpu.CompilerParams(vmem_limit_bytes=20 * 2**20),
        cost_estimate=pl.CostEstimate(flops=9 * 10**9, bytes_accessed=16 * 2**20, transcendentals=2**21),
        name="near_tiles",
    )(spots, weight, left_grade, *arrays)


def far_pass(spots, weight, left_grade, extra, scale, near_inner, near_acc, arrays):
    return pl.pallas_call(
        far_kernel,
        in_specs=[SMEM]
        + [whole(*a.shape) for a in (weight, left_grade, extra, scale, near_inner)]
        + [ANY]
        + [ANY] * len(arrays),
        out_specs=ANY,
        out_shape=jax.ShapeDtypeStruct((8, 1040, PAIR), jnp.bfloat16),
        scratch_shapes=[
            pltpu.VMEM((4, PAIR, WIDTH), jnp.bfloat16),
            pltpu.VMEM((4, PAIR, B), jnp.float32),
            pltpu.VMEM((4, 1, PAIR), jnp.float32),
            pltpu.VMEM((4, 8, PAIR, PAIR), jnp.bfloat16),
            pltpu.VMEM((8, 16, PAIR), jnp.bfloat16),
        ]
        + BUFFERS
        + [pltpu.SemaphoreType.DMA((4,)), pltpu.SemaphoreType.DMA],
        compiler_params=pltpu.CompilerParams(vmem_limit_bytes=24 * 2**20),
        cost_estimate=pl.CostEstimate(flops=8 * 10**9, bytes_accessed=24 * 2**20, transcendentals=2**21),
        name="far_tiles",
    )(spots, weight, left_grade, extra, scale, near_inner, near_acc, *arrays)


def across(line, rows):
    column = jnp.broadcast_to(line, (B, rows)).T
    return jnp.concatenate([column, column], axis=1)


def weight_kernel(core_ref, back_ref, projected_ref, hidden_ref, grads_ref, give_ref, keep_ref, pre):
    @pl.when(pl.program_id(0) == 0)
    def _():
        tail = back_ref[:, 1024:, :].astype(jnp.float32)
        inner = jnp.sum(tail[:, 0:4] + tail[:, 4:8], axis=0)
        for part in range(8):
            at = pl.ds(part * B, B)
            grads = back_ref[0, at, :].astype(jnp.float32)
            for source in range(1, 8):
                grads += back_ref[source, at, :].astype(jnp.float32)
            grads_ref[at, :] = grads
            norm = across(tail[part, 8:9, :B] + tail[part, 8:9, B:], B)
            half = part % 2 * B
            product = across(inner[part // 2 : part // 2 + 1, half : half + B], B)
            unit = projected_ref[at, :].astype(jnp.float32) / norm
            pre[at, :] = ((grads - unit * product) / norm).astype(jnp.bfloat16)

    product = lax.dot_general(
        hidden_ref[...], pre[...], (((0,), (0,)), ((), ())), preferred_element_type=jnp.float32
    )
    core = core_ref[0]
    for k in range(2):
        even = product[2 * k * 224 : (2 * k + 1) * 224].astype(jnp.bfloat16)
        odd = product[(2 * k + 1) * 224 : (2 * k + 2) * 224].astype(jnp.bfloat16)
        mine = core == 0
        keep_ref[k] = jnp.where(mine, even, odd)
        give_ref[k] = jnp.where(mine, odd, even)


def weight_pass(core, back, projected, hidden):
    halves = pl.BlockSpec((2, 224, PAIR), lambda s: (s, 0, 0))
    return pl.pallas_call(
        weight_kernel,
        grid=(4,),
        in_specs=[
            SMEM,
            whole(8, 1040, PAIR),
            whole(1024, PAIR),
            pl.BlockSpec((1024, 896), lambda s: (0, s)),
        ],
        out_specs=[whole(1024, PAIR), halves, halves],
        out_shape=[
            jax.ShapeDtypeStruct((1024, PAIR), jnp.float32),
            jax.ShapeDtypeStruct((8, 224, PAIR), jnp.bfloat16),
            jax.ShapeDtypeStruct((8, 224, PAIR), jnp.bfloat16),
        ],
        scratch_shapes=[pltpu.VMEM((1024, PAIR), jnp.bfloat16)],
        compiler_params=pltpu.CompilerParams(vmem_limit_bytes=32 * 2**20),
        cost_estimate=pl.CostEstimate(flops=2 * 10**9, bytes_accessed=15 * 2**20, transcendentals=0),
        name="weight_terms",
    )(core, back, projected, hidden)


def own_kernel(grade_ref, came_ref, unit_ref, extra_ref, left_grade_ref):
    squares = jnp.zeros((B, B), jnp.float32)
    for k in range(8):
        for half in (0, B):
            part = came_ref[k, :B, half : half + B].astype(jnp.float32)
            squares += part * part
    norm = jnp.sqrt(jnp.sum(squares, axis=1, keepdims=True) + epsilon)
    wide = jnp.broadcast_to(norm, (B, B))
    for k in range(8):
        for half in (0, B):
            part = came_ref[k, :B, half : half + B].astype(jnp.float32) / wide
            unit_ref[:B, k * PAIR + half : k * PAIR + half + B] = (-part if k < 4 else part).astype(jnp.bfloat16)
    for k in range(4):
        lines = [came_ref[j, B:, :B].astype(jnp.float32)[0:1] for j in (2 * k, 2 * k + 1)]
        left_grade_ref[k] = jnp.concatenate(lines, axis=1)
    unit_ref[B:, :] = jnp.zeros((LONG - B, WIDTH), jnp.bfloat16)
    unit_ref[B:, :B] = jnp.broadcast_to(grade_ref[...], (LONG - B, B)).astype(jnp.bfloat16)
    line = wide.T[0:1]
    high = line.astype(jnp.bfloat16).astype(jnp.float32)
    extra_ref[...] = jnp.broadcast_to(jnp.concatenate([high, line - high], axis=1), (8, PAIR))


def own_pass(grades, came):
    return pl.pallas_call(
        own_kernel,
        in_specs=[whole(1, B), whole(8, LONG, PAIR)],
        out_specs=[whole(LONG, WIDTH), whole(8, PAIR), whole(4, 1, PAIR)],
        grid=(1,),
        out_shape=[
            jax.ShapeDtypeStruct((LONG, WIDTH), jnp.bfloat16),
            jax.ShapeDtypeStruct((8, PAIR), jnp.float32),
            jax.ShapeDtypeStruct((4, 1, PAIR), jnp.float32),
        ],
        compiler_params=pltpu.CompilerParams(vmem_limit_bytes=8 * 2**20),
        cost_estimate=pl.CostEstimate(flops=10**6, bytes_accessed=2**20, transcendentals=0),
        name="own_rows",
    )(grades, came)


def shards(hidden, projection, grades, pattern):
    y, zh, core, x, zl = (lax.axis_index(a) for a in AXES)
    col_here = x * 2 + zl

    grade_mine = grades.astype(jnp.bfloat16).reshape(1, B)
    projected = jnp.dot(hidden, projection, preferred_element_type=jnp.float32).astype(jnp.bfloat16)
    grade_rows = jnp.broadcast_to(jnp.tile(grade_mine, (1, 2)), (8, 16, PAIR))
    sent = jnp.concatenate([projected.reshape(8, B, PAIR), grade_rows], axis=1)
    came = lax.all_to_all(sent, COL, 0, 0, tiled=True)
    across_z = shift(projected, "zl", 1)
    below = shift(projected, "x", 1)
    above = shift(projected, "x", -1)

    both = (pattern + pattern.T).astype(jnp.float32)
    row_here = ((y * 2 + zh) * 2 + core) * 8
    home = lax.dynamic_slice_in_dim(both, row_here, 8, 0)
    right_ids = jnp.stack(
        [((((y + d) % 4) * 2 + (zh ^ z)) * 2 + (core ^ c)) * 8 + col_here for d, z, c in RIGHT]
    )
    right_pick = (jnp.arange(128)[:, None] == right_ids[None]).astype(jnp.float32)
    tiles = jnp.dot(home, right_pick, preferred_element_type=jnp.float32).reshape(4, 2, 4, 4)
    weight = jnp.repeat((tiles * (-smoothing_divisor / B)).transpose(2, 0, 1, 3), B, axis=3)
    spots = jnp.stack([((x + d) % 4 * 2 + (zl ^ z) + 4) % 8 for d, z in SHARDS]).astype(jnp.int32)
    came, across_z, below, above, weight, spots = lax.optimization_barrier(
        (came, across_z, below, above, weight, spots)
    )

    unit, extra, left_grade = own_pass(grade_mine.astype(jnp.float32), came)

    y_below = shift(unit, "y", 1)
    y_above = shift(unit, "y", -1)
    unit_z = shift(unit, "zh", 1)
    below_z = shift(across_z, "x", 1)
    above_z = shift(across_z, "x", -1)
    y_below, y_above, unit_z, unit, below, below_z, above_z, left_grade, extra = lax.optimization_barrier(
        (y_below, y_above, unit_z, unit, below, below_z, above_z, left_grade, extra)
    )
    z_below = shift(unit_z, "y", 1)
    z_above = shift(unit_z, "y", -1)
    far = shift(below, "x", 1)
    far_z = shift(above_z, "x", -1)
    other = shift(jnp.concatenate([unit, unit_z], axis=0), "core", 1)
    y_both = jnp.concatenate([y_above, y_below], axis=0)
    y_below, z_above, z_below, y_above, far, far_z, y_both = lax.optimization_barrier(
        (y_below, z_above, z_below, y_above, far, far_z, y_both)
    )
    y_far = shift(y_below, "y", 1)
    z_far = shift(z_above, "y", -1)
    y_other = shift(y_both, "core", 1)
    z_other = shift(jnp.concatenate([z_above, z_below], axis=0), "core", 1)

    left = [projected, across_z, below, below_z, above, above_z, far, far_z]
    nearby = [unit, unit_z, y_above, y_below, z_above, z_below]
    near_acc, near_inner, scale = near_pass(spots, weight[:2], left_grade, left + nearby + [other])
    y_far, z_far, near_acc, near_inner = lax.optimization_barrier((y_far, z_far, near_acc, near_inner))
    beyond = [y_other, z_other, y_far, z_far, shift(y_far, "core", 1), shift(z_far, "core", 1)]
    sums = far_pass(
        spots, weight[2:], left_grade, extra, scale, near_inner, near_acc, left + beyond
    )
    back = lax.all_to_all(sums, COL, 0, 0, tiled=True)

    grads, give, keep = weight_pass(core.astype(jnp.int32).reshape(1), back, projected, hidden)
    chip = (keep.astype(jnp.float32) + shift(give, "core", 1).astype(jnp.float32)).astype(jnp.bfloat16)
    gathered = lax.all_to_all(chip, ("y", "zh"), 0, 0, tiled=True)
    weight_grad = jnp.sum(gathered.astype(jnp.float32), axis=0)
    return grads, weight_grad


def solution(mesh):
    fine = Mesh(np.asarray(mesh.devices).reshape(SIZES), AXES)
    return jax.shard_map(
        shards,
        mesh=fine,
        in_specs=(P(ROW, None), P(None, COL), P(ROW + COL), P()),
        out_specs=(P(ROW, COL), P(ROW, COL)),
        check_vma=False,
    )
```

```python
import functools

import jax
import jax.numpy as jnp
import numpy as np
from jax import lax
from jax.experimental import pallas as pl
from jax.experimental.pallas import tpu as pltpu
from jax.sharding import Mesh, PartitionSpec as P

smoothing_divisor = 64.0
epsilon = 1e-06
AXES = ("y", "zh", "core", "x", "zl")
SIZES = (4, 2, 2, 4, 2)
ROW = ("y", "zh", "core")
COL = ("x", "zl")
B = 128
PAIR = 2 * B
QUAD = 4 * B
LONG = B + 16
WIDTH = 2048
ANY = pl.BlockSpec(memory_space=pltpu.HBM)
SMEM = pl.BlockSpec(memory_space=pltpu.SMEM)

RIGHT = ((0, 0, 0), (0, 1, 0), (1, 0, 0), (3, 0, 0), (1, 1, 0), (3, 1, 0), (0, 0, 1), (0, 1, 1))
RIGHT += ((1, 0, 1), (3, 0, 1), (1, 1, 1), (3, 1, 1), (2, 0, 0), (2, 1, 0), (2, 0, 1), (2, 1, 1))
SHARDS = ((0, 0), (0, 1), (3, 0), (3, 1), (1, 0), (1, 1), (2, 0), (2, 1))


def shift(value, axis, by):
    size = SIZES[AXES.index(axis)]
    return lax.ppermute(value, axis, [(i, (i + by) % size) for i in range(size)])


def whole(*shape):
    return pl.BlockSpec(shape, lambda *_: (0,) * len(shape))


def fetch(pieces, buffer, sem):
    row = 0
    for ref, first, rows in pieces:
        pltpu.make_async_copy(ref.at[pl.ds(first, rows)], buffer.at[pl.ds(row, rows)], sem).start()
        row += rows


def blocks(ref, first=0, count=1):
    return [(ref, k * LONG, B) for k in range(first, first + count)]


def fetch_right(rights, right_buf, right_sem, grade_rows, grade_sem):
    for k, pieces in enumerate(rights):
        fetch(pieces, right_buf.at[quad_rows(k)], right_sem.at[k])
        for j, (ref, first, rows) in enumerate(pieces):
            grades = ref.at[pl.ds(first + rows, LONG - B), pl.ds(0, B)]
            pltpu.make_async_copy(grades, grade_rows.at[k * 4 + j], grade_sem).start()


def right_grades(grade_rows, grade_sem, right_grade):
    filled(grade_rows, grade_sem)
    for k in range(8):
        lanes = slice(k % 4 * B, k % 4 * B + B)
        right_grade[k // 4, :, lanes] = grade_rows[k].astype(jnp.float32)[0:1]


def fetch_left(spot_ref, shards, slot, buffer, sem):
    for k, ref in enumerate(shards):
        lanes = pl.ds(pl.multiple_of(spot_ref[k] * PAIR, PAIR), PAIR)
        pltpu.make_async_copy(ref.at[pl.ds(slot * PAIR, PAIR), :], buffer.at[slot, :, lanes], sem).start()


def filled(buffer, sem):
    pltpu.make_async_copy(buffer, buffer, sem).wait()


def columns(left_grade_ref, grade_cols, slots):
    for slot in slots:
        grade_cols[slot] = jnp.broadcast_to(left_grade_ref[slot], (B, PAIR)).T


def score(left, right, scores):
    scores[...] = lax.dot_general(left[...], right[...], (((1,), (1,)), ((), ())), preferred_element_type=jnp.float32)


def slope(scores, weight, grade_cols, right_grade, scale, slopes, inner, first):
    for part in range(4):
        rows = slice(part * 64, part * 64 + 64)
        here = grade_cols[rows, :]
        scaled = scale[rows, :]
        total = None
        for lane in range(4):
            lanes = slice(lane * B, lane * B + B)
            value = scores[rows, lanes] * scaled
            label = jnp.clip(here - right_grade[:, lanes], -1.0, 1.0)
            step = label * weight[part // 2 : part // 2 + 1, lanes]
            grown = jnp.exp(label * value)
            one = (step * pltpu.reciprocal(1.0 + grown, approx=True)).astype(jnp.bfloat16)
            slopes[rows, lanes] = one
            term = one.astype(jnp.float32) * value
            total = term if total is None else total + term
        inner[rows, :] = total if first else inner[rows, :] + total


def quad_rows(quad, count=1):
    return pl.ds(quad * QUAD, count * QUAD)


def pair_tiles(left_buf, right_buf, weight_ref, grade_cols, right_grade_ref, scale, scores, slopes, inner, first, begin, finish):
    def ahead(slot, quad):
        begin(slot, quad)
        score(left_buf.at[slot], right_buf.at[quad_rows(quad)], scores.at[slot % 2, :, quad_rows(quad)])

    def arithmetic(slot, quad):
        slope(
            scores.at[slot % 2, :, quad_rows(quad)], weight_ref.at[quad, slot], grade_cols.at[slot],
            right_grade_ref.at[quad], scale.at[slot], slopes.at[slot % 2, :, quad_rows(quad)], inner.at[slot],
            first and quad == 0,
        )

    ahead(0, 0)
    ahead(0, 1)
    for slot in range(4):
        arithmetic(slot, 0)
        if slot < 3:
            ahead(slot + 1, 0)
        arithmetic(slot, 1)
        if slot < 3:
            ahead(slot + 1, 1)
        finish(slot, slopes.at[slot % 2])


def near_kernel(spot_ref, weight_ref, left_grade_ref, *refs):
    shards = refs[:8]
    unit, unit_z, y_above, y_below, z_above, z_below, other = refs[8:15]
    rights = (
        blocks(unit) + blocks(unit_z) + blocks(y_above) + blocks(y_below),
        blocks(z_above) + blocks(z_below) + blocks(other, 0, 2),
    )
    acc_out, inner, scale, acc, left_buf, right_buf, grade_cols, scores, slopes = refs[15:24]
    grade_rows, right_grade_ref, left_sem, right_sem, acc_sem, grade_sem = refs[24:]
    fetch_left(spot_ref, shards, 0, left_buf, left_sem.at[0])
    fetch_right(rights, right_buf, right_sem, grade_rows, grade_sem)
    for slot in (1, 2, 3):
        fetch_left(spot_ref, shards, slot, left_buf, left_sem.at[slot])
    columns(left_grade_ref, grade_cols, range(4))
    right_grades(grade_rows, grade_sem, right_grade_ref)
    acc_copy = lambda slot: pltpu.make_async_copy(acc.at[slot], acc_out.at[slot], acc_sem.at[slot])

    def begin(slot, quad):
        if quad == 0:
            filled(left_buf.at[slot], left_sem.at[slot])
            squares = jnp.zeros((PAIR, B), jnp.float32)
            for chunk in range(16):
                part = left_buf[slot, :, chunk * B : (chunk + 1) * B].astype(jnp.float32)
                squares += part * part
            norm = jnp.sqrt(jnp.sum(squares, axis=1, keepdims=True) + epsilon)
            scale[slot] = jnp.broadcast_to(smoothing_divisor / norm, (PAIR, B))
        if slot == 0:
            filled(right_buf.at[quad_rows(quad)], right_sem.at[quad])

    def finish(slot, slopes_ref):
        for chunk in range(8):
            lanes = slice(chunk * PAIR, chunk * PAIR + PAIR)
            part = jnp.dot(slopes_ref[...], right_buf[:, lanes], preferred_element_type=jnp.float32)
            acc[slot, :, lanes] = part.astype(jnp.bfloat16)
        acc_copy(slot).start()

    pair_tiles(
        left_buf, right_buf, weight_ref, grade_cols, right_grade_ref, scale, scores, slopes, inner, True, begin, finish
    )
    for slot in range(4):
        acc_copy(slot).wait()


def far_kernel(spot_ref, weight_ref, left_grade_ref, extra_ref, scale, near_inner, near_acc, *refs):
    shards = refs[:8]
    y_other, z_other, y_far, z_far, y_far_other, z_far_other = refs[8:14]
    rights = (
        blocks(y_other, 0, 2) + blocks(z_other, 0, 2),
        blocks(y_far) + blocks(z_far) + blocks(y_far_other) + blocks(z_far_other),
    )
    out_ref, acc, inner, lines, sent, tail, left_buf, right_buf, grade_cols, scores, slopes = refs[14:25]
    grade_rows, right_grade_ref, left_sem, right_sem, acc_sem, grade_sem, sent_sem, tail_sem = refs[25:]
    acc_in = lambda k: pltpu.make_async_copy(near_acc.at[k], acc.at[k], acc_sem.at[k])
    fetch_left(spot_ref, shards, 0, left_buf, left_sem.at[0])
    fetch_right(rights, right_buf, right_sem, grade_rows, grade_sem)
    for slot in range(4):
        if slot > 0:
            fetch_left(spot_ref, shards, slot, left_buf, left_sem.at[slot])
        acc_in(slot).start()
    columns(left_grade_ref, grade_cols, range(4))
    right_grades(grade_rows, grade_sem, right_grade_ref)
    inner[...] = near_inner[...]

    def home(slot):
        return pltpu.make_async_copy(sent.at[slot], out_ref.at[:, pl.ds(slot * PAIR, PAIR), :], sent_sem.at[slot])

    def begin(slot, quad):
        if quad == 0:
            filled(left_buf.at[slot], left_sem.at[slot])
        if slot == 0:
            filled(right_buf.at[quad_rows(quad)], right_sem.at[quad])

    def finish(slot, slopes_ref):
        acc_in(slot).wait()
        for chunk in range(8):
            source = (chunk + 4) % 8
            lanes = slice(source * PAIR, source * PAIR + PAIR)
            part = jnp.dot(slopes_ref[...], right_buf[:, lanes], preferred_element_type=jnp.float32)
            sent[slot, chunk] = (part + acc[slot, :, lanes].astype(jnp.float32)).astype(jnp.bfloat16)
        home(slot).start()
        lines[slot] = jnp.sum(inner[slot].T, axis=0, keepdims=True) * (1.0 / smoothing_divisor)

    pair_tiles(
        left_buf, right_buf, weight_ref, grade_cols, right_grade_ref, scale, scores, slopes, inner, False, begin, finish
    )
    total = jnp.concatenate([lines[k] for k in range(4)], axis=0)
    high = total.astype(jnp.bfloat16).astype(jnp.float32)
    last = jnp.concatenate([high, total - high, extra_ref[...]], axis=0).astype(jnp.bfloat16)
    for chunk in range(8):
        tail[chunk] = last
    tail_copy = pltpu.make_async_copy(tail, out_ref.at[:, pl.ds(1024, 16), :], tail_sem)
    tail_copy.start()
    for slot in range(4):
        home(slot).wait()
    tail_copy.wait()


BUFFERS = [
    pltpu.VMEM((4, PAIR, WIDTH), jnp.bfloat16),
    pltpu.VMEM((2 * QUAD, WIDTH), jnp.bfloat16),
    pltpu.VMEM((4, PAIR, B), jnp.float32),
    pltpu.VMEM((2, PAIR, 2 * QUAD), jnp.float32),
    pltpu.VMEM((2, PAIR, 2 * QUAD), jnp.bfloat16),
    pltpu.VMEM((8, LONG - B, B), jnp.bfloat16),
    pltpu.VMEM((2, 1, QUAD), jnp.float32),
    pltpu.SemaphoreType.DMA((4,)),
    pltpu.SemaphoreType.DMA((2,)),
    pltpu.SemaphoreType.DMA((4,)),
    pltpu.SemaphoreType.DMA,
]


def near_pass(spots, weight, left_grade, arrays):
    rows = jax.ShapeDtypeStruct((4, PAIR, B), jnp.float32)
    return pl.pallas_call(
        near_kernel,
        in_specs=[SMEM] + [whole(*a.shape) for a in (weight, left_grade)] + [ANY] * len(arrays),
        out_specs=[ANY, whole(4, PAIR, B), whole(4, PAIR, B)],
        out_shape=[jax.ShapeDtypeStruct((4, PAIR, WIDTH), jnp.bfloat16), rows, rows],
        scratch_shapes=[pltpu.VMEM((4, PAIR, WIDTH), jnp.bfloat16)] + BUFFERS,
        compiler_params=pltpu.CompilerParams(vmem_limit_bytes=20 * 2**20),
        cost_estimate=pl.CostEstimate(flops=9 * 10**9, bytes_accessed=16 * 2**20, transcendentals=2**21),
        name="near_tiles",
    )(spots, weight, left_grade, *arrays)


def far_pass(spots, weight, left_grade, extra, scale, near_inner, near_acc, arrays):
    return pl.pallas_call(
        far_kernel,
        in_specs=[SMEM]
        + [whole(*a.shape) for a in (weight, left_grade, extra, scale, near_inner)]
        + [ANY]
        + [ANY] * len(arrays),
        out_specs=ANY,
        out_shape=jax.ShapeDtypeStruct((8, 1040, PAIR), jnp.bfloat16),
        scratch_shapes=[
            pltpu.VMEM((4, PAIR, WIDTH), jnp.bfloat16),
            pltpu.VMEM((4, PAIR, B), jnp.float32),
            pltpu.VMEM((4, 1, PAIR), jnp.float32),
            pltpu.VMEM((4, 8, PAIR, PAIR), jnp.bfloat16),
            pltpu.VMEM((8, 16, PAIR), jnp.bfloat16),
        ]
        + BUFFERS
        + [pltpu.SemaphoreType.DMA((4,)), pltpu.SemaphoreType.DMA],
        compiler_params=pltpu.CompilerParams(vmem_limit_bytes=24 * 2**20),
        cost_estimate=pl.CostEstimate(flops=8 * 10**9, bytes_accessed=24 * 2**20, transcendentals=2**21),
        name="far_tiles",
    )(spots, weight, left_grade, extra, scale, near_inner, near_acc, *arrays)


def across(line, rows):
    column = jnp.broadcast_to(line, (B, rows)).T
    return jnp.concatenate([column, column], axis=1)


def weight_kernel(core_ref, back_ref, projected_ref, hidden_ref, grads_ref, give_ref, keep_ref, pre):
    @pl.when(pl.program_id(0) == 0)
    def _():
        tail = back_ref[:, 1024:, :].astype(jnp.float32)
        inner = jnp.sum(tail[:, 0:4] + tail[:, 4:8], axis=0)
        for part in range(8):
            at = pl.ds(part * B, B)
            grads = back_ref[0, at, :].astype(jnp.float32)
            for source in range(1, 8):
                grads += back_ref[source, at, :].astype(jnp.float32)
            grads_ref[at, :] = grads
            norm = across(tail[part, 8:9, :B] + tail[part, 8:9, B:], B)
            half = part % 2 * B
            product = across(inner[part // 2 : part // 2 + 1, half : half + B], B)
            unit = projected_ref[at, :].astype(jnp.float32) / norm
            pre[at, :] = ((grads - unit * product) / norm).astype(jnp.bfloat16)

    product = lax.dot_general(
        hidden_ref[...], pre[...], (((0,), (0,)), ((), ())), preferred_element_type=jnp.float32
    )
    core = core_ref[0]
    for k in range(2):
        even = product[2 * k * 224 : (2 * k + 1) * 224].astype(jnp.bfloat16)
        odd = product[(2 * k + 1) * 224 : (2 * k + 2) * 224].astype(jnp.bfloat16)
        mine = core == 0
        keep_ref[k] = jnp.where(mine, even, odd)
        give_ref[k] = jnp.where(mine, odd, even)


def weight_pass(core, back, projected, hidden):
    halves = pl.BlockSpec((2, 224, PAIR), lambda s: (s, 0, 0))
    return pl.pallas_call(
        weight_kernel,
        grid=(4,),
        in_specs=[
            SMEM,
            whole(8, 1040, PAIR),
            whole(1024, PAIR),
            pl.BlockSpec((1024, 896), lambda s: (0, s)),
        ],
        out_specs=[whole(1024, PAIR), halves, halves],
        out_shape=[
            jax.ShapeDtypeStruct((1024, PAIR), jnp.float32),
            jax.ShapeDtypeStruct((8, 224, PAIR), jnp.bfloat16),
            jax.ShapeDtypeStruct((8, 224, PAIR), jnp.bfloat16),
        ],
        scratch_shapes=[pltpu.VMEM((1024, PAIR), jnp.bfloat16)],
        compiler_params=pltpu.CompilerParams(vmem_limit_bytes=32 * 2**20),
        cost_estimate=pl.CostEstimate(flops=2 * 10**9, bytes_accessed=15 * 2**20, transcendentals=0),
        name="weight_terms",
    )(core, back, projected, hidden)


def project_kernel(grade_ref, hidden_ref, projection_ref, out_ref, sent_ref):
    rows = jnp.dot(hidden_ref[...], projection_ref[...], preferred_element_type=jnp.float32).astype(jnp.bfloat16)
    out_ref[...] = rows
    grades = jnp.broadcast_to(grade_ref[...], (LONG - B, B)).astype(jnp.bfloat16)
    for k in range(2):
        sent_ref[k, :B, :] = rows[k * B : (k + 1) * B]
        sent_ref[k, B:, :B] = grades
        sent_ref[k, B:, B:] = grades


def project_pass(grades, hidden, projection):
    return pl.pallas_call(
        project_kernel,
        grid=(4,),
        in_specs=[whole(1, B), pl.BlockSpec((PAIR, 3584), lambda s: (s, 0)), whole(3584, PAIR)],
        out_specs=[
            pl.BlockSpec((PAIR, PAIR), lambda s: (s, 0)),
            pl.BlockSpec((2, LONG, PAIR), lambda s: (s, 0, 0)),
        ],
        out_shape=[
            jax.ShapeDtypeStruct((1024, PAIR), jnp.bfloat16),
            jax.ShapeDtypeStruct((8, LONG, PAIR), jnp.bfloat16),
        ],
        compiler_params=pltpu.CompilerParams(vmem_limit_bytes=62 * 2**20),
        cost_estimate=pl.CostEstimate(flops=2 * 10**9, bytes_accessed=11 * 2**20, transcendentals=0),
        name="project",
    )(grades, hidden, projection)


def own_kernel(grade_ref, came_ref, unit_ref, extra_ref, left_grade_ref):
    squares = jnp.zeros((B, B), jnp.float32)
    for k in range(8):
        for half in (0, B):
            part = came_ref[k, :B, half : half + B].astype(jnp.float32)
            squares += part * part
    norm = jnp.sqrt(jnp.sum(squares, axis=1, keepdims=True) + epsilon)
    wide = jnp.broadcast_to(norm, (B, B))
    for k in range(8):
        for half in (0, B):
            part = came_ref[k, :B, half : half + B].astype(jnp.float32) / wide
            unit_ref[:B, k * PAIR + half : k * PAIR + half + B] = (-part if k < 4 else part).astype(jnp.bfloat16)
    for k in range(4):
        lines = [came_ref[j, B:, :B].astype(jnp.float32)[0:1] for j in (2 * k, 2 * k + 1)]
        left_grade_ref[k] = jnp.concatenate(lines, axis=1)
    unit_ref[B:, :] = jnp.zeros((LONG - B, WIDTH), jnp.bfloat16)
    unit_ref[B:, :B] = jnp.broadcast_to(grade_ref[...], (LONG - B, B)).astype(jnp.bfloat16)
    line = wide.T[0:1]
    high = line.astype(jnp.bfloat16).astype(jnp.float32)
    extra_ref[...] = jnp.broadcast_to(jnp.concatenate([high, line - high], axis=1), (8, PAIR))


def own_pass(grades, came):
    return pl.pallas_call(
        own_kernel,
        in_specs=[whole(1, B), whole(8, LONG, PAIR)],
        out_specs=[whole(LONG, WIDTH), whole(8, PAIR), whole(4, 1, PAIR)],
        grid=(1,),
        out_shape=[
            jax.ShapeDtypeStruct((LONG, WIDTH), jnp.bfloat16),
            jax.ShapeDtypeStruct((8, PAIR), jnp.float32),
            jax.ShapeDtypeStruct((4, 1, PAIR), jnp.float32),
        ],
        compiler_params=pltpu.CompilerParams(vmem_limit_bytes=8 * 2**20),
        cost_estimate=pl.CostEstimate(flops=10**6, bytes_accessed=2**20, transcendentals=0),
        name="own_rows",
    )(grades, came)


def shards(hidden, projection, grades, pattern):
    y, zh, core, x, zl = (lax.axis_index(a) for a in AXES)
    col_here = x * 2 + zl

    grade_mine = grades.astype(jnp.float32).reshape(1, B)
    projected, sent = project_pass(grade_mine, hidden, projection)
    came = lax.all_to_all(sent, COL, 0, 0, tiled=True)
    across_z = shift(projected, "zl", 1)
    below = shift(projected, "x", 1)
    above = shift(projected, "x", -1)

    both = (pattern + pattern.T).astype(jnp.float32)
    row_here = ((y * 2 + zh) * 2 + core) * 8
    home = lax.dynamic_slice_in_dim(both, row_here, 8, 0)
    right_ids = jnp.stack(
        [((((y + d) % 4) * 2 + (zh ^ z)) * 2 + (core ^ c)) * 8 + col_here for d, z, c in RIGHT]
    )
    right_pick = (jnp.arange(128)[:, None] == right_ids[None]).astype(jnp.float32)
    tiles = jnp.dot(home, right_pick, preferred_element_type=jnp.float32).reshape(4, 2, 4, 4)
    weight = jnp.repeat((tiles * (-smoothing_divisor / B)).transpose(2, 0, 1, 3), B, axis=3)
    spots = jnp.stack([((x + d) % 4 * 2 + (zl ^ z) + 4) % 8 for d, z in SHARDS]).astype(jnp.int32)
    came, across_z, below, above, weight, spots = lax.optimization_barrier(
        (came, across_z, below, above, weight, spots)
    )

    unit, extra, left_grade = own_pass(grade_mine, came)

    y_below = shift(unit, "y", 1)
    y_above = shift(unit, "y", -1)
    unit_z = shift(unit, "zh", 1)
    below_z = shift(across_z, "x", 1)
    above_z = shift(across_z, "x", -1)
    y_below, y_above, unit_z, unit, below, below_z, above_z, left_grade, extra = lax.optimization_barrier(
        (y_below, y_above, unit_z, unit, below, below_z, above_z, left_grade, extra)
    )
    z_below = shift(unit_z, "y", 1)
    z_above = shift(unit_z, "y", -1)
    far = shift(below, "x", 1)
    far_z = shift(above_z, "x", -1)
    other = shift(jnp.concatenate([unit, unit_z], axis=0), "core", 1)
    y_both = jnp.concatenate([y_above, y_below], axis=0)
    y_below, z_above, z_below, y_above, far, far_z, y_both = lax.optimization_barrier(
        (y_below, z_above, z_below, y_above, far, far_z, y_both)
    )
    y_far = shift(y_below, "y", 1)
    z_far = shift(z_above, "y", -1)
    y_other = shift(y_both, "core", 1)
    z_other = shift(jnp.concatenate([z_above, z_below], axis=0), "core", 1)

    left = [projected, across_z, below, below_z, above, above_z, far, far_z]
    nearby = [unit, unit_z, y_above, y_below, z_above, z_below]
    near_acc, near_inner, scale = near_pass(spots, weight[:2], left_grade, left + nearby + [other])
    y_far, z_far, near_acc, near_inner = lax.optimization_barrier((y_far, z_far, near_acc, near_inner))
    beyond = [y_other, z_other, y_far, z_far, shift(y_far, "core", 1), shift(z_far, "core", 1)]
    sums = far_pass(
        spots, weight[2:], left_grade, extra, scale, near_inner, near_acc, left + beyond
    )
    back = lax.all_to_all(sums, COL, 0, 0, tiled=True)

    grads, give, keep = weight_pass(core.astype(jnp.int32).reshape(1), back, projected, hidden)
    chip = (keep.astype(jnp.float32) + shift(give, "core", 1).astype(jnp.float32)).astype(jnp.bfloat16)
    gathered = lax.all_to_all(chip, ("y", "zh"), 0, 0, tiled=True)
    weight_grad = jnp.sum(gathered.astype(jnp.float32), axis=0)
    return grads, weight_grad


def solution(mesh):
    fine = Mesh(np.asarray(mesh.devices).reshape(SIZES), AXES)
    return jax.shard_map(
        shards,
        mesh=fine,
        in_specs=(P(ROW, None), P(None, COL), P(ROW + COL), P()),
        out_specs=(P(ROW, COL), P(ROW, COL)),
        check_vma=False,
    )
```

```python
import functools

import jax
import jax.numpy as jnp
import numpy as np
from jax import lax
from jax.experimental import pallas as pl
from jax.experimental.pallas import tpu as pltpu
from jax.sharding import Mesh, PartitionSpec as P

smoothing_divisor = 64.0
epsilon = 1e-06
AXES = ("y", "zh", "core", "x", "zl")
SIZES = (4, 2, 2, 4, 2)
ROW = ("y", "zh", "core")
COL = ("x", "zl")
B = 128
PAIR = 2 * B
QUAD = 4 * B
LONG = B + 16
WIDTH = 2048
ANY = pl.BlockSpec(memory_space=pltpu.HBM)
SMEM = pl.BlockSpec(memory_space=pltpu.SMEM)
VMEM = pl.BlockSpec(memory_space=pltpu.VMEM)

RIGHT = ((0, 0, 0), (0, 1, 0), (1, 0, 0), (3, 0, 0), (1, 1, 0), (3, 1, 0), (0, 0, 1), (0, 1, 1))
RIGHT += ((1, 0, 1), (3, 0, 1), (1, 1, 1), (3, 1, 1), (2, 0, 0), (2, 1, 0), (2, 0, 1), (2, 1, 1))
SHARDS = ((0, 0), (0, 1), (3, 0), (3, 1), (1, 0), (1, 1), (2, 0), (2, 1))


def shift(value, axis, by):
    size = SIZES[AXES.index(axis)]
    return lax.ppermute(value, axis, [(i, (i + by) % size) for i in range(size)])


def whole(*shape):
    return pl.BlockSpec(shape, lambda *_: (0,) * len(shape))


def blocks(ref, first=0, count=1):
    return [(ref, k * LONG) for k in range(first, first + count)]


def stacked(pieces, lanes=slice(None)):
    return jnp.concatenate([ref[first : first + B, lanes] for ref, first in pieces], axis=0)


def right_grades(rights, right_grade):
    for k, pieces in enumerate(rights):
        for j, (ref, first) in enumerate(pieces):
            line = ref[first + B : first + LONG, :B].astype(jnp.float32)[0:1]
            right_grade[k, :, j * B : (j + 1) * B] = line


def fetch_left(spot_ref, shards, slot, buffer, sem):
    for k, ref in enumerate(shards):
        lanes = pl.ds(pl.multiple_of(spot_ref[k] * PAIR, PAIR), PAIR)
        pltpu.make_async_copy(ref.at[pl.ds(slot * PAIR, PAIR), :], buffer.at[slot, :, lanes], sem).start()


def filled(buffer, sem):
    pltpu.make_async_copy(buffer, buffer, sem).wait()


def columns(left_grade_ref, grade_cols, slots):
    for slot in slots:
        grade_cols[slot] = jnp.broadcast_to(left_grade_ref[slot], (B, PAIR)).T


def score(left, right, scores):
    scores[...] = lax.dot_general(left[...], right, (((1,), (1,)), ((), ())), preferred_element_type=jnp.float32)


def slope(scores, weight, grade_cols, right_grade, scale, slopes, inner, first):
    for part in range(4):
        rows = slice(part * 64, part * 64 + 64)
        here = grade_cols[rows, :]
        scaled = scale[rows, :]
        total = None
        for lane in range(4):
            lanes = slice(lane * B, lane * B + B)
            value = scores[rows, lanes] * scaled
            label = jnp.clip(here - right_grade[:, lanes], -1.0, 1.0)
            step = label * weight[part // 2 : part // 2 + 1, lanes]
            grown = jnp.exp(label * value)
            one = (step * pltpu.reciprocal(1.0 + grown, approx=True)).astype(jnp.bfloat16)
            slopes[rows, lanes] = one
            term = one.astype(jnp.float32) * value
            total = term if total is None else total + term
        inner[rows, :] = total if first else inner[rows, :] + total


def quad_rows(quad, count=1):
    return pl.ds(quad * QUAD, count * QUAD)


def pair_tiles(left_buf, rights, weight_ref, grade_cols, right_grade_ref, scale, scores, slopes, inner, first, begin, finish):
    def ahead(slot, quad):
        begin(slot, quad)
        score(left_buf.at[slot], stacked(rights[quad]), scores.at[slot % 2, :, quad_rows(quad)])

    def arithmetic(slot, quad):
        slope(
            scores.at[slot % 2, :, quad_rows(quad)], weight_ref.at[quad, slot], grade_cols.at[slot],
            right_grade_ref.at[quad], scale.at[slot], slopes.at[slot % 2, :, quad_rows(quad)], inner.at[slot],
            first and quad == 0,
        )

    ahead(0, 0)
    ahead(0, 1)
    for slot in range(4):
        arithmetic(slot, 0)
        if slot < 3:
            ahead(slot + 1, 0)
        arithmetic(slot, 1)
        if slot < 3:
            ahead(slot + 1, 1)
        finish(slot, slopes.at[slot % 2])


def near_kernel(spot_ref, weight_ref, left_grade_ref, *refs):
    shards = refs[:8]
    unit, unit_z, y_above, y_below, z_above, z_below, other = refs[8:15]
    rights = (
        blocks(unit) + blocks(unit_z) + blocks(y_above) + blocks(y_below),
        blocks(z_above) + blocks(z_below) + blocks(other, 0, 2),
    )
    acc, left_buf, inner, scale, grade_cols, scores, slopes, right_grade_ref, left_sem = refs[15:]
    fetch_left(spot_ref, shards, 0, left_buf, left_sem.at[0])
    for slot in (1, 2, 3):
        fetch_left(spot_ref, shards, slot, left_buf, left_sem.at[slot])
    columns(left_grade_ref, grade_cols, range(4))
    right_grades(rights, right_grade_ref)

    def begin(slot, quad):
        if quad == 0:
            filled(left_buf.at[slot], left_sem.at[slot])
            squares = jnp.zeros((PAIR, B), jnp.float32)
            for chunk in range(16):
                part = left_buf[slot, :, chunk * B : (chunk + 1) * B].astype(jnp.float32)
                squares += part * part
            norm = jnp.sqrt(jnp.sum(squares, axis=1, keepdims=True) + epsilon)
            scale[slot] = jnp.broadcast_to(smoothing_divisor / norm, (PAIR, B))

    def finish(slot, slopes_ref):
        for chunk in range(8):
            lanes = slice(chunk * PAIR, chunk * PAIR + PAIR)
            part = jnp.dot(slopes_ref[...], stacked(rights[0] + rights[1], lanes), preferred_element_type=jnp.float32)
            acc[slot, :, lanes] = part.astype(jnp.bfloat16)

    pair_tiles(
        left_buf, rights, weight_ref, grade_cols, right_grade_ref, scale, scores, slopes, inner, True, begin, finish
    )


def far_kernel(weight_ref, left_grade_ref, extra_ref, scale, near_inner, left_buf, acc, *refs):
    y_other, z_other, y_far, z_far, y_far_other, z_far_other = refs[:6]
    rights = (
        blocks(y_other, 0, 2) + blocks(z_other, 0, 2),
        blocks(y_far) + blocks(z_far) + blocks(y_far_other) + blocks(z_far_other),
    )
    out_ref, inner, lines, sent, tail, grade_cols, scores, slopes, right_grade_ref = refs[6:15]
    _, sent_sem, tail_sem = refs[15:]
    columns(left_grade_ref, grade_cols, range(4))
    right_grades(rights, right_grade_ref)
    inner[...] = near_inner[...]

    def home(slot):
        return pltpu.make_async_copy(sent.at[slot], out_ref.at[:, pl.ds(slot * PAIR, PAIR), :], sent_sem.at[slot])

    def finish(slot, slopes_ref):
        for chunk in range(8):
            source = (chunk + 4) % 8
            lanes = slice(source * PAIR, source * PAIR + PAIR)
            part = jnp.dot(slopes_ref[...], stacked(rights[0] + rights[1], lanes), preferred_element_type=jnp.float32)
            sent[slot, chunk] = (part + acc[slot, :, lanes].astype(jnp.float32)).astype(jnp.bfloat16)
        home(slot).start()
        lines[slot] = jnp.sum(inner[slot].T, axis=0, keepdims=True) * (1.0 / smoothing_divisor)

    pair_tiles(
        left_buf, rights, weight_ref, grade_cols, right_grade_ref, scale, scores, slopes, inner, False,
        lambda slot, quad: None, finish
    )
    total = jnp.concatenate([lines[k] for k in range(4)], axis=0)
    high = total.astype(jnp.bfloat16).astype(jnp.float32)
    last = jnp.concatenate([high, total - high, extra_ref[...]], axis=0).astype(jnp.bfloat16)
    for chunk in range(8):
        tail[chunk] = last
    tail_copy = pltpu.make_async_copy(tail, out_ref.at[:, pl.ds(1024, 16), :], tail_sem)
    tail_copy.start()
    for slot in range(4):
        home(slot).wait()
    tail_copy.wait()


BUFFERS = [
    pltpu.VMEM((4, PAIR, B), jnp.float32),
    pltpu.VMEM((2, PAIR, 2 * QUAD), jnp.float32),
    pltpu.VMEM((2, PAIR, 2 * QUAD), jnp.bfloat16),
    pltpu.VMEM((2, 1, QUAD), jnp.float32),
    pltpu.SemaphoreType.DMA((4,)),
]


def near_pass(spots, weight, left_grade, shards, arrays):
    wide = jax.ShapeDtypeStruct((4, PAIR, WIDTH), jnp.bfloat16)
    rows = jax.ShapeDtypeStruct((4, PAIR, B), jnp.float32)
    return pl.pallas_call(
        near_kernel,
        in_specs=[SMEM, VMEM, VMEM] + [ANY] * len(shards) + [VMEM] * len(arrays),
        out_specs=[VMEM] * 4,
        out_shape=[wide, wide, rows, rows],
        scratch_shapes=BUFFERS,
        compiler_params=pltpu.CompilerParams(vmem_limit_bytes=20 * 2**20),
        cost_estimate=pl.CostEstimate(flops=9 * 10**9, bytes_accessed=16 * 2**20, transcendentals=2**21),
        name="near_tiles",
    )(spots, weight, left_grade, *shards, *arrays)


def far_pass(*arrays):
    return pl.pallas_call(
        far_kernel,
        in_specs=[VMEM] * len(arrays),
        out_specs=ANY,
        out_shape=jax.ShapeDtypeStruct((8, 1040, PAIR), jnp.bfloat16),
        scratch_shapes=[
            pltpu.VMEM((4, PAIR, B), jnp.float32),
            pltpu.VMEM((4, 1, PAIR), jnp.float32),
            pltpu.VMEM((4, 8, PAIR, PAIR), jnp.bfloat16),
            pltpu.VMEM((8, 16, PAIR), jnp.bfloat16),
        ]
        + BUFFERS
        + [pltpu.SemaphoreType.DMA((4,)), pltpu.SemaphoreType.DMA],
        compiler_params=pltpu.CompilerParams(vmem_limit_bytes=24 * 2**20),
        cost_estimate=pl.CostEstimate(flops=8 * 10**9, bytes_accessed=24 * 2**20, transcendentals=2**21),
        name="far_tiles",
    )(*arrays)


def across(line, rows):
    column = jnp.broadcast_to(line, (B, rows)).T
    return jnp.concatenate([column, column], axis=1)


def weight_kernel(core_ref, back_ref, projected_ref, hidden_ref, grads_ref, give_ref, keep_ref, pre):
    @pl.when(pl.program_id(0) == 0)
    def _():
        tail = back_ref[:, 1024:, :].astype(jnp.float32)
        inner = jnp.sum(tail[:, 0:4] + tail[:, 4:8], axis=0)
        for part in range(8):
            at = pl.ds(part * B, B)
            grads = back_ref[0, at, :].astype(jnp.float32)
            for source in range(1, 8):
                grads += back_ref[source, at, :].astype(jnp.float32)
            grads_ref[at, :] = grads
            norm = across(tail[part, 8:9, :B] + tail[part, 8:9, B:], B)
            half = part % 2 * B
            product = across(inner[part // 2 : part // 2 + 1, half : half + B], B)
            unit = projected_ref[at, :].astype(jnp.float32) / norm
            pre[at, :] = ((grads - unit * product) / norm).astype(jnp.bfloat16)

    product = lax.dot_general(
        hidden_ref[...], pre[...], (((0,), (0,)), ((), ())), preferred_element_type=jnp.float32
    )
    core = core_ref[0]
    for k in range(2):
        even = product[2 * k * 224 : (2 * k + 1) * 224].astype(jnp.bfloat16)
        odd = product[(2 * k + 1) * 224 : (2 * k + 2) * 224].astype(jnp.bfloat16)
        mine = core == 0
        keep_ref[k] = jnp.where(mine, even, odd)
        give_ref[k] = jnp.where(mine, odd, even)


def weight_pass(core, back, projected, hidden):
    halves = pl.BlockSpec((2, 224, PAIR), lambda s: (s, 0, 0))
    return pl.pallas_call(
        weight_kernel,
        grid=(4,),
        in_specs=[
            SMEM,
            whole(8, 1040, PAIR),
            whole(1024, PAIR),
            pl.BlockSpec((1024, 896), lambda s: (0, s)),
        ],
        out_specs=[whole(1024, PAIR), halves, halves],
        out_shape=[
            jax.ShapeDtypeStruct((1024, PAIR), jnp.float32),
            jax.ShapeDtypeStruct((8, 224, PAIR), jnp.bfloat16),
            jax.ShapeDtypeStruct((8, 224, PAIR), jnp.bfloat16),
        ],
        scratch_shapes=[pltpu.VMEM((1024, PAIR), jnp.bfloat16)],
        compiler_params=pltpu.CompilerParams(vmem_limit_bytes=32 * 2**20),
        cost_estimate=pl.CostEstimate(flops=2 * 10**9, bytes_accessed=15 * 2**20, transcendentals=0),
        name="weight_terms",
    )(core, back, projected, hidden)


def own_kernel(grade_ref, came_ref, unit_ref, extra_ref, left_grade_ref):
    squares = jnp.zeros((B, B), jnp.float32)
    for k in range(8):
        for half in (0, B):
            part = came_ref[k, :B, half : half + B].astype(jnp.float32)
            squares += part * part
    norm = jnp.sqrt(jnp.sum(squares, axis=1, keepdims=True) + epsilon)
    wide = jnp.broadcast_to(norm, (B, B))
    for k in range(8):
        for half in (0, B):
            part = came_ref[k, :B, half : half + B].astype(jnp.float32) / wide
            unit_ref[:B, k * PAIR + half : k * PAIR + half + B] = (-part if k < 4 else part).astype(jnp.bfloat16)
    for k in range(4):
        lines = [came_ref[j, B:, :B].astype(jnp.float32)[0:1] for j in (2 * k, 2 * k + 1)]
        left_grade_ref[k] = jnp.concatenate(lines, axis=1)
    unit_ref[B:, :] = jnp.zeros((LONG - B, WIDTH), jnp.bfloat16)
    unit_ref[B:, :B] = jnp.broadcast_to(grade_ref[...], (LONG - B, B)).astype(jnp.bfloat16)
    line = wide.T[0:1]
    high = line.astype(jnp.bfloat16).astype(jnp.float32)
    extra_ref[...] = jnp.broadcast_to(jnp.concatenate([high, line - high], axis=1), (8, PAIR))


def own_pass(grades, came):
    return pl.pallas_call(
        own_kernel,
        in_specs=[whole(1, B), whole(8, LONG, PAIR)],
        out_specs=[whole(LONG, WIDTH), whole(8, PAIR), whole(4, 1, PAIR)],
        grid=(1,),
        out_shape=[
            jax.ShapeDtypeStruct((LONG, WIDTH), jnp.bfloat16),
            jax.ShapeDtypeStruct((8, PAIR), jnp.float32),
            jax.ShapeDtypeStruct((4, 1, PAIR), jnp.float32),
        ],
        compiler_params=pltpu.CompilerParams(vmem_limit_bytes=8 * 2**20),
        cost_estimate=pl.CostEstimate(flops=10**6, bytes_accessed=2**20, transcendentals=0),
        name="own_rows",
    )(grades, came)


def shards(hidden, projection, grades, pattern):
    y, zh, core, x, zl = (lax.axis_index(a) for a in AXES)
    col_here = x * 2 + zl

    grade_mine = grades.astype(jnp.bfloat16).reshape(1, B)
    projected = jnp.dot(hidden, projection, preferred_element_type=jnp.float32).astype(jnp.bfloat16)
    grade_rows = jnp.broadcast_to(jnp.tile(grade_mine, (1, 2)), (8, 16, PAIR))
    sent = jnp.concatenate([projected.reshape(8, B, PAIR), grade_rows], axis=1)
    came = lax.all_to_all(sent, COL, 0, 0, tiled=True)
    across_z = shift(projected, "zl", 1)
    below = shift(projected, "x", 1)
    above = shift(projected, "x", -1)

    both = (pattern + pattern.T).astype(jnp.float32)
    row_here = ((y * 2 + zh) * 2 + core) * 8
    home = lax.dynamic_slice_in_dim(both, row_here, 8, 0)
    right_ids = jnp.stack(
        [((((y + d) % 4) * 2 + (zh ^ z)) * 2 + (core ^ c)) * 8 + col_here for d, z, c in RIGHT]
    )
    right_pick = (jnp.arange(128)[:, None] == right_ids[None]).astype(jnp.float32)
    tiles = jnp.dot(home, right_pick, preferred_element_type=jnp.float32).reshape(4, 2, 4, 4)
    weight = jnp.repeat((tiles * (-smoothing_divisor / B)).transpose(2, 0, 1, 3), B, axis=3)
    spots = jnp.stack([((x + d) % 4 * 2 + (zl ^ z) + 4) % 8 for d, z in SHARDS]).astype(jnp.int32)
    came, across_z, below, above, weight, spots = lax.optimization_barrier(
        (came, across_z, below, above, weight, spots)
    )

    unit, extra, left_grade = own_pass(grade_mine.astype(jnp.float32), came)

    y_below = shift(unit, "y", 1)
    y_above = shift(unit, "y", -1)
    unit_z = shift(unit, "zh", 1)
    below_z = shift(across_z, "x", 1)
    above_z = shift(across_z, "x", -1)
    y_below, y_above, unit_z, unit, below, below_z, above_z, left_grade, extra = lax.optimization_barrier(
        (y_below, y_above, unit_z, unit, below, below_z, above_z, left_grade, extra)
    )
    z_below = shift(unit_z, "y", 1)
    z_above = shift(unit_z, "y", -1)
    far = shift(below, "x", 1)
    far_z = shift(above_z, "x", -1)
    other = shift(jnp.concatenate([unit, unit_z], axis=0), "core", 1)
    y_both = jnp.concatenate([y_above, y_below], axis=0)
    y_below, z_above, z_below, y_above, far, far_z, y_both = lax.optimization_barrier(
        (y_below, z_above, z_below, y_above, far, far_z, y_both)
    )
    y_far = shift(y_below, "y", 1)
    z_far = shift(z_above, "y", -1)
    y_other = shift(y_both, "core", 1)
    z_other = shift(jnp.concatenate([z_above, z_below], axis=0), "core", 1)

    left = [projected, across_z, below, below_z, above, above_z, far, far_z]
    nearby = [unit, unit_z, y_above, y_below, z_above, z_below]
    near_acc, left_rows, near_inner, scale = near_pass(spots, weight[:2], left_grade, left, nearby + [other])
    y_far, z_far, near_acc, near_inner = lax.optimization_barrier((y_far, z_far, near_acc, near_inner))
    beyond = [y_other, z_other, y_far, z_far, shift(y_far, "core", 1), shift(z_far, "core", 1)]
    sums = far_pass(weight[2:], left_grade, extra, scale, near_inner, left_rows, near_acc, *beyond)
    back = lax.all_to_all(sums, COL, 0, 0, tiled=True)

    grads, give, keep = weight_pass(core.astype(jnp.int32).reshape(1), back, projected, hidden)
    chip = (keep.astype(jnp.float32) + shift(give, "core", 1).astype(jnp.float32)).astype(jnp.bfloat16)
    gathered = lax.all_to_all(chip, ("y", "zh"), 0, 0, tiled=True)
    weight_grad = jnp.sum(gathered.astype(jnp.float32), axis=0)
    return grads, weight_grad


def solution(mesh):
    fine = Mesh(np.asarray(mesh.devices).reshape(SIZES), AXES)
    return jax.shard_map(
        shards,
        mesh=fine,
        in_specs=(P(ROW, None), P(None, COL), P(ROW + COL), P()),
        out_specs=(P(ROW, COL), P(ROW, COL)),
        check_vma=False,
    )
```

```python
import functools

import jax
import jax.numpy as jnp
import numpy as np
from jax import lax
from jax.experimental import pallas as pl
from jax.experimental.pallas import tpu as pltpu
from jax.sharding import Mesh, PartitionSpec as P

smoothing_divisor = 64.0
epsilon = 1e-06
AXES = ("y", "zh", "core", "x", "zl")
SIZES = (4, 2, 2, 4, 2)
ROW = ("y", "zh", "core")
COL = ("x", "zl")
B = 128
PAIR = 2 * B
QUAD = 4 * B
LONG = B + 16
WIDTH = 2048
ANY = pl.BlockSpec(memory_space=pltpu.HBM)
SMEM = pl.BlockSpec(memory_space=pltpu.SMEM)
VMEM = pl.BlockSpec(memory_space=pltpu.VMEM)

RIGHT = ((0, 0, 0), (0, 1, 0), (1, 0, 0), (3, 0, 0), (1, 1, 0), (3, 1, 0), (0, 0, 1), (0, 1, 1))
RIGHT += ((1, 0, 1), (3, 0, 1), (1, 1, 1), (3, 1, 1), (2, 0, 0), (2, 1, 0), (2, 0, 1), (2, 1, 1))
SHARDS = ((0, 0), (0, 1), (3, 0), (3, 1), (1, 0), (1, 1), (2, 0), (2, 1))


def shift(value, axis, by):
    size = SIZES[AXES.index(axis)]
    return lax.ppermute(value, axis, [(i, (i + by) % size) for i in range(size)])


def whole(*shape):
    return pl.BlockSpec(shape, lambda *_: (0,) * len(shape))


def blocks(ref, first=0, count=1):
    return [(ref, k * LONG) for k in range(first, first + count)]


def stacked(pieces, lanes=slice(None)):
    return jnp.concatenate([ref[first : first + B, lanes] for ref, first in pieces], axis=0)


def right_grades(rights, right_grade):
    for k, pieces in enumerate(rights):
        for j, (ref, first) in enumerate(pieces):
            line = ref[first + B : first + LONG, :B].astype(jnp.float32)[0:1]
            right_grade[k, :, j * B : (j + 1) * B] = line


def fetch_left(spot_ref, shards, slot, buffer, sem):
    for k, ref in enumerate(shards):
        lanes = pl.ds(pl.multiple_of(spot_ref[k] * PAIR, PAIR), PAIR)
        pltpu.make_async_copy(ref.at[pl.ds(slot * PAIR, PAIR), :], buffer.at[slot, :, lanes], sem).start()


def filled(buffer, sem):
    pltpu.make_async_copy(buffer, buffer, sem).wait()


def columns(left_grade_ref, grade_cols, slots):
    for slot in slots:
        grade_cols[slot] = jnp.broadcast_to(left_grade_ref[slot], (B, PAIR)).T


def score(left, right, scores):
    scores[...] = lax.dot_general(left[...], right, (((1,), (1,)), ((), ())), preferred_element_type=jnp.float32)


def slope(scores, weight, grade_cols, right_grade, scale, slopes, inner, first):
    for part in range(4):
        rows = slice(part * 64, part * 64 + 64)
        here = grade_cols[rows, :]
        scaled = scale[rows, :]
        total = None
        for lane in range(4):
            lanes = slice(lane * B, lane * B + B)
            value = scores[rows, lanes] * scaled
            label = jnp.clip(here - right_grade[:, lanes], -1.0, 1.0)
            step = label * weight[part // 2 : part // 2 + 1, lanes]
            grown = jnp.exp(label * value)
            one = (step * pltpu.reciprocal(1.0 + grown, approx=True)).astype(jnp.bfloat16)
            slopes[rows, lanes] = one
            term = one.astype(jnp.float32) * value
            total = term if total is None else total + term
        inner[rows, :] = total if first else inner[rows, :] + total


def quad_rows(quad, count=1):
    return pl.ds(quad * QUAD, count * QUAD)


def pair_tiles(left_buf, rights, weight_ref, grade_cols, right_grade_ref, scale, scores, slopes, inner, first, begin, finish):
    def ahead(slot, quad):
        begin(slot, quad)
        score(left_buf.at[slot], stacked(rights[quad]), scores.at[slot % 2, :, quad_rows(quad)])

    def arithmetic(slot, quad):
        slope(
            scores.at[slot % 2, :, quad_rows(quad)], weight_ref.at[quad, slot], grade_cols.at[slot],
            right_grade_ref.at[quad], scale.at[slot], slopes.at[slot % 2, :, quad_rows(quad)], inner.at[slot],
            first and quad == 0,
        )

    ahead(0, 0)
    ahead(0, 1)
    for slot in range(4):
        arithmetic(slot, 0)
        if slot < 3:
            ahead(slot + 1, 0)
        arithmetic(slot, 1)
        if slot < 3:
            ahead(slot + 1, 1)
        finish(slot, slopes.at[slot % 2])


def near_kernel(spot_ref, weight_ref, left_grade_ref, *refs):
    shards = refs[:8]
    unit, unit_z, y_above, y_below, z_above, z_below, other = refs[8:15]
    rights = (
        blocks(unit) + blocks(unit_z) + blocks(y_above) + blocks(y_below),
        blocks(z_above) + blocks(z_below) + blocks(other, 0, 2),
    )
    acc, left_buf, inner, scale, grade_cols, scores, slopes, right_grade_ref, left_sem = refs[15:]
    fetch_left(spot_ref, shards, 0, left_buf, left_sem.at[0])
    for slot in (1, 2, 3):
        fetch_left(spot_ref, shards, slot, left_buf, left_sem.at[slot])
    columns(left_grade_ref, grade_cols, range(4))
    right_grades(rights, right_grade_ref)

    def begin(slot, quad):
        if quad == 0:
            filled(left_buf.at[slot], left_sem.at[slot])
            squares = jnp.zeros((PAIR, B), jnp.float32)
            for chunk in range(16):
                part = left_buf[slot, :, chunk * B : (chunk + 1) * B].astype(jnp.float32)
                squares += part * part
            norm = jnp.sqrt(jnp.sum(squares, axis=1, keepdims=True) + epsilon)
            scale[slot] = jnp.broadcast_to(smoothing_divisor / norm, (PAIR, B))

    def finish(slot, slopes_ref):
        for chunk in range(8):
            lanes = slice(chunk * PAIR, chunk * PAIR + PAIR)
            part = jnp.dot(slopes_ref[...], stacked(rights[0] + rights[1], lanes), preferred_element_type=jnp.float32)
            acc[slot, :, lanes] = part.astype(jnp.bfloat16)

    pair_tiles(
        left_buf, rights, weight_ref, grade_cols, right_grade_ref, scale, scores, slopes, inner, True, begin, finish
    )


def far_kernel(weight_ref, left_grade_ref, extra_ref, scale, near_inner, left_buf, acc, *refs):
    y_other, z_other, y_far, z_far, y_far_other, z_far_other = refs[:6]
    rights = (
        blocks(y_other, 0, 2) + blocks(z_other, 0, 2),
        blocks(y_far) + blocks(z_far) + blocks(y_far_other) + blocks(z_far_other),
    )
    out_ref, inner, lines, sent, tail, grade_cols, scores, slopes, right_grade_ref = refs[6:15]
    _, sent_sem, tail_sem = refs[15:]
    columns(left_grade_ref, grade_cols, range(4))
    right_grades(rights, right_grade_ref)
    inner[...] = near_inner[...]

    def home(slot):
        return pltpu.make_async_copy(sent.at[slot], out_ref.at[:, pl.ds(slot * PAIR, PAIR), :], sent_sem.at[slot])

    def finish(slot, slopes_ref):
        for chunk in range(8):
            source = (chunk + 4) % 8
            lanes = slice(source * PAIR, source * PAIR + PAIR)
            part = jnp.dot(slopes_ref[...], stacked(rights[0] + rights[1], lanes), preferred_element_type=jnp.float32)
            sent[slot, chunk] = (part + acc[slot, :, lanes].astype(jnp.float32)).astype(jnp.bfloat16)
        home(slot).start()
        lines[slot] = jnp.sum(inner[slot].T, axis=0, keepdims=True) * (1.0 / smoothing_divisor)

    pair_tiles(
        left_buf, rights, weight_ref, grade_cols, right_grade_ref, scale, scores, slopes, inner, False,
        lambda slot, quad: None, finish
    )
    total = jnp.concatenate([lines[k] for k in range(4)], axis=0)
    high = total.astype(jnp.bfloat16).astype(jnp.float32)
    last = jnp.concatenate([high, total - high, extra_ref[...]], axis=0).astype(jnp.bfloat16)
    for chunk in range(8):
        tail[chunk] = last
    tail_copy = pltpu.make_async_copy(tail, out_ref.at[:, pl.ds(1024, 16), :], tail_sem)
    tail_copy.start()
    for slot in range(4):
        home(slot).wait()
    tail_copy.wait()


BUFFERS = [
    pltpu.VMEM((4, PAIR, B), jnp.float32),
    pltpu.VMEM((2, PAIR, 2 * QUAD), jnp.float32),
    pltpu.VMEM((2, PAIR, 2 * QUAD), jnp.bfloat16),
    pltpu.VMEM((2, 1, QUAD), jnp.float32),
    pltpu.SemaphoreType.DMA((4,)),
]


def near_pass(spots, weight, left_grade, shards, arrays):
    wide = jax.ShapeDtypeStruct((4, PAIR, WIDTH), jnp.bfloat16)
    rows = jax.ShapeDtypeStruct((4, PAIR, B), jnp.float32)
    return pl.pallas_call(
        near_kernel,
        in_specs=[SMEM, VMEM, VMEM] + [ANY] * len(shards) + [VMEM] * len(arrays),
        out_specs=[VMEM] * 4,
        out_shape=[wide, wide, rows, rows],
        scratch_shapes=BUFFERS,
        compiler_params=pltpu.CompilerParams(vmem_limit_bytes=20 * 2**20),
        cost_estimate=pl.CostEstimate(flops=9 * 10**9, bytes_accessed=16 * 2**20, transcendentals=2**21),
        name="near_tiles",
    )(spots, weight, left_grade, *shards, *arrays)


def far_pass(*arrays):
    return pl.pallas_call(
        far_kernel,
        in_specs=[VMEM] * len(arrays),
        out_specs=ANY,
        out_shape=jax.ShapeDtypeStruct((8, 1040, PAIR), jnp.bfloat16),
        scratch_shapes=[
            pltpu.VMEM((4, PAIR, B), jnp.float32),
            pltpu.VMEM((4, 1, PAIR), jnp.float32),
            pltpu.VMEM((4, 8, PAIR, PAIR), jnp.bfloat16),
            pltpu.VMEM((8, 16, PAIR), jnp.bfloat16),
        ]
        + BUFFERS
        + [pltpu.SemaphoreType.DMA((4,)), pltpu.SemaphoreType.DMA],
        compiler_params=pltpu.CompilerParams(vmem_limit_bytes=24 * 2**20),
        cost_estimate=pl.CostEstimate(flops=8 * 10**9, bytes_accessed=24 * 2**20, transcendentals=2**21),
        name="far_tiles",
    )(*arrays)


def across(line, rows):
    column = jnp.broadcast_to(line, (B, rows)).T
    return jnp.concatenate([column, column], axis=1)


def weight_kernel(core_ref, back_ref, projected_ref, hidden_ref, grads_ref, give_ref, keep_ref, pre):
    tail = back_ref[:, 1024:, :].astype(jnp.float32)
    inner = jnp.sum(tail[:, 0:4] + tail[:, 4:8], axis=0)
    for part in range(8):
        at = slice(part * B, part * B + B)
        grads = back_ref[0, at, :].astype(jnp.float32)
        for source in range(1, 8):
            grads += back_ref[source, at, :].astype(jnp.float32)
        grads_ref[at, :] = grads
        norm = across(tail[part, 8:9, :B] + tail[part, 8:9, B:], B)
        half = part % 2 * B
        product = across(inner[part // 2 : part // 2 + 1, half : half + B], B)
        unit = projected_ref[at, :].astype(jnp.float32) / norm
        pre[at, :] = ((grads - unit * product) / norm).astype(jnp.bfloat16)
    mine = core_ref[0] == 0
    for k in range(4):
        product = lax.dot_general(
            hidden_ref[:, k * 896 : (k + 1) * 896], pre[...], (((0,), (0,)), ((), ())), preferred_element_type=jnp.float32
        )
        for j in range(2):
            even = product[2 * j * 224 : (2 * j + 1) * 224].astype(jnp.bfloat16)
            odd = product[(2 * j + 1) * 224 : (2 * j + 2) * 224].astype(jnp.bfloat16)
            keep_ref[2 * k + j] = jnp.where(mine, even, odd)
            give_ref[2 * k + j] = jnp.where(mine, odd, even)


def weight_pass(core, back, projected, hidden):
    chip = jax.ShapeDtypeStruct((8, 224, PAIR), jnp.bfloat16)
    return pl.pallas_call(
        weight_kernel,
        in_specs=[SMEM, VMEM, VMEM, VMEM],
        out_specs=[VMEM, VMEM, VMEM],
        out_shape=[jax.ShapeDtypeStruct((1024, PAIR), jnp.float32), chip, chip],
        scratch_shapes=[pltpu.VMEM((1024, PAIR), jnp.bfloat16)],
        compiler_params=pltpu.CompilerParams(vmem_limit_bytes=32 * 2**20),
        cost_estimate=pl.CostEstimate(flops=2 * 10**9, bytes_accessed=15 * 2**20, transcendentals=0),
        name="weight_terms",
    )(core, back, projected, hidden)


def own_kernel(grade_ref, came_ref, unit_ref, extra_ref, left_grade_ref):
    squares = jnp.zeros((B, B), jnp.float32)
    for k in range(8):
        for half in (0, B):
            part = came_ref[k, :B, half : half + B].astype(jnp.float32)
            squares += part * part
    norm = jnp.sqrt(jnp.sum(squares, axis=1, keepdims=True) + epsilon)
    wide = jnp.broadcast_to(norm, (B, B))
    for k in range(8):
        for half in (0, B):
            part = came_ref[k, :B, half : half + B].astype(jnp.float32) / wide
            unit_ref[:B, k * PAIR + half : k * PAIR + half + B] = (-part if k < 4 else part).astype(jnp.bfloat16)
    for k in range(4):
        lines = [came_ref[j, B:, :B].astype(jnp.float32)[0:1] for j in (2 * k, 2 * k + 1)]
        left_grade_ref[k] = jnp.concatenate(lines, axis=1)
    unit_ref[B:, :] = jnp.zeros((LONG - B, WIDTH), jnp.bfloat16)
    unit_ref[B:, :B] = jnp.broadcast_to(grade_ref[...], (LONG - B, B)).astype(jnp.bfloat16)
    line = wide.T[0:1]
    high = line.astype(jnp.bfloat16).astype(jnp.float32)
    extra_ref[...] = jnp.broadcast_to(jnp.concatenate([high, line - high], axis=1), (8, PAIR))


def own_pass(grades, came):
    return pl.pallas_call(
        own_kernel,
        in_specs=[whole(1, B), whole(8, LONG, PAIR)],
        out_specs=[whole(LONG, WIDTH), whole(8, PAIR), whole(4, 1, PAIR)],
        grid=(1,),
        out_shape=[
            jax.ShapeDtypeStruct((LONG, WIDTH), jnp.bfloat16),
            jax.ShapeDtypeStruct((8, PAIR), jnp.float32),
            jax.ShapeDtypeStruct((4, 1, PAIR), jnp.float32),
        ],
        compiler_params=pltpu.CompilerParams(vmem_limit_bytes=8 * 2**20),
        cost_estimate=pl.CostEstimate(flops=10**6, bytes_accessed=2**20, transcendentals=0),
        name="own_rows",
    )(grades, came)


def shards(hidden, projection, grades, pattern):
    y, zh, core, x, zl = (lax.axis_index(a) for a in AXES)
    col_here = x * 2 + zl

    grade_mine = grades.astype(jnp.bfloat16).reshape(1, B)
    projected = jnp.dot(hidden, projection, preferred_element_type=jnp.float32).astype(jnp.bfloat16)
    grade_rows = jnp.broadcast_to(jnp.tile(grade_mine, (1, 2)), (8, 16, PAIR))
    sent = jnp.concatenate([projected.reshape(8, B, PAIR), grade_rows], axis=1)
    came = lax.all_to_all(sent, COL, 0, 0, tiled=True)
    across_z = shift(projected, "zl", 1)
    below = shift(projected, "x", 1)
    above = shift(projected, "x", -1)

    both = (pattern + pattern.T).astype(jnp.float32)
    row_here = ((y * 2 + zh) * 2 + core) * 8
    home = lax.dynamic_slice_in_dim(both, row_here, 8, 0)
    right_ids = jnp.stack(
        [((((y + d) % 4) * 2 + (zh ^ z)) * 2 + (core ^ c)) * 8 + col_here for d, z, c in RIGHT]
    )
    right_pick = (jnp.arange(128)[:, None] == right_ids[None]).astype(jnp.float32)
    tiles = jnp.dot(home, right_pick, preferred_element_type=jnp.float32).reshape(4, 2, 4, 4)
    weight = jnp.repeat((tiles * (-smoothing_divisor / B)).transpose(2, 0, 1, 3), B, axis=3)
    spots = jnp.stack([((x + d) % 4 * 2 + (zl ^ z) + 4) % 8 for d, z in SHARDS]).astype(jnp.int32)
    came, across_z, below, above, weight, spots = lax.optimization_barrier(
        (came, across_z, below, above, weight, spots)
    )

    unit, extra, left_grade = own_pass(grade_mine.astype(jnp.float32), came)

    y_below = shift(unit, "y", 1)
    y_above = shift(unit, "y", -1)
    unit_z = shift(unit, "zh", 1)
    below_z = shift(across_z, "x", 1)
    above_z = shift(across_z, "x", -1)
    y_below, y_above, unit_z, unit, below, below_z, above_z, left_grade, extra = lax.optimization_barrier(
        (y_below, y_above, unit_z, unit, below, below_z, above_z, left_grade, extra)
    )
    z_below = shift(unit_z, "y", 1)
    z_above = shift(unit_z, "y", -1)
    far = shift(below, "x", 1)
    far_z = shift(above_z, "x", -1)
    other = shift(jnp.concatenate([unit, unit_z], axis=0), "core", 1)
    y_both = jnp.concatenate([y_above, y_below], axis=0)
    y_below, z_above, z_below, y_above, far, far_z, y_both = lax.optimization_barrier(
        (y_below, z_above, z_below, y_above, far, far_z, y_both)
    )
    y_far = shift(y_below, "y", 1)
    z_far = shift(z_above, "y", -1)
    y_other = shift(y_both, "core", 1)
    z_other = shift(jnp.concatenate([z_above, z_below], axis=0), "core", 1)

    left = [projected, across_z, below, below_z, above, above_z, far, far_z]
    nearby = [unit, unit_z, y_above, y_below, z_above, z_below]
    near_acc, left_rows, near_inner, scale = near_pass(spots, weight[:2], left_grade, left, nearby + [other])
    y_far, z_far, near_acc, near_inner = lax.optimization_barrier((y_far, z_far, near_acc, near_inner))
    beyond = [y_other, z_other, y_far, z_far, shift(y_far, "core", 1), shift(z_far, "core", 1)]
    sums = far_pass(weight[2:], left_grade, extra, scale, near_inner, left_rows, near_acc, *beyond)
    back = lax.all_to_all(sums, COL, 0, 0, tiled=True)

    grads, give, keep = weight_pass(core.astype(jnp.int32).reshape(1), back, projected, hidden)
    chip = (keep.astype(jnp.float32) + shift(give, "core", 1).astype(jnp.float32)).astype(jnp.bfloat16)
    gathered = lax.all_to_all(chip, ("y", "zh"), 0, 0, tiled=True)
    weight_grad = jnp.sum(gathered.astype(jnp.float32), axis=0)
    return grads, weight_grad


def solution(mesh):
    fine = Mesh(np.asarray(mesh.devices).reshape(SIZES), AXES)
    return jax.shard_map(
        shards,
        mesh=fine,
        in_specs=(P(ROW, None), P(None, COL), P(ROW + COL), P()),
        out_specs=(P(ROW, COL), P(ROW, COL)),
        check_vma=False,
    )
```

```python
import functools

import jax
import jax.numpy as jnp
import numpy as np
from jax import lax
from jax.experimental import pallas as pl
from jax.experimental.pallas import tpu as pltpu
from jax.sharding import Mesh, PartitionSpec as P

smoothing_divisor = 64.0
epsilon = 1e-06
AXES = ("y", "zh", "core", "x", "zl")
SIZES = (4, 2, 2, 4, 2)
ROW = ("y", "zh", "core")
COL = ("x", "zl")
B = 128
PAIR = 2 * B
QUAD = 4 * B
LONG = B + 16
WIDTH = 2048
ANY = pl.BlockSpec(memory_space=pltpu.HBM)
SMEM = pl.BlockSpec(memory_space=pltpu.SMEM)
VMEM = pl.BlockSpec(memory_space=pltpu.VMEM)

RIGHT = ((0, 0, 0), (0, 1, 0), (1, 0, 0), (3, 0, 0), (1, 1, 0), (3, 1, 0), (0, 0, 1), (0, 1, 1))
RIGHT += ((1, 0, 1), (3, 0, 1), (1, 1, 1), (3, 1, 1), (2, 0, 0), (2, 1, 0), (2, 0, 1), (2, 1, 1))
SHARDS = ((0, 0), (0, 1), (3, 0), (3, 1), (1, 0), (1, 1), (2, 0), (2, 1))


def shift(value, axis, by):
    size = SIZES[AXES.index(axis)]
    return lax.ppermute(value, axis, [(i, (i + by) % size) for i in range(size)])


def whole(*shape):
    return pl.BlockSpec(shape, lambda *_: (0,) * len(shape))


def blocks(ref, first=0, count=1):
    return [(ref, k * LONG) for k in range(first, first + count)]


def stacked(pieces, lanes=slice(None)):
    return jnp.concatenate([ref[first : first + B, lanes] for ref, first in pieces], axis=0)


def right_grades(rights, right_grade):
    for k, pieces in enumerate(rights):
        for j, (ref, first) in enumerate(pieces):
            line = ref[first + B : first + LONG, :B].astype(jnp.float32)[0:1]
            right_grade[k, :, j * B : (j + 1) * B] = line


def fetch_left(spot_ref, shards, slot, buffer, sem):
    for k, ref in enumerate(shards):
        lanes = pl.ds(pl.multiple_of(spot_ref[k] * PAIR, PAIR), PAIR)
        pltpu.make_async_copy(ref.at[pl.ds(slot * PAIR, PAIR), :], buffer.at[slot, :, lanes], sem).start()


def filled(buffer, sem):
    pltpu.make_async_copy(buffer, buffer, sem).wait()


def columns(left_grade_ref, grade_cols, slots):
    for slot in slots:
        grade_cols[slot] = jnp.broadcast_to(left_grade_ref[slot], (B, PAIR)).T


def score(left, right, scores):
    scores[...] = lax.dot_general(left[...], right, (((1,), (1,)), ((), ())), preferred_element_type=jnp.float32)


def slope(scores, weight, grade_cols, right_grade, scale, slopes, inner, first):
    for part in range(4):
        rows = slice(part * 64, part * 64 + 64)
        here = grade_cols[rows, :]
        scaled = scale[rows, :]
        total = None
        for lane in range(4):
            lanes = slice(lane * B, lane * B + B)
            value = scores[rows, lanes] * scaled
            label = jnp.clip(here - right_grade[:, lanes], -1.0, 1.0)
            step = label * weight[part // 2 : part // 2 + 1, lanes]
            grown = jnp.exp(label * value)
            one = (step * pltpu.reciprocal(1.0 + grown, approx=True)).astype(jnp.bfloat16)
            slopes[rows, lanes] = one
            term = one.astype(jnp.float32) * value
            total = term if total is None else total + term
        inner[rows, :] = total if first else inner[rows, :] + total


def quad_rows(quad, count=1):
    return pl.ds(quad * QUAD, count * QUAD)


def pair_tiles(left_buf, rights, weight_ref, grade_cols, right_grade_ref, scale, scores, slopes, inner, first, begin, finish):
    def ahead(slot, quad):
        begin(slot, quad)
        score(left_buf.at[slot], stacked(rights[quad]), scores.at[slot % 2, :, quad_rows(quad)])

    def arithmetic(slot, quad):
        slope(
            scores.at[slot % 2, :, quad_rows(quad)], weight_ref.at[quad, slot], grade_cols.at[slot],
            right_grade_ref.at[quad], scale.at[slot], slopes.at[slot % 2, :, quad_rows(quad)], inner.at[slot],
            first and quad == 0,
        )

    ahead(0, 0)
    ahead(0, 1)
    for slot in range(4):
        arithmetic(slot, 0)
        if slot < 3:
            ahead(slot + 1, 0)
        arithmetic(slot, 1)
        if slot < 3:
            ahead(slot + 1, 1)
        finish(slot, slopes.at[slot % 2])


def near_kernel(spot_ref, weight_ref, left_grade_ref, *refs):
    shards = refs[:8]
    unit, unit_z, y_above, y_below, z_above, z_below, other = refs[8:15]
    rights = (
        blocks(unit) + blocks(unit_z) + blocks(y_above) + blocks(y_below),
        blocks(z_above) + blocks(z_below) + blocks(other, 0, 2),
    )
    acc, left_buf, inner, scale, grade_cols, scores, slopes, right_grade_ref, left_sem = refs[15:]
    fetch_left(spot_ref, shards, 0, left_buf, left_sem.at[0])
    for slot in (1, 2, 3):
        fetch_left(spot_ref, shards, slot, left_buf, left_sem.at[slot])
    columns(left_grade_ref, grade_cols, range(4))
    right_grades(rights, right_grade_ref)

    def begin(slot, quad):
        if quad == 0:
            filled(left_buf.at[slot], left_sem.at[slot])
            squares = jnp.zeros((PAIR, B), jnp.float32)
            for chunk in range(16):
                part = left_buf[slot, :, chunk * B : (chunk + 1) * B].astype(jnp.float32)
                squares += part * part
            norm = jnp.sqrt(jnp.sum(squares, axis=1, keepdims=True) + epsilon)
            scale[slot] = jnp.broadcast_to(smoothing_divisor / norm, (PAIR, B))

    def finish(slot, slopes_ref):
        for chunk in range(8):
            lanes = slice(chunk * PAIR, chunk * PAIR + PAIR)
            part = jnp.dot(slopes_ref[...], stacked(rights[0] + rights[1], lanes), preferred_element_type=jnp.float32)
            acc[slot, :, lanes] = part.astype(jnp.bfloat16)

    pair_tiles(
        left_buf, rights, weight_ref, grade_cols, right_grade_ref, scale, scores, slopes, inner, True, begin, finish
    )


def far_kernel(weight_ref, left_grade_ref, extra_ref, scale, near_inner, left_buf, acc, *refs):
    y_other, z_other, y_far, z_far, y_far_other, z_far_other = refs[:6]
    rights = (
        blocks(y_other, 0, 2) + blocks(z_other, 0, 2),
        blocks(y_far) + blocks(z_far) + blocks(y_far_other) + blocks(z_far_other),
    )
    out_ref, inner, lines, grade_cols, scores, slopes, right_grade_ref, _ = refs[6:]
    columns(left_grade_ref, grade_cols, range(4))
    right_grades(rights, right_grade_ref)
    inner[...] = near_inner[...]

    def finish(slot, slopes_ref):
        for chunk in range(8):
            source = (chunk + 4) % 8
            lanes = slice(source * PAIR, source * PAIR + PAIR)
            part = jnp.dot(slopes_ref[...], stacked(rights[0] + rights[1], lanes), preferred_element_type=jnp.float32)
            out_ref[chunk, slot * PAIR : (slot + 1) * PAIR, :] = (part + acc[slot, :, lanes].astype(jnp.float32)).astype(jnp.bfloat16)
        lines[slot] = jnp.sum(inner[slot].T, axis=0, keepdims=True) * (1.0 / smoothing_divisor)

    pair_tiles(
        left_buf, rights, weight_ref, grade_cols, right_grade_ref, scale, scores, slopes, inner, False,
        lambda slot, quad: None, finish
    )
    total = jnp.concatenate([lines[k] for k in range(4)], axis=0)
    high = total.astype(jnp.bfloat16).astype(jnp.float32)
    last = jnp.concatenate([high, total - high, extra_ref[...]], axis=0).astype(jnp.bfloat16)
    for chunk in range(8):
        out_ref[chunk, 1024:, :] = last


BUFFERS = [
    pltpu.VMEM((4, PAIR, B), jnp.float32),
    pltpu.VMEM((2, PAIR, 2 * QUAD), jnp.float32),
    pltpu.VMEM((2, PAIR, 2 * QUAD), jnp.bfloat16),
    pltpu.VMEM((2, 1, QUAD), jnp.float32),
    pltpu.SemaphoreType.DMA((4,)),
]


def near_pass(spots, weight, left_grade, shards, arrays):
    wide = jax.ShapeDtypeStruct((4, PAIR, WIDTH), jnp.bfloat16)
    rows = jax.ShapeDtypeStruct((4, PAIR, B), jnp.float32)
    return pl.pallas_call(
        near_kernel,
        in_specs=[SMEM, VMEM, VMEM] + [ANY] * len(shards) + [VMEM] * len(arrays),
        out_specs=[VMEM] * 4,
        out_shape=[wide, wide, rows, rows],
        scratch_shapes=BUFFERS,
        compiler_params=pltpu.CompilerParams(vmem_limit_bytes=20 * 2**20),
        cost_estimate=pl.CostEstimate(flops=9 * 10**9, bytes_accessed=16 * 2**20, transcendentals=2**21),
        name="near_tiles",
    )(spots, weight, left_grade, *shards, *arrays)


def far_pass(*arrays):
    return pl.pallas_call(
        far_kernel,
        in_specs=[VMEM] * len(arrays),
        out_specs=VMEM,
        out_shape=jax.ShapeDtypeStruct((8, 1040, PAIR), jnp.bfloat16),
        scratch_shapes=[pltpu.VMEM((4, PAIR, B), jnp.float32), pltpu.VMEM((4, 1, PAIR), jnp.float32)] + BUFFERS,
        compiler_params=pltpu.CompilerParams(vmem_limit_bytes=24 * 2**20),
        cost_estimate=pl.CostEstimate(flops=8 * 10**9, bytes_accessed=24 * 2**20, transcendentals=2**21),
        name="far_tiles",
    )(*arrays)


def across(line, rows):
    column = jnp.broadcast_to(line, (B, rows)).T
    return jnp.concatenate([column, column], axis=1)


def weight_kernel(core_ref, back_ref, projected_ref, hidden_ref, grads_ref, give_ref, keep_ref, pre):
    tail = back_ref[:, 1024:, :].astype(jnp.float32)
    inner = jnp.sum(tail[:, 0:4] + tail[:, 4:8], axis=0)
    for part in range(8):
        at = slice(part * B, part * B + B)
        grads = back_ref[0, at, :].astype(jnp.float32)
        for source in range(1, 8):
            grads += back_ref[source, at, :].astype(jnp.float32)
        grads_ref[at, :] = grads
        norm = across(tail[part, 8:9, :B] + tail[part, 8:9, B:], B)
        half = part % 2 * B
        product = across(inner[part // 2 : part // 2 + 1, half : half + B], B)
        unit = projected_ref[at, :].astype(jnp.float32) / norm
        pre[at, :] = ((grads - unit * product) / norm).astype(jnp.bfloat16)
    mine = core_ref[0] == 0
    for k in range(4):
        product = lax.dot_general(
            hidden_ref[:, k * 896 : (k + 1) * 896], pre[...], (((0,), (0,)), ((), ())), preferred_element_type=jnp.float32
        )
        for j in range(2):
            even = product[2 * j * 224 : (2 * j + 1) * 224].astype(jnp.bfloat16)
            odd = product[(2 * j + 1) * 224 : (2 * j + 2) * 224].astype(jnp.bfloat16)
            keep_ref[2 * k + j] = jnp.where(mine, even, odd)
            give_ref[2 * k + j] = jnp.where(mine, odd, even)


def weight_pass(core, back, projected, hidden):
    chip = jax.ShapeDtypeStruct((8, 224, PAIR), jnp.bfloat16)
    return pl.pallas_call(
        weight_kernel,
        in_specs=[SMEM, VMEM, VMEM, VMEM],
        out_specs=[VMEM, VMEM, VMEM],
        out_shape=[jax.ShapeDtypeStruct((1024, PAIR), jnp.float32), chip, chip],
        scratch_shapes=[pltpu.VMEM((1024, PAIR), jnp.bfloat16)],
        compiler_params=pltpu.CompilerParams(vmem_limit_bytes=32 * 2**20),
        cost_estimate=pl.CostEstimate(flops=2 * 10**9, bytes_accessed=15 * 2**20, transcendentals=0),
        name="weight_terms",
    )(core, back, projected, hidden)


def own_kernel(grade_ref, came_ref, unit_ref, extra_ref, left_grade_ref):
    squares = jnp.zeros((B, B), jnp.float32)
    for k in range(8):
        for half in (0, B):
            part = came_ref[k, :B, half : half + B].astype(jnp.float32)
            squares += part * part
    norm = jnp.sqrt(jnp.sum(squares, axis=1, keepdims=True) + epsilon)
    wide = jnp.broadcast_to(norm, (B, B))
    for k in range(8):
        for half in (0, B):
            part = came_ref[k, :B, half : half + B].astype(jnp.float32) / wide
            unit_ref[:B, k * PAIR + half : k * PAIR + half + B] = (-part if k < 4 else part).astype(jnp.bfloat16)
    for k in range(4):
        lines = [came_ref[j, B:, :B].astype(jnp.float32)[0:1] for j in (2 * k, 2 * k + 1)]
        left_grade_ref[k] = jnp.concatenate(lines, axis=1)
    unit_ref[B:, :] = jnp.zeros((LONG - B, WIDTH), jnp.bfloat16)
    unit_ref[B:, :B] = jnp.broadcast_to(grade_ref[...], (LONG - B, B)).astype(jnp.bfloat16)
    line = wide.T[0:1]
    high = line.astype(jnp.bfloat16).astype(jnp.float32)
    extra_ref[...] = jnp.broadcast_to(jnp.concatenate([high, line - high], axis=1), (8, PAIR))


def own_pass(grades, came):
    return pl.pallas_call(
        own_kernel,
        in_specs=[whole(1, B), whole(8, LONG, PAIR)],
        out_specs=[whole(LONG, WIDTH), whole(8, PAIR), whole(4, 1, PAIR)],
        grid=(1,),
        out_shape=[
            jax.ShapeDtypeStruct((LONG, WIDTH), jnp.bfloat16),
            jax.ShapeDtypeStruct((8, PAIR), jnp.float32),
            jax.ShapeDtypeStruct((4, 1, PAIR), jnp.float32),
        ],
        compiler_params=pltpu.CompilerParams(vmem_limit_bytes=8 * 2**20),
        cost_estimate=pl.CostEstimate(flops=10**6, bytes_accessed=2**20, transcendentals=0),
        name="own_rows",
    )(grades, came)


def shards(hidden, projection, grades, pattern):
    y, zh, core, x, zl = (lax.axis_index(a) for a in AXES)
    col_here = x * 2 + zl

    grade_mine = grades.astype(jnp.bfloat16).reshape(1, B)
    projected = jnp.dot(hidden, projection, preferred_element_type=jnp.float32).astype(jnp.bfloat16)
    grade_rows = jnp.broadcast_to(jnp.tile(grade_mine, (1, 2)), (8, 16, PAIR))
    sent = jnp.concatenate([projected.reshape(8, B, PAIR), grade_rows], axis=1)
    came = lax.all_to_all(sent, COL, 0, 0, tiled=True)
    across_z = shift(projected, "zl", 1)
    below = shift(projected, "x", 1)
    above = shift(projected, "x", -1)

    both = (pattern + pattern.T).astype(jnp.float32)
    row_here = ((y * 2 + zh) * 2 + core) * 8
    home = lax.dynamic_slice_in_dim(both, row_here, 8, 0)
    right_ids = jnp.stack(
        [((((y + d) % 4) * 2 + (zh ^ z)) * 2 + (core ^ c)) * 8 + col_here for d, z, c in RIGHT]
    )
    right_pick = (jnp.arange(128)[:, None] == right_ids[None]).astype(jnp.float32)
    tiles = jnp.dot(home, right_pick, preferred_element_type=jnp.float32).reshape(4, 2, 4, 4)
    weight = jnp.repeat((tiles * (-smoothing_divisor / B)).transpose(2, 0, 1, 3), B, axis=3)
    spots = jnp.stack([((x + d) % 4 * 2 + (zl ^ z) + 4) % 8 for d, z in SHARDS]).astype(jnp.int32)
    came, across_z, below, above, weight, spots = lax.optimization_barrier(
        (came, across_z, below, above, weight, spots)
    )

    unit, extra, left_grade = own_pass(grade_mine.astype(jnp.float32), came)

    y_below = shift(unit, "y", 1)
    y_above = shift(unit, "y", -1)
    unit_z = shift(unit, "zh", 1)
    below_z = shift(across_z, "x", 1)
    above_z = shift(across_z, "x", -1)
    y_below, y_above, unit_z, unit, below, below_z, above_z, left_grade, extra = lax.optimization_barrier(
        (y_below, y_above, unit_z, unit, below, below_z, above_z, left_grade, extra)
    )
    z_below = shift(unit_z, "y", 1)
    z_above = shift(unit_z, "y", -1)
    far = shift(below, "x", 1)
    far_z = shift(above_z, "x", -1)
    other = shift(jnp.concatenate([unit, unit_z], axis=0), "core", 1)
    y_both = jnp.concatenate([y_above, y_below], axis=0)
    y_below, z_above, z_below, y_above, far, far_z, y_both = lax.optimization_barrier(
        (y_below, z_above, z_below, y_above, far, far_z, y_both)
    )
    y_far = shift(y_below, "y", 1)
    z_far = shift(z_above, "y", -1)
    y_other = shift(y_both, "core", 1)
    z_other = shift(jnp.concatenate([z_above, z_below], axis=0), "core", 1)

    left = [projected, across_z, below, below_z, above, above_z, far, far_z]
    nearby = [unit, unit_z, y_above, y_below, z_above, z_below]
    near_acc, left_rows, near_inner, scale = near_pass(spots, weight[:2], left_grade, left, nearby + [other])
    y_far, z_far, near_acc, near_inner = lax.optimization_barrier((y_far, z_far, near_acc, near_inner))
    beyond = [y_other, z_other, y_far, z_far, shift(y_far, "core", 1), shift(z_far, "core", 1)]
    sums = far_pass(weight[2:], left_grade, extra, scale, near_inner, left_rows, near_acc, *beyond)
    back = lax.all_to_all(sums, COL, 0, 0, tiled=True)

    grads, give, keep = weight_pass(core.astype(jnp.int32).reshape(1), back, projected, hidden)
    chip = (keep.astype(jnp.float32) + shift(give, "core", 1).astype(jnp.float32)).astype(jnp.bfloat16)
    gathered = lax.all_to_all(chip, ("y", "zh"), 0, 0, tiled=True)
    weight_grad = jnp.sum(gathered.astype(jnp.float32), axis=0)
    return grads, weight_grad


def solution(mesh):
    fine = Mesh(np.asarray(mesh.devices).reshape(SIZES), AXES)
    return jax.shard_map(
        shards,
        mesh=fine,
        in_specs=(P(ROW, None), P(None, COL), P(ROW + COL), P()),
        out_specs=(P(ROW, COL), P(ROW, COL)),
        check_vma=False,
    )
```

```python
import functools

import jax
import jax.numpy as jnp
import numpy as np
from jax import lax
from jax.experimental import pallas as pl
from jax.experimental.pallas import tpu as pltpu
from jax.sharding import Mesh, PartitionSpec as P

smoothing_divisor = 64.0
epsilon = 1e-06
AXES = ("y", "zh", "core", "x", "zl")
SIZES = (4, 2, 2, 4, 2)
ROW = ("y", "zh", "core")
COL = ("x", "zl")
B = 128
PAIR = 2 * B
QUAD = 4 * B
LONG = B + 16
WIDTH = 2048
ANY = pl.BlockSpec(memory_space=pltpu.HBM)
SMEM = pl.BlockSpec(memory_space=pltpu.SMEM)
VMEM = pl.BlockSpec(memory_space=pltpu.VMEM)

RIGHT = ((0, 0, 0), (0, 1, 0), (1, 0, 0), (3, 0, 0), (1, 1, 0), (3, 1, 0), (0, 0, 1), (0, 1, 1))
RIGHT += ((1, 0, 1), (3, 0, 1), (1, 1, 1), (3, 1, 1), (2, 0, 0), (2, 1, 0), (2, 0, 1), (2, 1, 1))
SHARDS = ((0, 0), (0, 1), (3, 0), (3, 1), (1, 0), (1, 1), (2, 0), (2, 1))


def shift(value, axis, by):
    size = SIZES[AXES.index(axis)]
    return lax.ppermute(value, axis, [(i, (i + by) % size) for i in range(size)])


def whole(*shape):
    return pl.BlockSpec(shape, lambda *_: (0,) * len(shape))


def blocks(ref, first=0, count=1):
    return [(ref, k * LONG) for k in range(first, first + count)]


def stacked(pieces, lanes=slice(None)):
    return jnp.concatenate([ref[first : first + B, lanes] for ref, first in pieces], axis=0)


def right_grades(rights, right_grade):
    for k, pieces in enumerate(rights):
        for j, (ref, first) in enumerate(pieces):
            line = ref[first + B : first + LONG, :B].astype(jnp.float32)[0:1]
            right_grade[k, :, j * B : (j + 1) * B] = line


def fetch_left(spot_ref, shards, slot, buffer, sem):
    for k, ref in enumerate(shards):
        lanes = pl.ds(pl.multiple_of(spot_ref[k] * PAIR, PAIR), PAIR)
        pltpu.make_async_copy(ref.at[pl.ds(slot * PAIR, PAIR), :], buffer.at[slot, :, lanes], sem).start()


def filled(buffer, sem):
    pltpu.make_async_copy(buffer, buffer, sem).wait()


def columns(left_grade_ref, grade_cols, slots):
    for slot in slots:
        grade_cols[slot] = jnp.broadcast_to(left_grade_ref[slot], (B, PAIR)).T


def score(left, right, scores):
    scores[...] = lax.dot_general(left[...], right, (((1,), (1,)), ((), ())), preferred_element_type=jnp.float32)


def slope(scores, weight, grade_cols, right_grade, scale, slopes, inner, first):
    for part in range(4):
        rows = slice(part * 64, part * 64 + 64)
        here = grade_cols[rows, :]
        scaled = scale[rows, :]
        total = None
        for lane in range(4):
            lanes = slice(lane * B, lane * B + B)
            value = scores[rows, lanes] * scaled
            label = jnp.clip(here - right_grade[:, lanes], -1.0, 1.0)
            step = label * weight[part // 2 : part // 2 + 1, lanes]
            grown = jnp.exp(label * value)
            one = (step * pltpu.reciprocal(1.0 + grown, approx=True)).astype(jnp.bfloat16)
            slopes[rows, lanes] = one
            term = one.astype(jnp.float32) * value
            total = term if total is None else total + term
        inner[rows, :] = total if first else inner[rows, :] + total


def quad_rows(quad, count=1):
    return pl.ds(quad * QUAD, count * QUAD)


def pair_tiles(left_buf, rights, weight_ref, grade_cols, right_grade_ref, scale, scores, slopes, inner, first, begin, finish):
    def ahead(slot, quad):
        begin(slot, quad)
        score(left_buf.at[slot], stacked(rights[quad]), scores.at[slot % 2, :, quad_rows(quad)])

    def arithmetic(slot, quad):
        slope(
            scores.at[slot % 2, :, quad_rows(quad)], weight_ref.at[quad, slot], grade_cols.at[slot],
            right_grade_ref.at[quad], scale.at[slot], slopes.at[slot % 2, :, quad_rows(quad)], inner.at[slot],
            first and quad == 0,
        )

    ahead(0, 0)
    ahead(0, 1)
    for slot in range(4):
        arithmetic(slot, 0)
        if slot < 3:
            ahead(slot + 1, 0)
        arithmetic(slot, 1)
        if slot < 3:
            ahead(slot + 1, 1)
        finish(slot, slopes.at[slot % 2])


def near_kernel(spot_ref, weight_ref, left_grade_ref, *refs):
    shards = refs[:8]
    unit, unit_z, y_above, y_below, z_above, z_below, other = refs[8:15]
    rights = (
        blocks(unit) + blocks(unit_z) + blocks(y_above) + blocks(y_below),
        blocks(z_above) + blocks(z_below) + blocks(other, 0, 2),
    )
    acc, left_buf, inner, scale, grade_cols, scores, slopes, right_grade_ref, left_sem = refs[15:]
    fetch_left(spot_ref, shards, 0, left_buf, left_sem.at[0])
    columns(left_grade_ref, grade_cols, range(4))
    right_grades(rights, right_grade_ref)

    def begin(slot, quad):
        if quad == 0:
            filled(left_buf.at[slot], left_sem.at[slot])
            if slot == 0:
                for later in (1, 2, 3):
                    fetch_left(spot_ref, shards, later, left_buf, left_sem.at[later])
        else:
            squares = jnp.zeros((PAIR, B), jnp.float32)
            for chunk in range(16):
                part = left_buf[slot, :, chunk * B : (chunk + 1) * B].astype(jnp.float32)
                squares += part * part
            norm = jnp.sqrt(jnp.sum(squares, axis=1, keepdims=True) + epsilon)
            scale[slot] = jnp.broadcast_to(smoothing_divisor / norm, (PAIR, B))

    def finish(slot, slopes_ref):
        for chunk in range(8):
            lanes = slice(chunk * PAIR, chunk * PAIR + PAIR)
            part = jnp.dot(slopes_ref[...], stacked(rights[0] + rights[1], lanes), preferred_element_type=jnp.float32)
            acc[slot, :, lanes] = part.astype(jnp.bfloat16)

    pair_tiles(
        left_buf, rights, weight_ref, grade_cols, right_grade_ref, scale, scores, slopes, inner, True, begin, finish
    )


def far_kernel(weight_ref, left_grade_ref, extra_ref, scale, near_inner, left_buf, acc, *refs):
    y_other, z_other, y_far, z_far, y_far_other, z_far_other = refs[:6]
    rights = (
        blocks(y_other, 0, 2) + blocks(z_other, 0, 2),
        blocks(y_far) + blocks(z_far) + blocks(y_far_other) + blocks(z_far_other),
    )
    out_ref, inner, lines, grade_cols, scores, slopes, right_grade_ref, _ = refs[6:]
    columns(left_grade_ref, grade_cols, range(4))
    right_grades(rights, right_grade_ref)
    inner[...] = near_inner[...]

    def finish(slot, slopes_ref):
        for chunk in range(8):
            source = (chunk + 4) % 8
            lanes = slice(source * PAIR, source * PAIR + PAIR)
            part = jnp.dot(slopes_ref[...], stacked(rights[0] + rights[1], lanes), preferred_element_type=jnp.float32)
            out_ref[chunk, slot * PAIR : (slot + 1) * PAIR, :] = (part + acc[slot, :, lanes].astype(jnp.float32)).astype(jnp.bfloat16)
        lines[slot] = jnp.sum(inner[slot].T, axis=0, keepdims=True) * (1.0 / smoothing_divisor)

    pair_tiles(
        left_buf, rights, weight_ref, grade_cols, right_grade_ref, scale, scores, slopes, inner, False,
        lambda slot, quad: None, finish
    )
    total = jnp.concatenate([lines[k] for k in range(4)], axis=0)
    high = total.astype(jnp.bfloat16).astype(jnp.float32)
    last = jnp.concatenate([high, total - high, extra_ref[...]], axis=0).astype(jnp.bfloat16)
    for chunk in range(8):
        out_ref[chunk, 1024:, :] = last


BUFFERS = [
    pltpu.VMEM((4, PAIR, B), jnp.float32),
    pltpu.VMEM((2, PAIR, 2 * QUAD), jnp.float32),
    pltpu.VMEM((2, PAIR, 2 * QUAD), jnp.bfloat16),
    pltpu.VMEM((2, 1, QUAD), jnp.float32),
    pltpu.SemaphoreType.DMA((4,)),
]


def near_pass(spots, weight, left_grade, shards, arrays):
    wide = jax.ShapeDtypeStruct((4, PAIR, WIDTH), jnp.bfloat16)
    rows = jax.ShapeDtypeStruct((4, PAIR, B), jnp.float32)
    return pl.pallas_call(
        near_kernel,
        in_specs=[SMEM, VMEM, VMEM] + [ANY] * len(shards) + [VMEM] * len(arrays),
        out_specs=[VMEM] * 4,
        out_shape=[wide, wide, rows, rows],
        scratch_shapes=BUFFERS,
        compiler_params=pltpu.CompilerParams(vmem_limit_bytes=20 * 2**20),
        cost_estimate=pl.CostEstimate(flops=9 * 10**9, bytes_accessed=16 * 2**20, transcendentals=2**21),
        name="near_tiles",
    )(spots, weight, left_grade, *shards, *arrays)


def far_pass(*arrays):
    return pl.pallas_call(
        far_kernel,
        in_specs=[VMEM] * len(arrays),
        out_specs=VMEM,
        out_shape=jax.ShapeDtypeStruct((8, 1040, PAIR), jnp.bfloat16),
        scratch_shapes=[pltpu.VMEM((4, PAIR, B), jnp.float32), pltpu.VMEM((4, 1, PAIR), jnp.float32)] + BUFFERS,
        compiler_params=pltpu.CompilerParams(vmem_limit_bytes=24 * 2**20),
        cost_estimate=pl.CostEstimate(flops=8 * 10**9, bytes_accessed=24 * 2**20, transcendentals=2**21),
        name="far_tiles",
    )(*arrays)


def across(line, rows):
    column = jnp.broadcast_to(line, (B, rows)).T
    return jnp.concatenate([column, column], axis=1)


def weight_kernel(core_ref, back_ref, projected_ref, hidden_ref, grads_ref, give_ref, keep_ref, pre):
    tail = back_ref[:, 1024:, :].astype(jnp.float32)
    inner = jnp.sum(tail[:, 0:4] + tail[:, 4:8], axis=0)
    for part in range(8):
        at = slice(part * B, part * B + B)
        grads = back_ref[0, at, :].astype(jnp.float32)
        for source in range(1, 8):
            grads += back_ref[source, at, :].astype(jnp.float32)
        grads_ref[at, :] = grads
        norm = across(tail[part, 8:9, :B] + tail[part, 8:9, B:], B)
        half = part % 2 * B
        product = across(inner[part // 2 : part // 2 + 1, half : half + B], B)
        unit = projected_ref[at, :].astype(jnp.float32) / norm
        pre[at, :] = ((grads - unit * product) / norm).astype(jnp.bfloat16)
    mine = core_ref[0] == 0
    for k in range(4):
        product = lax.dot_general(
            hidden_ref[:, k * 896 : (k + 1) * 896], pre[...], (((0,), (0,)), ((), ())), preferred_element_type=jnp.float32
        )
        for j in range(2):
            even = product[2 * j * 224 : (2 * j + 1) * 224].astype(jnp.bfloat16)
            odd = product[(2 * j + 1) * 224 : (2 * j + 2) * 224].astype(jnp.bfloat16)
            keep_ref[2 * k + j] = jnp.where(mine, even, odd)
            give_ref[2 * k + j] = jnp.where(mine, odd, even)


def weight_pass(core, back, projected, hidden):
    chip = jax.ShapeDtypeStruct((8, 224, PAIR), jnp.bfloat16)
    return pl.pallas_call(
        weight_kernel,
        in_specs=[SMEM, VMEM, VMEM, VMEM],
        out_specs=[VMEM, VMEM, VMEM],
        out_shape=[jax.ShapeDtypeStruct((1024, PAIR), jnp.float32), chip, chip],
        scratch_shapes=[pltpu.VMEM((1024, PAIR), jnp.bfloat16)],
        compiler_params=pltpu.CompilerParams(vmem_limit_bytes=32 * 2**20),
        cost_estimate=pl.CostEstimate(flops=2 * 10**9, bytes_accessed=15 * 2**20, transcendentals=0),
        name="weight_terms",
    )(core, back, projected, hidden)


def own_kernel(grade_ref, came_ref, unit_ref, extra_ref, left_grade_ref):
    squares = jnp.zeros((B, B), jnp.float32)
    for k in range(8):
        for half in (0, B):
            part = came_ref[k, :B, half : half + B].astype(jnp.float32)
            squares += part * part
    norm = jnp.sqrt(jnp.sum(squares, axis=1, keepdims=True) + epsilon)
    wide = jnp.broadcast_to(norm, (B, B))
    for k in range(8):
        for half in (0, B):
            part = came_ref[k, :B, half : half + B].astype(jnp.float32) / wide
            unit_ref[:B, k * PAIR + half : k * PAIR + half + B] = (-part if k < 4 else part).astype(jnp.bfloat16)
    for k in range(4):
        lines = [came_ref[j, B:, :B].astype(jnp.float32)[0:1] for j in (2 * k, 2 * k + 1)]
        left_grade_ref[k] = jnp.concatenate(lines, axis=1)
    unit_ref[B:, :] = jnp.zeros((LONG - B, WIDTH), jnp.bfloat16)
    unit_ref[B:, :B] = jnp.broadcast_to(grade_ref[...], (LONG - B, B)).astype(jnp.bfloat16)
    line = wide.T[0:1]
    high = line.astype(jnp.bfloat16).astype(jnp.float32)
    extra_ref[...] = jnp.broadcast_to(jnp.concatenate([high, line - high], axis=1), (8, PAIR))


def own_pass(grades, came):
    return pl.pallas_call(
        own_kernel,
        in_specs=[whole(1, B), whole(8, LONG, PAIR)],
        out_specs=[whole(LONG, WIDTH), whole(8, PAIR), whole(4, 1, PAIR)],
        grid=(1,),
        out_shape=[
            jax.ShapeDtypeStruct((LONG, WIDTH), jnp.bfloat16),
            jax.ShapeDtypeStruct((8, PAIR), jnp.float32),
            jax.ShapeDtypeStruct((4, 1, PAIR), jnp.float32),
        ],
        compiler_params=pltpu.CompilerParams(vmem_limit_bytes=8 * 2**20),
        cost_estimate=pl.CostEstimate(flops=10**6, bytes_accessed=2**20, transcendentals=0),
        name="own_rows",
    )(grades, came)


def shards(hidden, projection, grades, pattern):
    y, zh, core, x, zl = (lax.axis_index(a) for a in AXES)
    col_here = x * 2 + zl

    grade_mine = grades.astype(jnp.bfloat16).reshape(1, B)
    projected = jnp.dot(hidden, projection, preferred_element_type=jnp.float32).astype(jnp.bfloat16)
    grade_rows = jnp.broadcast_to(jnp.tile(grade_mine, (1, 2)), (8, 16, PAIR))
    sent = jnp.concatenate([projected.reshape(8, B, PAIR), grade_rows], axis=1)
    came = lax.all_to_all(sent, COL, 0, 0, tiled=True)
    across_z = shift(projected, "zl", 1)
    below = shift(projected, "x", 1)
    above = shift(projected, "x", -1)

    both = (pattern + pattern.T).astype(jnp.float32)
    row_here = ((y * 2 + zh) * 2 + core) * 8
    home = lax.dynamic_slice_in_dim(both, row_here, 8, 0)
    right_ids = jnp.stack(
        [((((y + d) % 4) * 2 + (zh ^ z)) * 2 + (core ^ c)) * 8 + col_here for d, z, c in RIGHT]
    )
    right_pick = (jnp.arange(128)[:, None] == right_ids[None]).astype(jnp.float32)
    tiles = jnp.dot(home, right_pick, preferred_element_type=jnp.float32).reshape(4, 2, 4, 4)
    weight = jnp.repeat((tiles * (-smoothing_divisor / B)).transpose(2, 0, 1, 3), B, axis=3)
    spots = jnp.stack([((x + d) % 4 * 2 + (zl ^ z) + 4) % 8 for d, z in SHARDS]).astype(jnp.int32)
    came, across_z, below, above, weight, spots = lax.optimization_barrier(
        (came, across_z, below, above, weight, spots)
    )

    unit, extra, left_grade = own_pass(grade_mine.astype(jnp.float32), came)

    y_below = shift(unit, "y", 1)
    y_above = shift(unit, "y", -1)
    unit_z = shift(unit, "zh", 1)
    below_z = shift(across_z, "x", 1)
    above_z = shift(across_z, "x", -1)
    y_below, y_above, unit_z, unit, below, below_z, above_z, left_grade, extra = lax.optimization_barrier(
        (y_below, y_above, unit_z, unit, below, below_z, above_z, left_grade, extra)
    )
    z_below = shift(unit_z, "y", 1)
    z_above = shift(unit_z, "y", -1)
    far = shift(below, "x", 1)
    far_z = shift(above_z, "x", -1)
    other = shift(jnp.concatenate([unit, unit_z], axis=0), "core", 1)
    y_both = jnp.concatenate([y_above, y_below], axis=0)
    y_below, z_above, z_below, y_above, far, far_z, y_both = lax.optimization_barrier(
        (y_below, z_above, z_below, y_above, far, far_z, y_both)
    )
    y_far = shift(y_below, "y", 1)
    z_far = shift(z_above, "y", -1)
    y_other = shift(y_both, "core", 1)
    z_other = shift(jnp.concatenate([z_above, z_below], axis=0), "core", 1)

    left = [projected, across_z, below, below_z, above, above_z, far, far_z]
    nearby = [unit, unit_z, y_above, y_below, z_above, z_below]
    near_acc, left_rows, near_inner, scale = near_pass(spots, weight[:2], left_grade, left, nearby + [other])
    y_far, z_far, near_acc, near_inner = lax.optimization_barrier((y_far, z_far, near_acc, near_inner))
    beyond = [y_other, z_other, y_far, z_far, shift(y_far, "core", 1), shift(z_far, "core", 1)]
    sums = far_pass(weight[2:], left_grade, extra, scale, near_inner, left_rows, near_acc, *beyond)
    back = lax.all_to_all(sums, COL, 0, 0, tiled=True)

    grads, give, keep = weight_pass(core.astype(jnp.int32).reshape(1), back, projected, hidden)
    chip = (keep.astype(jnp.float32) + shift(give, "core", 1).astype(jnp.float32)).astype(jnp.bfloat16)
    gathered = lax.all_to_all(chip, ("y", "zh"), 0, 0, tiled=True)
    weight_grad = jnp.sum(gathered.astype(jnp.float32), axis=0)
    return grads, weight_grad


def solution(mesh):
    fine = Mesh(np.asarray(mesh.devices).reshape(SIZES), AXES)
    return jax.shard_map(
        shards,
        mesh=fine,
        in_specs=(P(ROW, None), P(None, COL), P(ROW + COL), P()),
        out_specs=(P(ROW, COL), P(ROW, COL)),
        check_vma=False,
    )
```

```python
import functools

import jax
import jax.numpy as jnp
import numpy as np
from jax import lax
from jax.experimental import pallas as pl
from jax.experimental.pallas import tpu as pltpu
from jax.sharding import Mesh, PartitionSpec as P

smoothing_divisor = 64.0
epsilon = 1e-06
AXES = ("y", "zh", "core", "x", "zl")
SIZES = (4, 2, 2, 4, 2)
ROW = ("y", "zh", "core")
COL = ("x", "zl")
B = 128
PAIR = 2 * B
QUAD = 4 * B
LONG = B + 16
WIDTH = 2048
ANY = pl.BlockSpec(memory_space=pltpu.HBM)
SMEM = pl.BlockSpec(memory_space=pltpu.SMEM)
VMEM = pl.BlockSpec(memory_space=pltpu.VMEM)

RIGHT = ((0, 0, 0), (0, 1, 0), (1, 0, 0), (3, 0, 0), (1, 1, 0), (3, 1, 0), (0, 0, 1), (0, 1, 1))
RIGHT += ((1, 0, 1), (3, 0, 1), (1, 1, 1), (3, 1, 1), (2, 0, 0), (2, 1, 0), (2, 0, 1), (2, 1, 1))
SHARDS = ((0, 0), (0, 1), (3, 0), (3, 1), (1, 0), (1, 1), (2, 0), (2, 1))


def shift(value, axis, by):
    size = SIZES[AXES.index(axis)]
    return lax.ppermute(value, axis, [(i, (i + by) % size) for i in range(size)])


def whole(*shape):
    return pl.BlockSpec(shape, lambda *_: (0,) * len(shape))


def blocks(ref, first=0, count=1):
    return [(ref, k * LONG) for k in range(first, first + count)]


def stacked(pieces, lanes=slice(None)):
    return jnp.concatenate([ref[first : first + B, lanes] for ref, first in pieces], axis=0)


def right_grades(rights, right_grade):
    for k, pieces in enumerate(rights):
        for j, (ref, first) in enumerate(pieces):
            line = ref[first + B : first + LONG, :B].astype(jnp.float32)[0:1]
            right_grade[k, :, j * B : (j + 1) * B] = line


def fetch_left(spot_ref, shards, slot, buffer, sem):
    for k, ref in enumerate(shards):
        lanes = pl.ds(pl.multiple_of(spot_ref[k] * PAIR, PAIR), PAIR)
        pltpu.make_async_copy(ref.at[pl.ds(slot * PAIR, PAIR), :], buffer.at[slot, :, lanes], sem).start()


def filled(buffer, sem):
    pltpu.make_async_copy(buffer, buffer, sem).wait()


def columns(left_grade_ref, grade_cols, slots):
    for slot in slots:
        grade_cols[slot] = jnp.broadcast_to(left_grade_ref[slot], (B, PAIR)).T


def score(left, right, scores):
    scores[...] = lax.dot_general(left[...], right, (((1,), (1,)), ((), ())), preferred_element_type=jnp.float32)


def slope(scores, weight, grade_cols, right_grade, scale, slopes, inner, first):
    for part in range(4):
        rows = slice(part * 64, part * 64 + 64)
        here = grade_cols[rows, :]
        scaled = scale[rows, :]
        total = None
        for lane in range(4):
            lanes = slice(lane * B, lane * B + B)
            value = scores[rows, lanes] * scaled
            label = jnp.clip(here - right_grade[:, lanes], -1.0, 1.0)
            step = label * weight[part // 2 : part // 2 + 1, lanes]
            grown = jnp.exp(label * value)
            one = (step * pltpu.reciprocal(1.0 + grown, approx=True)).astype(jnp.bfloat16)
            slopes[rows, lanes] = one
            term = one.astype(jnp.float32) * value
            total = term if total is None else total + term
        inner[rows, :] = total if first else inner[rows, :] + total


def quad_rows(quad, count=1):
    return pl.ds(quad * QUAD, count * QUAD)


def pair_tiles(left_buf, rights, weight_ref, grade_cols, right_grade_ref, scale, scores, slopes, inner, first, begin, finish):
    def ahead(slot, quad):
        begin(slot, quad)
        score(left_buf.at[slot], stacked(rights[quad]), scores.at[slot % 2, :, quad_rows(quad)])

    def arithmetic(slot, quad):
        slope(
            scores.at[slot % 2, :, quad_rows(quad)], weight_ref.at[quad, slot], grade_cols.at[slot],
            right_grade_ref.at[quad], scale.at[slot], slopes.at[slot % 2, :, quad_rows(quad)], inner.at[slot],
            first and quad == 0,
        )

    ahead(0, 0)
    ahead(0, 1)
    for slot in range(4):
        arithmetic(slot, 0)
        if slot < 3:
            ahead(slot + 1, 0)
        arithmetic(slot, 1)
        if slot < 3:
            ahead(slot + 1, 1)
        finish(slot, slopes.at[slot % 2])


def near_kernel(spot_ref, weight_ref, left_grade_ref, *refs):
    shards = refs[:8]
    unit, unit_z, y_above, y_below, z_above, z_below, other = refs[8:15]
    rights = (
        blocks(unit) + blocks(unit_z) + blocks(y_above) + blocks(y_below),
        blocks(z_above) + blocks(z_below) + blocks(other, 0, 2),
    )
    acc, left_buf, inner, scale, grade_cols, scores, slopes, right_grade_ref, left_sem = refs[15:]
    fetch_left(spot_ref, shards, 0, left_buf, left_sem.at[0])
    for slot in (1, 2, 3):
        fetch_left(spot_ref, shards, slot, left_buf, left_sem.at[slot])
    columns(left_grade_ref, grade_cols, range(4))
    right_grades(rights, right_grade_ref)

    def begin(slot, quad):
        if quad == 0:
            filled(left_buf.at[slot], left_sem.at[slot])
            squares = jnp.zeros((PAIR, B), jnp.float32)
            for chunk in range(16):
                part = left_buf[slot, :, chunk * B : (chunk + 1) * B].astype(jnp.float32)
                squares += part * part
            norm = jnp.sqrt(jnp.sum(squares, axis=1, keepdims=True) + epsilon)
            scale[slot] = jnp.broadcast_to(smoothing_divisor / norm, (PAIR, B))

    def finish(slot, slopes_ref):
        for chunk in range(8):
            lanes = slice(chunk * PAIR, chunk * PAIR + PAIR)
            part = jnp.dot(slopes_ref[...], stacked(rights[0] + rights[1], lanes), preferred_element_type=jnp.float32)
            acc[slot, :, lanes] = part.astype(jnp.bfloat16)

    pair_tiles(
        left_buf, rights, weight_ref, grade_cols, right_grade_ref, scale, scores, slopes, inner, True, begin, finish
    )


def far_kernel(weight_ref, left_grade_ref, extra_ref, scale, near_inner, left_buf, acc, *refs):
    y_other, z_other, y_far, z_far, y_far_other, z_far_other = refs[:6]
    rights = (
        blocks(y_other, 0, 2) + blocks(z_other, 0, 2),
        blocks(y_far) + blocks(z_far) + blocks(y_far_other) + blocks(z_far_other),
    )
    out_ref, inner, lines, grade_cols, scores, slopes, right_grade_ref, _ = refs[6:]
    columns(left_grade_ref, grade_cols, range(4))
    right_grades(rights, right_grade_ref)
    inner[...] = near_inner[...]

    def finish(slot, slopes_ref):
        for chunk in range(8):
            source = (chunk + 4) % 8
            lanes = slice(source * PAIR, source * PAIR + PAIR)
            part = jnp.dot(slopes_ref[...], stacked(rights[0] + rights[1], lanes), preferred_element_type=jnp.float32)
            out_ref[chunk, slot * PAIR : (slot + 1) * PAIR, :] = (part + acc[slot, :, lanes].astype(jnp.float32)).astype(jnp.bfloat16)
        lines[slot] = jnp.sum(inner[slot].T, axis=0, keepdims=True) * (1.0 / smoothing_divisor)

    pair_tiles(
        left_buf, rights, weight_ref, grade_cols, right_grade_ref, scale, scores, slopes, inner, False,
        lambda slot, quad: None, finish
    )
    total = jnp.concatenate([lines[k] for k in range(4)], axis=0)
    high = total.astype(jnp.bfloat16).astype(jnp.float32)
    last = jnp.concatenate([high, total - high, extra_ref[...]], axis=0).astype(jnp.bfloat16)
    for chunk in range(8):
        out_ref[chunk, 1024:, :] = last


BUFFERS = [
    pltpu.VMEM((4, PAIR, B), jnp.float32),
    pltpu.VMEM((2, PAIR, 2 * QUAD), jnp.float32),
    pltpu.VMEM((2, PAIR, 2 * QUAD), jnp.bfloat16),
    pltpu.VMEM((2, 1, QUAD), jnp.float32),
    pltpu.SemaphoreType.DMA((4,)),
]


def near_pass(spots, weight, left_grade, shards, arrays):
    wide = jax.ShapeDtypeStruct((4, PAIR, WIDTH), jnp.bfloat16)
    rows = jax.ShapeDtypeStruct((4, PAIR, B), jnp.float32)
    return pl.pallas_call(
        near_kernel,
        in_specs=[SMEM, VMEM, VMEM] + [ANY] * len(shards) + [VMEM] * len(arrays),
        out_specs=[VMEM] * 4,
        out_shape=[wide, wide, rows, rows],
        scratch_shapes=BUFFERS,
        compiler_params=pltpu.CompilerParams(vmem_limit_bytes=20 * 2**20),
        cost_estimate=pl.CostEstimate(flops=9 * 10**9, bytes_accessed=16 * 2**20, transcendentals=2**21),
        name="near_tiles",
    )(spots, weight, left_grade, *shards, *arrays)


def far_pass(*arrays):
    return pl.pallas_call(
        far_kernel,
        in_specs=[VMEM] * len(arrays),
        out_specs=VMEM,
        out_shape=jax.ShapeDtypeStruct((8, 1040, PAIR), jnp.bfloat16),
        scratch_shapes=[pltpu.VMEM((4, PAIR, B), jnp.float32), pltpu.VMEM((4, 1, PAIR), jnp.float32)] + BUFFERS,
        compiler_params=pltpu.CompilerParams(vmem_limit_bytes=24 * 2**20),
        cost_estimate=pl.CostEstimate(flops=8 * 10**9, bytes_accessed=24 * 2**20, transcendentals=2**21),
        name="far_tiles",
    )(*arrays)


def across(line, rows):
    column = jnp.broadcast_to(line, (B, rows)).T
    return jnp.concatenate([column, column], axis=1)


def weight_kernel(core_ref, back_ref, projected_ref, hidden_ref, grads_ref, give_ref, keep_ref, pre):
    tail = back_ref[:, 1024:, :].astype(jnp.float32)
    inner = jnp.sum(tail[:, 0:4] + tail[:, 4:8], axis=0)
    for part in range(8):
        at = slice(part * B, part * B + B)
        grads = back_ref[0, at, :].astype(jnp.float32)
        for source in range(1, 8):
            grads += back_ref[source, at, :].astype(jnp.float32)
        grads_ref[at, :] = grads
        norm = across(tail[part, 8:9, :B] + tail[part, 8:9, B:], B)
        half = part % 2 * B
        product = across(inner[part // 2 : part // 2 + 1, half : half + B], B)
        unit = projected_ref[at, :].astype(jnp.float32) / norm
        pre[at, :] = ((grads - unit * product) / norm).astype(jnp.bfloat16)
    mine = core_ref[0] == 0
    for k in range(4):
        product = lax.dot_general(
            hidden_ref[:, k * 896 : (k + 1) * 896], pre[...], (((0,), (0,)), ((), ())), preferred_element_type=jnp.float32
        )
        for j in range(2):
            even = product[2 * j * 224 : (2 * j + 1) * 224].astype(jnp.bfloat16)
            odd = product[(2 * j + 1) * 224 : (2 * j + 2) * 224].astype(jnp.bfloat16)
            keep_ref[2 * k + j] = jnp.where(mine, even, odd)
            give_ref[2 * k + j] = jnp.where(mine, odd, even)


def weight_pass(core, back, projected, hidden):
    chip = jax.ShapeDtypeStruct((8, 224, PAIR), jnp.bfloat16)
    return pl.pallas_call(
        weight_kernel,
        in_specs=[SMEM, VMEM, VMEM, VMEM],
        out_specs=[VMEM, VMEM, VMEM],
        out_shape=[jax.ShapeDtypeStruct((1024, PAIR), jnp.float32), chip, chip],
        scratch_shapes=[pltpu.VMEM((1024, PAIR), jnp.bfloat16)],
        compiler_params=pltpu.CompilerParams(vmem_limit_bytes=32 * 2**20),
        cost_estimate=pl.CostEstimate(flops=2 * 10**9, bytes_accessed=15 * 2**20, transcendentals=0),
        name="weight_terms",
    )(core, back, projected, hidden)


def own_kernel(grade_ref, came_ref, unit_ref, extra_ref, left_grade_ref):
    squares = jnp.zeros((B, B), jnp.float32)
    for k in range(8):
        for half in (0, B):
            part = came_ref[k, :B, half : half + B].astype(jnp.float32)
            squares += part * part
    norm = jnp.sqrt(jnp.sum(squares, axis=1, keepdims=True) + epsilon)
    wide = jnp.broadcast_to(norm, (B, B))
    for k in range(8):
        for half in (0, B):
            part = came_ref[k, :B, half : half + B].astype(jnp.float32) / wide
            unit_ref[:B, k * PAIR + half : k * PAIR + half + B] = (-part if k < 4 else part).astype(jnp.bfloat16)
    for k in range(4):
        lines = [came_ref[j, B:, :B].astype(jnp.float32)[0:1] for j in (2 * k, 2 * k + 1)]
        left_grade_ref[k] = jnp.concatenate(lines, axis=1)
    unit_ref[B:, :] = jnp.zeros((LONG - B, WIDTH), jnp.bfloat16)
    unit_ref[B:, :B] = jnp.broadcast_to(grade_ref[...], (LONG - B, B)).astype(jnp.bfloat16)
    line = wide.T[0:1]
    high = line.astype(jnp.bfloat16).astype(jnp.float32)
    extra_ref[...] = jnp.broadcast_to(jnp.concatenate([high, line - high], axis=1), (8, PAIR))


def own_pass(grades, came):
    return pl.pallas_call(
        own_kernel,
        in_specs=[whole(1, B), whole(8, LONG, PAIR)],
        out_specs=[whole(LONG, WIDTH), whole(8, PAIR), whole(4, 1, PAIR)],
        grid=(1,),
        out_shape=[
            jax.ShapeDtypeStruct((LONG, WIDTH), jnp.bfloat16),
            jax.ShapeDtypeStruct((8, PAIR), jnp.float32),
            jax.ShapeDtypeStruct((4, 1, PAIR), jnp.float32),
        ],
        compiler_params=pltpu.CompilerParams(vmem_limit_bytes=8 * 2**20),
        cost_estimate=pl.CostEstimate(flops=10**6, bytes_accessed=2**20, transcendentals=0),
        name="own_rows",
    )(grades, came)


def shards(hidden, projection, grades, pattern):
    y, zh, core, x, zl = (lax.axis_index(a) for a in AXES)
    col_here = x * 2 + zl

    grade_mine = grades.astype(jnp.bfloat16).reshape(1, B)
    projected = jnp.dot(hidden, projection, preferred_element_type=jnp.float32).astype(jnp.bfloat16)
    grade_rows = jnp.broadcast_to(jnp.tile(grade_mine, (1, 2)), (8, 16, PAIR))
    sent = jnp.concatenate([projected.reshape(8, B, PAIR), grade_rows], axis=1)
    came = lax.all_to_all(sent, COL, 0, 0, tiled=True)
    across_z = shift(projected, "zl", 1)
    below = shift(projected, "x", 1)
    above = shift(projected, "x", -1)

    both = (pattern + pattern.T).astype(jnp.float32)
    row_here = ((y * 2 + zh) * 2 + core) * 8
    home = lax.dynamic_slice_in_dim(both, row_here, 8, 0)
    right_ids = jnp.stack(
        [((((y + d) % 4) * 2 + (zh ^ z)) * 2 + (core ^ c)) * 8 + col_here for d, z, c in RIGHT]
    )
    right_pick = (jnp.arange(128)[:, None] == right_ids[None]).astype(jnp.float32)
    tiles = jnp.dot(home, right_pick, preferred_element_type=jnp.float32).reshape(4, 2, 4, 4)
    weight = jnp.repeat((tiles * (-smoothing_divisor / B)).transpose(2, 0, 1, 3), B, axis=3)
    spots = jnp.stack([((x + d) % 4 * 2 + (zl ^ z) + 4) % 8 for d, z in SHARDS]).astype(jnp.int32)
    came, across_z, below, above, weight, spots = lax.optimization_barrier(
        (came, across_z, below, above, weight, spots)
    )

    unit, extra, left_grade = own_pass(grade_mine.astype(jnp.float32), came)

    y_below = shift(unit, "y", 1)
    y_above = shift(unit, "y", -1)
    unit_z = shift(unit, "zh", 1)
    below_z = shift(across_z, "x", 1)
    above_z = shift(across_z, "x", -1)
    y_below, y_above, unit_z, unit, below, below_z, above_z, left_grade, extra = lax.optimization_barrier(
        (y_below, y_above, unit_z, unit, below, below_z, above_z, left_grade, extra)
    )
    z_below = shift(unit_z, "y", 1)
    z_above = shift(unit_z, "y", -1)
    far = shift(below, "x", 1)
    far_z = shift(above_z, "x", -1)
    other = shift(jnp.concatenate([unit, unit_z], axis=0), "core", 1)
    y_both = jnp.concatenate([y_above, y_below], axis=0)
    y_below, z_above, z_below, y_above, y_both = lax.optimization_barrier(
        (y_below, z_above, z_below, y_above, y_both)
    )
    y_far = shift(y_below, "y", 1)
    z_far = shift(z_above, "y", -1)
    y_other = shift(y_both, "core", 1)
    z_other = shift(jnp.concatenate([z_above, z_below], axis=0), "core", 1)

    left = [projected, across_z, below, below_z, above, above_z, far, far_z]
    nearby = [unit, unit_z, y_above, y_below, z_above, z_below]
    near_acc, left_rows, near_inner, scale = near_pass(spots, weight[:2], left_grade, left, nearby + [other])
    y_far, z_far, near_acc, near_inner = lax.optimization_barrier((y_far, z_far, near_acc, near_inner))
    beyond = [y_other, z_other, y_far, z_far, shift(y_far, "core", 1), shift(z_far, "core", 1)]
    sums = far_pass(weight[2:], left_grade, extra, scale, near_inner, left_rows, near_acc, *beyond)
    back = lax.all_to_all(sums, COL, 0, 0, tiled=True)

    grads, give, keep = weight_pass(core.astype(jnp.int32).reshape(1), back, projected, hidden)
    chip = (keep.astype(jnp.float32) + shift(give, "core", 1).astype(jnp.float32)).astype(jnp.bfloat16)
    gathered = lax.all_to_all(chip, ("y", "zh"), 0, 0, tiled=True)
    weight_grad = jnp.sum(gathered.astype(jnp.float32), axis=0)
    return grads, weight_grad


def solution(mesh):
    fine = Mesh(np.asarray(mesh.devices).reshape(SIZES), AXES)
    return jax.shard_map(
        shards,
        mesh=fine,
        in_specs=(P(ROW, None), P(None, COL), P(ROW + COL), P()),
        out_specs=(P(ROW, COL), P(ROW, COL)),
        check_vma=False,
    )
```
